32 devices in a mesh: seq: 8 (over z, y), head: 4 (over x, core).
Axes of the slice: x: 2, y: 2, z: 4, core: 2. Of those that a mesh axis runs over, the one named last changes fastest.
Arguments:
- features: bfloat16 [1024, 1024], P('seq'), may hold values from -6 to 6
- w_in: bfloat16 [1024, 1024], P(None, 'head'), may hold values from -0.1875 to 0.1875
- b_ahead: bfloat16 [1024, 128], P('seq'), may hold values from -6 to 6
- c_ahead: bfloat16 [1024, 128], P('seq'), may hold values from -0.015625 to 0.015625
- b_behind: bfloat16 [1024, 128], P('seq'), may hold values from -6 to 6
- c_behind: bfloat16 [1024, 128], P('seq'), may hold values from -0.015625 to 0.015625
- decay_ahead: float32 [16, 1024], P('head', 'seq'), may hold values from -2 to 0, as said below
- decay_behind: float32 [16, 1024], P('head', 'seq'), may hold values from -2 to 0, as said below
- skip_gain: float32 [16], P('head'), may hold values from 0.5 to 1.5
- grad_y: bfloat16 [1024, 1024], P('seq', 'head'), may hold values from -6 to 6
Outputs:
- grad_features: bfloat16 [1024, 1024], P('seq', 'head')
- grad_w_in: float32 [1024, 1024], P('seq', 'head')
- grad_b_ahead: float32 [1024, 128], P('seq')
- grad_c_ahead: float32 [1024, 128], P('seq')
- grad_b_behind: float32 [1024, 128], P('seq')
- grad_c_behind: float32 [1024, 128], P('seq')
- grad_decay_ahead: float32 [16, 1024], P('head', 'seq')
- grad_decay_behind: float32 [16, 1024], P('head', 'seq')
The draws below stay inside these ranges and needn't reach their ends.
Inputs may be any that keep to these rules, and one draw needn't show every extreme that they name: `decay_ahead`: every log-decay is negative. `decay_behind`: every log-decay is negative.
All inputs are finite; a program needn't handle non-finite values.
Results may differ from the reference program's by a relative error of at most 0.039.
Values may be sent and summed in bfloat16 or wider, within the bound.
No kernel may reach another device: no remote copies, remote signals or barrier semaphores. Data moves between devices by JAX's collectives and lax.ppermute only.
A program may use at most 128 MiB of HBM per device.

```python
import math
import jax
import jax.numpy as jnp
from jax import lax

D = 1024
ATTENTION_UNITS = 16
P_SIZE = 64
N = 128
SPAN = 128
T_DEV = 128
TOTAL_SLICES = 1024


def decay_table(key):
    keys = jax.random.split(key, 6)
    quick = jax.random.randint(keys[0], (ATTENTION_UNITS, 1), 0, 2) == 0
    starting_level = jnp.where(quick, 6.0 / SPAN, 0.7 / TOTAL_SLICES)
    starting_level = starting_level * jnp.exp(jax.random.uniform(keys[1], (ATTENTION_UNITS, 1), jnp.float32, -0.35, 0.35))
    blocks = TOTAL_SLICES // T_DEV
    multiplier_coefficient = jnp.exp(jax.random.uniform(keys[2], (1, blocks), jnp.float32, -0.357, 0.336))
    multiplier_coefficient = jnp.repeat(multiplier_coefficient, T_DEV, axis=1)
    approximate_guess = jax.random.uniform(keys[3], (ATTENTION_UNITS, TOTAL_SLICES), jnp.float32, 0.5, 1.5)
    selected_locations = jax.random.randint(keys[4], (3, ATTENTION_UNITS), 0, TOTAL_SLICES)
    increment_sizes = jax.random.uniform(keys[5], (3, ATTENTION_UNITS), jnp.float32, 0.22, 0.69)
    temporal_offset = jax.lax.broadcasted_iota(jnp.int32, (ATTENTION_UNITS, TOTAL_SLICES), 1)
    spike_clusters = jnp.zeros((ATTENTION_UNITS, TOTAL_SLICES), jnp.float32)
    for option_selector in range(3):
        spike_clusters = spike_clusters + jnp.where(temporal_offset == selected_locations[option_selector][:, None], increment_sizes[option_selector][:, None], 0.0)
    return -(starting_level * multiplier_coefficient * approximate_guess + spike_clusters)


def draw_decay_ahead(key, part):
    return decay_table(jax.random.fold_in(key, 11))


def draw_decay_behind(key, part):
    return decay_table(jax.random.fold_in(key, 23))


def level_of(key, shape, shards, low, largest):
    loudness = 1.0
    for position, blocks in shards:
        heights = jax.random.uniform(jax.random.fold_in(jax.random.fold_in(key, 6), position), (blocks,), jnp.float32, low / len(shards), largest / len(shards))
        loudness = loudness * jnp.repeat(jnp.exp(heights), shape[position] // blocks).reshape((-1,) + (1,) * (len(shape) - 1 - position))
    return loudness


def normal_values(key, shape, scale, reach, pieces=(), held_as=jnp.bfloat16):
    gain = level_of(key, shape, pieces, -0.22, 0.18) if pieces else 1.0
    values = jax.random.normal(key, shape, jnp.float32) * scale * gain
    return jnp.minimum(jnp.maximum(values, -reach), reach).astype(held_as)


def setup_inputs(seed: int = 0) -> dict:
    key_list = jax.random.split(jax.random.key(seed), 11)
    return {
        "features": normal_values(key_list[0], (TOTAL_SLICES, D), 1.0, 6.0, ((0, 8),)),
        "w_in": normal_values(key_list[1], (D, ATTENTION_UNITS * P_SIZE), D ** -0.5, 0.1875, ((1, 4),)),
        "b_ahead": normal_values(key_list[2], (TOTAL_SLICES, N), 1.0, 6.0, ((0, 8),)),
        "c_ahead": normal_values(key_list[3], (TOTAL_SLICES, N), (N * 8 * SPAN) ** -0.5, 0.015625, ((0, 8),)),
        "b_behind": normal_values(key_list[4], (TOTAL_SLICES, N), 1.0, 6.0, ((0, 8),)),
        "c_behind": normal_values(key_list[5], (TOTAL_SLICES, N), (N * 8 * SPAN) ** -0.5, 0.015625, ((0, 8),)),
        "decay_ahead": draw_decay_ahead(jax.random.fold_in(key_list[10], 71), 0),
        "decay_behind": draw_decay_behind(jax.random.fold_in(key_list[10], 71), 0),
        "skip_gain": jnp.clip(0.5 + 1.0 * jax.random.uniform(key_list[8], (ATTENTION_UNITS,), jnp.float32) ** level_of(key_list[8], (ATTENTION_UNITS,), ((0, 4),), -0.2, 0.2), 0.5, 1.5),
        "grad_y": normal_values(key_list[9], (TOTAL_SLICES, ATTENTION_UNITS * P_SIZE), 1.0, 6.0, ((0, 8), (1, 4))),
    }


HIGH = lax.Precision.HIGHEST

def block_step(states, inputs):
    signal, b_proj, c_proj, log_decay = inputs
    length = log_decay.shape[1]
    signal_low = signal.astype(jnp.bfloat16)
    b_low = b_proj.astype(jnp.bfloat16)
    c_low = c_proj.astype(jnp.bfloat16)
    cumulative = jnp.cumsum(log_decay, axis=1)
    row_index = lax.broadcasted_iota(jnp.int32, (length, length), 0)
    col_index = lax.broadcasted_iota(jnp.int32, (length, length), 1)
    causal = (col_index <= row_index)[None]
    spread = cumulative[:, :, None] - cumulative[:, None, :]
    decays = jnp.where(causal, jnp.exp(jnp.where(causal, spread, 0.0)), 0.0)
    affinity = jnp.dot(c_low, b_low.T, preferred_element_type=jnp.float32)
    scores = (decays * affinity[None]).astype(jnp.bfloat16)
    within = jnp.einsum('hts,shp->thp', scores, signal_low, preferred_element_type=jnp.float32)
    carried = jnp.exp(cumulative).T[:, :, None] * jnp.einsum('tn,hpn->thp', c_proj, states, precision=HIGH)
    final_log = cumulative[:, -1:]
    weighted = (signal * jnp.exp(final_log - cumulative).T[:, :, None]).astype(jnp.bfloat16)
    fresh = jnp.einsum('shp,sn->hpn', weighted, b_low, preferred_element_type=jnp.float32)
    return (jnp.exp(final_log)[:, :, None] * states + fresh, within + carried)

def scan_direction(signal, b_proj, c_proj, log_decay):
    length = SPAN
    blocks = signal.shape[0] // length
    heads = signal.shape[1]
    signal_blocks = signal.reshape(blocks, length, heads, signal.shape[2])
    b_blocks = b_proj.reshape(blocks, length, b_proj.shape[1])
    c_blocks = c_proj.reshape(blocks, length, c_proj.shape[1])
    decay_blocks = log_decay.reshape(heads, blocks, length).transpose(1, 0, 2)
    init = jnp.zeros((heads, signal.shape[2], b_proj.shape[1]), jnp.float32)
    _, outputs = lax.scan(jax.checkpoint(block_step), init, (signal_blocks, b_blocks, c_blocks, decay_blocks))
    return outputs.reshape(signal.shape)

def layer_core(signal, b_fore, c_fore, b_back, c_back, decay_fore, decay_back):
    ahead = scan_direction(signal, b_fore, c_fore, decay_fore)
    behind = scan_direction(jnp.flip(signal, 0), jnp.flip(b_back, 0), jnp.flip(c_back, 0), jnp.flip(decay_back, 1))
    return ahead + jnp.flip(behind, 0)

def reference(features, w_in, b_ahead, c_ahead, b_behind, c_behind, decay_ahead, decay_behind, skip_gain, grad_y):
    x_proj = jnp.dot(features, w_in, preferred_element_type=jnp.float32).astype(jnp.bfloat16)
    signal = x_proj.astype(jnp.float32).reshape(TOTAL_SLICES, ATTENTION_UNITS, P_SIZE)
    cotangent = grad_y.astype(jnp.float32).reshape(TOTAL_SLICES, ATTENTION_UNITS, P_SIZE)
    _, pullback = jax.vjp(layer_core, signal, b_ahead.astype(jnp.float32), c_ahead.astype(jnp.float32), b_behind.astype(jnp.float32), c_behind.astype(jnp.float32), decay_ahead, decay_behind)
    grad_sig, gb_fore, gc_fore, gb_back, gc_back, gd_fore, gd_back = pullback(cotangent)
    grad_x = (grad_sig + skip_gain[None, :, None] * cotangent).astype(jnp.bfloat16).reshape(TOTAL_SLICES, ATTENTION_UNITS * P_SIZE)
    grad_features = jnp.dot(grad_x, w_in.T, preferred_element_type=jnp.float32).astype(jnp.bfloat16)
    grad_w_in = jnp.dot(features.T, grad_x, preferred_element_type=jnp.float32) * (1.0 / math.sqrt(TOTAL_SLICES))
    return (grad_features, grad_w_in, gb_fore, gc_fore, gb_back, gc_back, gd_fore, gd_back)
```

```python
import functools
import math

import jax
import jax.numpy as jnp
from jax import lax
from jax.experimental import pallas as pl
from jax.experimental.pallas import tpu as pltpu
from jax.sharding import PartitionSpec as P

F32 = jnp.float32
BF16 = jnp.bfloat16
HIGH = lax.Precision.HIGHEST
GAIN_ROWS = 16
DIRECT_PEERS = 8


def nn(a, b, **kw):
    return lax.dot_general(a, b, (((1,), (0,)), ((), ())), preferred_element_type=F32, **kw)


def nt(a, b, **kw):
    return lax.dot_general(a, b, (((1,), (1,)), ((), ())), preferred_element_type=F32, **kw)


def iotas(rows, cols):
    return (
        lax.broadcasted_iota(jnp.int32, (rows, cols), 0),
        lax.broadcasted_iota(jnp.int32, (rows, cols), 1),
    )


def spread_rows(values, width):
    heads, length = values.shape
    return jnp.concatenate(
        [jnp.broadcast_to(values[h : h + 1], (width, length)) for h in range(heads)], axis=0
    )


def split3(value):
    high = value.astype(BF16)
    rest = value - high.astype(F32)
    middle = rest.astype(BF16)
    low = (rest - middle.astype(F32)).astype(BF16)
    return high, middle, low


def masked_sums(masks, values):
    masks = masks.astype(BF16)
    return sum(nt(masks, part) for part in split3(values))


def decay_factors(d_ahead, d_behind, width):
    length = d_ahead.shape[1]
    row, col = iotas(length, length)
    upto = (col <= row).astype(F32)
    since = (col >= row).astype(F32)
    ahead = masked_sums(
        jnp.concatenate([upto, 1.0 - upto], axis=0), spread_rows(d_ahead, width)
    )
    behind = masked_sums(
        jnp.concatenate([since, 1.0 - since], axis=0), spread_rows(d_behind, width)
    )
    ahead, behind = jnp.exp(ahead), jnp.exp(behind)
    return ahead[:length], ahead[length:], behind[:length], behind[length:]


def radices(peers):
    bits = peers.bit_length() - 1
    return ([2] if bits % 2 else []) + [4] * (bits // 2)


def digit(index, stride, radix):
    return lax.rem(lax.div(index, stride), radix)


def read_gains(block):
    rows = block.astype(F32)
    return (
        rows[0:1] + rows[1:2] + rows[2:3],
        rows[3:4] + rows[4:5] + rows[5:6],
    )


def gain_block(gains):
    width = gains[0].shape[1]
    parts = [p for g in gains for p in split3(g)]
    rows = [p.astype(F32) for p in parts]
    pad = jnp.zeros((GAIN_ROWS - len(rows), width), F32)
    return jnp.concatenate(rows + [pad], axis=0).astype(BF16)


def product_where(conditions, gains):
    result = jnp.ones_like(gains[0])
    for condition, gain in zip(conditions, gains):
        result = jnp.where(condition, result * gain, result)
    return result


def merge_coefficients(me, members, gains):
    below, above = [], []
    zero = jnp.zeros_like(gains[0])
    others = range(1, len(members))
    for j in others:
        q = members[j]
        low = product_where(
            [jnp.logical_and(members[i] > q, members[i] < me) for i in others], [gains[i] for i in others]
        )
        high = product_where(
            [jnp.logical_and(members[i] < q, members[i] > me) for i in others], [gains[i] for i in others]
        )
        below.append(jnp.where(q < me, low, zero))
        above.append(jnp.where(q > me, high, zero))
    return below, above


def write_payloads(out_refs, totals, gains, me, last):
    n = totals[0].shape[0]
    block = gain_block(gains)
    rounded = [t.astype(BF16) for t in totals]
    if not last:
        for k in range(4):
            out_refs[0][k * n : (k + 1) * n] = rounded[k]
        out_refs[0][4 * n :] = block
        return
    for j, ref in enumerate(out_refs, start=1):
        up = (me ^ j) > me
        ref[0:n] = jnp.where(up, rounded[0], rounded[2])
        ref[n : 2 * n] = jnp.where(up, rounded[1], rounded[3])
        ref[2 * n :] = block


def front_kernel(me, last, peers_out, features, w_in, gy, ba, ca, bb, cb, da, db, x_out, own_out, *sends):
    width = w_in.shape[1] // da.shape[0]
    x = nn(features[...], w_in[...]).astype(BF16)
    x_out[...] = x
    grow_a, left_a, grow_b, left_b = decay_factors(da[...], db[...], width)
    xf, gyf = x.astype(F32), gy[...].astype(F32)
    length = x.shape[0]
    up0 = nn(ba[...].T, (xf * left_a).astype(BF16))
    up1 = nn(cb[...].T, (gyf * grow_b).astype(BF16))
    down0 = nn(ca[...].T, (gyf * grow_a).astype(BF16))
    down1 = nn(bb[...].T, (xf * left_b).astype(BF16))
    gains = (grow_a[length - 1 : length], grow_b[0:1])
    totals = (up0, up1, down0, down1)
    write_payloads([own_out], totals, gains, None, False)
    if last:
        write_payloads(sends, totals, gains, me(), True)


def load_member(ref, n):
    return [ref[k * n : (k + 1) * n].astype(F32) for k in range(4)], read_gains(ref[4 * n :])


def step_kernel(index, stride, radix, first, next_last, next_radix, *refs):
    refs = list(refs)
    own = refs.pop(0)
    received = [refs.pop(0) for _ in range(radix - 1)]
    before = None if first else refs.pop(0)
    pre_out, own_out = refs.pop(0), refs.pop(0)
    n = (own.shape[0] - GAIN_ROWS) // 4
    seq = index()
    me = digit(seq, stride, radix)
    members = [me ^ j for j in range(radix)]
    loaded = [load_member(ref, n) for ref in [own] + received]
    gains = [[l[1][d] for l in loaded] for d in range(2)]
    coefficients = [merge_coefficients(me, members, gains[d]) for d in range(2)]
    width = own.shape[1]
    one = jnp.ones((1, width), F32)
    grow = [one] * 4 if first else [before[4 * n + k : 4 * n + k + 1] for k in range(4)]
    new_grow = []
    totals = []
    for k in range(4):
        d, down = k % 2, k // 2
        total = sum(coefficients[d][down][j - 1] * loaded[j][0][k] for j in range(1, radix))
        if not first:
            total = grow[k] * total + before[k * n : (k + 1) * n]
        pre_out[k * n : (k + 1) * n] = total
        inside = [(members[j] > me) if down else (members[j] < me) for j in range(1, radix)]
        new_grow.append(product_where(inside, gains[d][1:]) * grow[k])
        group = 0.0
        for j in range(radix):
            outer = [
                (members[i] < members[j]) if down else (members[i] > members[j])
                for i in range(radix)
                if i != j
            ]
            others = [gains[d][i] for i in range(radix) if i != j]
            group = group + product_where(outer, others) * loaded[j][0][k]
        totals.append(group)
    pre_out[4 * n :] = jnp.concatenate(new_grow + [jnp.zeros((4, width), F32)], axis=0)
    new_gains = tuple(functools.reduce(lambda a, b: a * b, gains[d]) for d in range(2))
    write_payloads([own_out], totals, new_gains, None, False)
    if next_last:
        write_payloads(refs, totals, new_gains, digit(seq, stride * radix, next_radix), True)


def local_kernel(
    skip, x, gy, features, ba, ca, bb, cb, da, db, gx_out, maps_out, decay_out, factors_out, turned_out
):
    heads, length = da.shape
    width = x.shape[1] // heads
    n = ba.shape[1]
    factors = decay_factors(da[...], db[...], width)
    for k in range(4):
        factors_out[k] = factors[k]
    row, col = iotas(length, length)
    upto = (col <= row).astype(F32)
    since = (col >= row).astype(F32)
    pad = jnp.zeros((8 - heads, length), F32)
    d_ahead = jnp.concatenate([da[...], pad], axis=0)
    d_behind = jnp.concatenate([db[...], pad], axis=0)
    columns_a = masked_sums(upto, d_ahead)
    columns_b = masked_sums(since, d_behind)
    rows_a = columns_a.T
    rows_b = columns_b.T
    later, same = col > row, col == row
    raw_a = nt(ba[...], ca[...])
    raw_b = nt(bb[...], cb[...])
    affinity = jnp.where(same, raw_a + raw_b, jnp.where(later, raw_a, raw_b))
    weight_sum = jnp.zeros((length, length), F32)
    counts = jnp.concatenate([since.T, upto.T], axis=1).astype(BF16)
    cross = jnp.concatenate([row < col, row > col], axis=1).astype(F32)
    totals = []
    for h in range(heads):
        part = slice(h * width, (h + 1) * width)
        gap = jnp.where(
            later,
            rows_a[h : h + 1] - columns_a[:, h : h + 1],
            rows_b[h : h + 1] - columns_b[:, h : h + 1],
        )
        decay = jnp.exp(jnp.where(same, 0.0, gap))
        score_grad = nt(x[:, part], gy[:, part])
        weighted = score_grad * decay
        weight_sum = weight_sum + weighted
        gx_out[:, part] = nn((decay * affinity).astype(BF16), gy[:, part]) + skip[h] * gy[:, part].astype(F32)
        pieces = nn((weighted * affinity).astype(BF16), counts)
        totals.append(jnp.sum(pieces * cross, axis=0, keepdims=True))
    for h in range(heads):
        decay_out[h : h + 1] = totals[h]
    ahead = jnp.where(col >= row, weight_sum, 0.0).astype(BF16)
    behind = jnp.where(col <= row, weight_sum, 0.0).astype(BF16)
    maps_out[:, 0:n] = nn(ahead, ca[...])
    maps_out[:, n : 2 * n] = nn(ahead.T, ba[...])
    maps_out[:, 2 * n : 3 * n] = nn(behind, cb[...])
    maps_out[:, 3 * n :] = nn(behind.T, bb[...])
    turned_out[...] = features[...].T


def carry_kernel(index, radix, stride, first, direct, n_head, *refs):
    refs = list(refs)
    own = refs.pop(0)
    received = [refs.pop(0) for _ in range(radix - 1)]
    before = None if first else refs.pop(0)
    x, gy, turned, w_in, ba, ca, bb, cb = [refs.pop(0) for _ in range(8)]
    gx_local, maps_local, decay_local, factors = [refs.pop(0) for _ in range(4)]
    heads = decay_local.shape[0]
    n = ba.shape[1]
    length, columns = x.shape
    width = columns // heads
    seq, head = index()

    me = digit(seq, stride, radix)
    members = [me ^ j for j in range(radix)]
    gains = [[], []]
    for ref, at in [(own, 4 * n)] + [(r, 2 * n) for r in received]:
        for d, gain in enumerate(read_gains(ref[at:])):
            gains[d].append(gain)
    states = [None] * 4
    for d in range(2):
        coefficients = merge_coefficients(me, members, gains[d])
        for down in range(2):
            k = 2 * down + d
            total = jnp.zeros((n, columns), F32)
            for j, ref in enumerate(received):
                total = total + coefficients[down][j] * ref[d * n : (d + 1) * n].astype(F32)
            if not first:
                total = before[4 * n + k : 4 * n + k + 1] * total + before[k * n : (k + 1) * n]
            states[k] = total
    state_a, grad_b, grad_a, state_b = states

    grow_a, left_a, grow_b, left_b = [factors[k] for k in range(4)]
    xf, gyf = x[...].astype(F32), gy[...].astype(F32)
    row, col = iotas(length, length)
    own_rows, own_cols = iotas(8, columns)
    group = (lax.div(own_cols, width) == own_rows).astype(BF16)
    frame = lax.broadcasted_iota(jnp.int32, (length, 1), 0)

    def direction(state, grad, grow, left, b, c, at_end, later, earlier):
        gain = jnp.sum(jnp.where(frame == at_end, grow, 0.0), axis=0, keepdims=True)
        state_low, grad_low = state.astype(BF16), grad.astype(BF16)
        carried = grow * nn(c[...], state_low)
        through = gain * jnp.sum(state * grad, axis=0, keepdims=True)
        read = gyf * carried + jnp.where(frame == at_end, through, 0.0)
        grad_x = nn(b[...], grad_low).astype(BF16).astype(F32) * left
        write = grad_x * xf
        reads = nt(group, read.astype(BF16))
        writes = nt(group, write.astype(BF16))
        grad_decay = nn(reads, later, precision=HIGH) + nn(writes, earlier, precision=HIGH)
        grad_c = nt((gyf * grow).astype(BF16), state_low)
        grad_b = nt((xf * left).astype(BF16), grad_low)
        return grad_x, grad_b, grad_c, grad_decay

    gx_a, gb_a, gc_a, gd_a = direction(
        state_a, grad_a, grow_a, left_a, ba, ca, length - 1, (row >= col).astype(F32), (row < col).astype(F32)
    )
    gx_b, gb_b, gc_b, gd_b = direction(
        state_b, grad_b, grow_b, left_b, bb, cb, 0, (row <= col).astype(F32), (row > col).astype(F32)
    )
    gd_a_out, gd_b_out, own_out = refs.pop(0), refs.pop(0), refs.pop(0)
    gd_a_out[...] = gd_a[:heads] + decay_local[:, 0:length]
    gd_b_out[...] = gd_b[:heads] + decay_local[:, length:]
    grad_x = (gx_local[...] + gx_a + gx_b).astype(BF16)
    maps = maps_local[...] + jnp.concatenate([gb_a, gc_a, gb_b, gc_b], axis=1)
    maps_low = maps.astype(BF16)
    rows_out = w_in.shape[0] // n_head
    own_out[:, rows_out:] = maps
    for k in range(n_head):
        at = pl.multiple_of((head ^ k) * rows_out, rows_out)
        share = nt(grad_x, w_in[pl.ds(at, rows_out), :])
        if k == 0:
            own_out[:, 0:rows_out] = share
        else:
            ref = refs.pop(0)
            ref[:, 0:rows_out] = share.astype(BF16)
            ref[:, rows_out:] = maps_low
    if not direct:
        refs.pop(0)[...] = nn(turned[...], grad_x)
        return
    rows_w = turned.shape[0] // direct
    for k in range(direct):
        at = pl.multiple_of((seq ^ k) * rows_w, rows_w)
        share = nn(turned[pl.ds(at, rows_w), :], grad_x)
        ref = refs.pop(0)
        ref[...] = share.astype(ref.dtype)


def sum_kernel(n_head, direct, scale, *refs):
    refs = list(refs)
    own = refs.pop(0)
    others = [refs.pop(0) for _ in range(n_head - 1)]
    shares = [refs.pop(0) for _ in range(max(direct, 1))]
    gf_out, gw_out = refs.pop(0), refs.pop(0)
    columns = gf_out.shape[1]
    n = refs[0].shape[1]

    def total(part):
        return sum([other[:, part].astype(F32) for other in others], own[:, part])

    gf_out[...] = total(slice(0, columns)).astype(BF16)
    for k, ref in enumerate(refs):
        ref[...] = total(slice(columns + k * n, columns + (k + 1) * n))
    gw_out[...] = sum([share[...].astype(F32) for share in shares[1:]], shares[0][...]) * scale


def call(kernel, outs, *args, flops=0, scalars=0):
    specs = [pl.BlockSpec(memory_space=pltpu.SMEM)] * scalars
    specs += [pl.BlockSpec(memory_space=pltpu.VMEM)] * (len(args) - scalars)
    bytes_moved = sum(math.prod(a.shape) * a.dtype.itemsize for a in args)
    bytes_moved += sum(math.prod(o.shape) * o.dtype.itemsize for o in outs)
    return pl.pallas_call(
        kernel,
        out_shape=outs,
        in_specs=specs,
        out_specs=[pl.BlockSpec(memory_space=pltpu.VMEM)] * len(outs),
        cost_estimate=pl.CostEstimate(flops=flops, bytes_accessed=bytes_moved, transcendentals=0),
        compiler_params=pltpu.CompilerParams(vmem_limit_bytes=48 * 1024 * 1024),
    )(*args)


def swap(value, axis, mask):
    return lax.ppermute(value, axis, [(i, i ^ mask) for i in range(lax.axis_size(axis))])


def local(features, w_in, b_ahead, c_ahead, b_behind, c_behind, decay_ahead, decay_behind, skip_gain, grad_y):
    peers, n_head = lax.axis_size("seq"), lax.axis_size("head")
    length, depth = features.shape
    heads, columns = decay_ahead.shape[0], w_in.shape[1]
    n = b_ahead.shape[1]
    maps = (b_ahead, c_ahead, b_behind, c_behind)
    decays = (decay_ahead, decay_behind)
    seq_index = lambda: lax.axis_index("seq")
    both_index = lambda: (lax.axis_index("seq"), lax.axis_index("head"))
    shape = jax.ShapeDtypeStruct
    whole = shape((4 * n + GAIN_ROWS, columns), BF16)
    half = shape((2 * n + GAIN_ROWS, columns), BF16)
    prefix = shape((4 * n + 8, columns), F32)

    steps = radices(peers)
    only = len(steps) == 1
    x, own, *sends = call(
        functools.partial(front_kernel, seq_index, only, peers),
        [shape((length, columns), BF16), whole] + [half] * ((steps[0] - 1) if only else 0),
        features, w_in, grad_y, *maps, *decays,
        flops=2 * length * depth * columns,
    )
    gx_local, maps_local, decay_local, factors, turned = call(
        local_kernel,
        [
            shape((length, columns), F32),
            shape((length, 4 * n), F32),
            shape((heads, 2 * length), F32),
            shape((4, length, columns), F32),
            shape((depth, length), BF16),
        ],
        skip_gain, x, grad_y, features, *maps, *decays,
        flops=2 * length * depth * columns,
        scalars=1,
    )
    stride, before = 1, None
    for at, radix in enumerate(steps[:-1]):
        received = [swap(own, "seq", j * stride) for j in range(1, radix)]
        next_last = at == len(steps) - 2
        following = steps[at + 1]
        before, own, *sends = call(
            functools.partial(step_kernel, seq_index, stride, radix, at == 0, next_last, following),
            [prefix, whole] + [half] * ((following - 1) if next_last else 0),
            own, *received, *([] if at == 0 else [before]),
            flops=40 * n * columns,
        )
        stride *= radix
    received = [swap(send, "seq", j * stride) for j, send in enumerate(sends, start=1)]
    direct = peers if peers <= DIRECT_PEERS else 0
    rows_out = depth // n_head
    w_shapes = [shape((depth, columns), F32)]
    if direct:
        block = (depth // direct, columns)
        w_shapes = [shape(block, F32)] + [shape(block, BF16)] * (direct - 1)
    gd_ahead, gd_behind, own_share, *shares = call(
        functools.partial(carry_kernel, both_index, steps[-1], stride, only, direct, n_head),
        [shape((heads, length), F32)] * 2
        + [shape((length, rows_out + 4 * n), F32)]
        + [shape((length, rows_out + 4 * n), BF16)] * (n_head - 1)
        + w_shapes,
        own, *received, *([] if only else [before]),
        x, grad_y, turned, w_in, *maps, gx_local, maps_local, decay_local, factors,
        flops=6 * length * depth * columns,
    )
    head_shares, w_shares = shares[: n_head - 1], shares[n_head - 1 :]
    if direct:
        w_shares = w_shares[:1] + [swap(s, "seq", k) for k, s in enumerate(w_shares[1:], start=1)]
    else:
        w_shares = [lax.psum_scatter(w_shares[0], "seq", scatter_dimension=0, tiled=True)]
    head_shares = [swap(s, "head", k) for k, s in enumerate(head_shares, start=1)]
    grad_features, grad_w_in, *grad_maps = call(
        functools.partial(sum_kernel, n_head, direct, 1.0 / math.sqrt(length * peers)),
        [shape((length, rows_out), BF16), shape((depth // peers, columns), F32)]
        + [shape((length, n), F32)] * 4,
        own_share, *head_shares, *w_shares,
    )
    return (grad_features, grad_w_in, *grad_maps, gd_ahead, gd_behind)


def solution(mesh):
    in_specs = (
        P("seq", None),
        P(None, "head"),
        P("seq", None),
        P("seq", None),
        P("seq", None),
        P("seq", None),
        P("head", "seq"),
        P("head", "seq"),
        P("head"),
        P("seq", "head"),
    )
    out_specs = (
        P("seq", "head"),
        P("seq", "head"),
        P("seq", None),
        P("seq", None),
        P("seq", None),
        P("seq", None),
        P("head", "seq"),
        P("head", "seq"),
    )
    return jax.shard_map(local, mesh=mesh, in_specs=in_specs, out_specs=out_specs, check_vma=False)
```

```python
import functools
import math

import jax
import jax.numpy as jnp
from jax import lax
from jax.experimental import pallas as pl
from jax.experimental.pallas import tpu as pltpu
from jax.sharding import PartitionSpec as P

F32 = jnp.float32
BF16 = jnp.bfloat16
HIGH = lax.Precision.HIGHEST
GAIN_ROWS = 16
HELD_LIMIT = 48


def nn(a, b, **kw):
    return lax.dot_general(a, b, (((1,), (0,)), ((), ())), preferred_element_type=F32, **kw)


def nt(a, b, **kw):
    return lax.dot_general(a, b, (((1,), (1,)), ((), ())), preferred_element_type=F32, **kw)


def iotas(rows, cols):
    return (
        lax.broadcasted_iota(jnp.int32, (rows, cols), 0),
        lax.broadcasted_iota(jnp.int32, (rows, cols), 1),
    )


def spread_rows(values, width):
    heads, length = values.shape
    return jnp.concatenate(
        [jnp.broadcast_to(values[h : h + 1], (width, length)) for h in range(heads)], axis=0
    )


def split3(value):
    high = value.astype(BF16)
    rest = value - high.astype(F32)
    middle = rest.astype(BF16)
    low = (rest - middle.astype(F32)).astype(BF16)
    return high, middle, low


def masked_sums(masks, values):
    masks = masks.astype(BF16)
    return sum(nt(masks, part) for part in split3(values))


def decay_factors(d_ahead, d_behind, width):
    length = d_ahead.shape[1]
    row, col = iotas(length, length)
    upto = (col <= row).astype(F32)
    since = (col >= row).astype(F32)
    ahead = masked_sums(
        jnp.concatenate([upto, 1.0 - upto], axis=0), spread_rows(d_ahead, width)
    )
    behind = masked_sums(
        jnp.concatenate([since, 1.0 - since], axis=0), spread_rows(d_behind, width)
    )
    ahead, behind = jnp.exp(ahead), jnp.exp(behind)
    return ahead[:length], ahead[length:], behind[:length], behind[length:]


def radices(peers):
    bits = peers.bit_length() - 1
    return ([2] if bits % 2 else []) + [4] * (bits // 2)


def digit(index, stride, radix):
    return lax.rem(lax.div(index, stride), radix)


def read_gains(block):
    rows = block.astype(F32)
    return (
        rows[0:1] + rows[1:2] + rows[2:3],
        rows[3:4] + rows[4:5] + rows[5:6],
    )


def gain_block(gains):
    width = gains[0].shape[1]
    parts = [p for g in gains for p in split3(g)]
    rows = [p.astype(F32) for p in parts]
    pad = jnp.zeros((GAIN_ROWS - len(rows), width), F32)
    return jnp.concatenate(rows + [pad], axis=0).astype(BF16)


def product_where(conditions, gains):
    result = jnp.ones_like(gains[0])
    for condition, gain in zip(conditions, gains):
        result = jnp.where(condition, result * gain, result)
    return result


def merge_coefficients(me, members, gains):
    below, above = [], []
    zero = jnp.zeros_like(gains[0])
    others = range(1, len(members))
    for j in others:
        q = members[j]
        low = product_where(
            [jnp.logical_and(members[i] > q, members[i] < me) for i in others], [gains[i] for i in others]
        )
        high = product_where(
            [jnp.logical_and(members[i] < q, members[i] > me) for i in others], [gains[i] for i in others]
        )
        below.append(jnp.where(q < me, low, zero))
        above.append(jnp.where(q > me, high, zero))
    return below, above


def write_payloads(out_refs, totals, gains, me, last):
    n = totals[0].shape[0]
    block = gain_block(gains)
    rounded = [t.astype(BF16) for t in totals]
    if not last:
        for k in range(4):
            out_refs[0][k * n : (k + 1) * n] = rounded[k]
        out_refs[0][4 * n :] = block
        return
    for j, ref in enumerate(out_refs, start=1):
        up = (me ^ j) > me
        ref[0:n] = jnp.where(up, rounded[0], rounded[2])
        ref[n : 2 * n] = jnp.where(up, rounded[1], rounded[3])
        ref[2 * n :] = block


def front_kernel(me, last, *refs):
    refs = list(refs)
    sources = [refs.pop(0) for _ in range(9)]
    x_out, own_out = refs.pop(0), refs.pop(0)
    sems = refs.pop()
    held = refs[-9:]
    sends = refs[:-9]
    copies = [pltpu.make_async_copy(s, h, sems.at[k]) for k, (s, h) in enumerate(zip(sources, held))]
    for copy in copies:
        copy.start()
    da, db, gy, ba, ca, bb, cb, features, w_in = held
    for copy in copies[:2]:
        copy.wait()
    width = w_in.shape[1] // da.shape[0]
    grow_a, left_a, grow_b, left_b = decay_factors(da[...], db[...], width)
    for copy in copies[2:]:
        copy.wait()
    x = nn(features[...], w_in[...]).astype(BF16)
    x_out[...] = x
    xf, gyf = x.astype(F32), gy[...].astype(F32)
    length = x.shape[0]
    up0 = nn(ba[...].T, (xf * left_a).astype(BF16))
    up1 = nn(cb[...].T, (gyf * grow_b).astype(BF16))
    down0 = nn(ca[...].T, (gyf * grow_a).astype(BF16))
    down1 = nn(bb[...].T, (xf * left_b).astype(BF16))
    gains = (grow_a[length - 1 : length], grow_b[0:1])
    totals = (up0, up1, down0, down1)
    write_payloads([own_out], totals, gains, None, False)
    if last:
        write_payloads(sends, totals, gains, me(), True)


def load_member(ref, n):
    return [ref[k * n : (k + 1) * n].astype(F32) for k in range(4)], read_gains(ref[4 * n :])


def step_kernel(index, stride, radix, first, next_last, next_radix, *refs):
    refs = list(refs)
    own = refs.pop(0)
    received = [refs.pop(0) for _ in range(radix - 1)]
    before = None if first else refs.pop(0)
    pre_out, own_out = refs.pop(0), refs.pop(0)
    n = (own.shape[0] - GAIN_ROWS) // 4
    seq = index()
    me = digit(seq, stride, radix)
    members = [me ^ j for j in range(radix)]
    loaded = [load_member(ref, n) for ref in [own] + received]
    gains = [[l[1][d] for l in loaded] for d in range(2)]
    coefficients = [merge_coefficients(me, members, gains[d]) for d in range(2)]
    width = own.shape[1]
    one = jnp.ones((1, width), F32)
    grow = [one] * 4 if first else [before[4 * n + k : 4 * n + k + 1] for k in range(4)]
    new_grow = []
    totals = []
    for k in range(4):
        d, down = k % 2, k // 2
        total = sum(coefficients[d][down][j - 1] * loaded[j][0][k] for j in range(1, radix))
        if not first:
            total = grow[k] * total + before[k * n : (k + 1) * n]
        pre_out[k * n : (k + 1) * n] = total
        inside = [(members[j] > me) if down else (members[j] < me) for j in range(1, radix)]
        new_grow.append(product_where(inside, gains[d][1:]) * grow[k])
        group = 0.0
        for j in range(radix):
            outer = [
                (members[i] < members[j]) if down else (members[i] > members[j])
                for i in range(radix)
                if i != j
            ]
            others = [gains[d][i] for i in range(radix) if i != j]
            group = group + product_where(outer, others) * loaded[j][0][k]
        totals.append(group)
    pre_out[4 * n :] = jnp.concatenate(new_grow + [jnp.zeros((4, width), F32)], axis=0)
    new_gains = tuple(functools.reduce(lambda a, b: a * b, gains[d]) for d in range(2))
    write_payloads([own_out], totals, new_gains, None, False)
    if next_last:
        write_payloads(refs, totals, new_gains, digit(seq, stride * radix, next_radix), True)


def local_kernel(
    skip, x, gy, features, ba, ca, bb, cb, da, db, gx_out, maps_out, decay_out, factors_out, turned_out
):
    heads, length = da.shape
    width = x.shape[1] // heads
    n = ba.shape[1]
    factors = decay_factors(da[...], db[...], width)
    for k in range(4):
        factors_out[k] = factors[k]
    row, col = iotas(length, length)
    upto = (col <= row).astype(F32)
    since = (col >= row).astype(F32)
    pad = jnp.zeros((8 - heads, length), F32)
    d_ahead = jnp.concatenate([da[...], pad], axis=0)
    d_behind = jnp.concatenate([db[...], pad], axis=0)
    columns_a = masked_sums(upto, d_ahead)
    columns_b = masked_sums(since, d_behind)
    rows_a = columns_a.T
    rows_b = columns_b.T
    later, same = col > row, col == row
    raw_a = nt(ba[...], ca[...])
    raw_b = nt(bb[...], cb[...])
    affinity = jnp.where(same, raw_a + raw_b, jnp.where(later, raw_a, raw_b))
    weight_sum = jnp.zeros((length, length), F32)
    counts = jnp.concatenate([since.T, upto.T], axis=1).astype(BF16)
    cross = jnp.concatenate([row < col, row > col], axis=1).astype(F32)
    totals = []
    for h in range(heads):
        part = slice(h * width, (h + 1) * width)
        gap = jnp.where(
            later,
            rows_a[h : h + 1] - columns_a[:, h : h + 1],
            rows_b[h : h + 1] - columns_b[:, h : h + 1],
        )
        decay = jnp.exp(jnp.where(same, 0.0, gap))
        score_grad = nt(x[:, part], gy[:, part])
        weighted = score_grad * decay
        weight_sum = weight_sum + weighted
        gx_out[:, part] = nn((decay * affinity).astype(BF16), gy[:, part]) + skip[h] * gy[:, part].astype(F32)
        pieces = nn((weighted * affinity).astype(BF16), counts)
        totals.append(jnp.sum(pieces * cross, axis=0, keepdims=True))
    for h in range(heads):
        decay_out[h : h + 1] = totals[h]
    ahead = jnp.where(col >= row, weight_sum, 0.0).astype(BF16)
    behind = jnp.where(col <= row, weight_sum, 0.0).astype(BF16)
    maps_out[:, 0:n] = nn(ahead, ca[...])
    maps_out[:, n : 2 * n] = nn(ahead.T, ba[...])
    maps_out[:, 2 * n : 3 * n] = nn(behind, cb[...])
    maps_out[:, 3 * n :] = nn(behind.T, bb[...])
    turned_out[...] = features[...].T


def carry_kernel(index, radix, stride, first, peers, n_head, *refs):
    refs = list(refs)
    own = refs.pop(0)
    received = [refs.pop(0) for _ in range(radix - 1)]
    before = None if first else refs.pop(0)
    x, gy, turned, w_in, ba, ca, bb, cb = [refs.pop(0) for _ in range(8)]
    gx_local, maps_local, decay_local, factors = [refs.pop(0) for _ in range(4)]
    heads = decay_local.shape[0]
    n = ba.shape[1]
    length, columns = x.shape
    width = columns // heads
    seq, head = index()

    me = digit(seq, stride, radix)
    members = [me ^ j for j in range(radix)]
    gains = [[], []]
    for ref, at in [(own, 4 * n)] + [(r, 2 * n) for r in received]:
        for d, gain in enumerate(read_gains(ref[at:])):
            gains[d].append(gain)
    states = [None] * 4
    for d in range(2):
        coefficients = merge_coefficients(me, members, gains[d])
        for down in range(2):
            k = 2 * down + d
            total = jnp.zeros((n, columns), F32)
            for j, ref in enumerate(received):
                total = total + coefficients[down][j] * ref[d * n : (d + 1) * n].astype(F32)
            if not first:
                total = before[4 * n + k : 4 * n + k + 1] * total + before[k * n : (k + 1) * n]
            states[k] = total
    state_a, grad_b, grad_a, state_b = states

    grow_a, left_a, grow_b, left_b = [factors[k] for k in range(4)]
    xf, gyf = x[...].astype(F32), gy[...].astype(F32)
    row, col = iotas(length, length)
    own_rows, own_cols = iotas(8, columns)
    group = (lax.div(own_cols, width) == own_rows).astype(BF16)
    frame = lax.broadcasted_iota(jnp.int32, (length, 1), 0)

    def direction(state, grad, grow, left, b, c, at_end, later, earlier):
        gain = jnp.sum(jnp.where(frame == at_end, grow, 0.0), axis=0, keepdims=True)
        state_low, grad_low = state.astype(BF16), grad.astype(BF16)
        carried = grow * nn(c[...], state_low)
        through = gain * jnp.sum(state * grad, axis=0, keepdims=True)
        read = gyf * carried + jnp.where(frame == at_end, through, 0.0)
        grad_x = nn(b[...], grad_low).astype(BF16).astype(F32) * left
        write = grad_x * xf
        reads = nt(group, read.astype(BF16))
        writes = nt(group, write.astype(BF16))
        grad_decay = nn(reads, later, precision=HIGH) + nn(writes, earlier, precision=HIGH)
        grad_c = nt((gyf * grow).astype(BF16), state_low)
        grad_b = nt((xf * left).astype(BF16), grad_low)
        return grad_x, grad_b, grad_c, grad_decay

    gx_a, gb_a, gc_a, gd_a = direction(
        state_a, grad_a, grow_a, left_a, ba, ca, length - 1, (row >= col).astype(F32), (row < col).astype(F32)
    )
    gx_b, gb_b, gc_b, gd_b = direction(
        state_b, grad_b, grow_b, left_b, bb, cb, 0, (row <= col).astype(F32), (row > col).astype(F32)
    )
    gd_a_out, gd_b_out, own_out = refs.pop(0), refs.pop(0), refs.pop(0)
    gd_a_out[...] = gd_a[:heads] + decay_local[:, 0:length]
    gd_b_out[...] = gd_b[:heads] + decay_local[:, length:]
    grad_x = (gx_local[...] + gx_a + gx_b).astype(BF16)
    maps = maps_local[...] + jnp.concatenate([gb_a, gc_a, gb_b, gc_b], axis=1)
    maps_low = maps.astype(BF16)
    rows_out = w_in.shape[0] // n_head
    own_out[:, rows_out:] = maps
    for k in range(n_head):
        at = pl.multiple_of((head ^ k) * rows_out, rows_out)
        share = nt(grad_x, w_in[pl.ds(at, rows_out), :])
        if k == 0:
            own_out[:, 0:rows_out] = share
        else:
            ref = refs.pop(0)
            ref[:, 0:rows_out] = share.astype(BF16)
            ref[:, rows_out:] = maps_low
    share = nn(turned[...], grad_x).astype(BF16)
    refs.pop(0)[...] = share.reshape(peers, turned.shape[0] // peers, columns)


def sum_kernel(n_head, scale, *refs):
    refs = list(refs)
    own = refs.pop(0)
    others = [refs.pop(0) for _ in range(n_head - 1)]
    shares = refs.pop(0)
    gf_out, gw_out = refs.pop(0), refs.pop(0)
    columns = gf_out.shape[1]
    n = refs[0].shape[1]

    def total(part):
        return sum([other[:, part].astype(F32) for other in others], own[:, part])

    gf_out[...] = total(slice(0, columns)).astype(BF16)
    for k, ref in enumerate(refs):
        ref[...] = total(slice(columns + k * n, columns + (k + 1) * n))
    gw_out[...] = jnp.sum(shares[...].astype(F32), axis=0) * scale


def call(kernel, outs, *args, flops=0, scalars=0, held=False):
    space = pltpu.HBM if held else pltpu.VMEM
    specs = [pl.BlockSpec(memory_space=pltpu.SMEM)] * scalars
    specs += [pl.BlockSpec(memory_space=space)] * (len(args) - scalars)
    scratch = []
    if held:
        scratch = [pltpu.VMEM(a.shape, a.dtype) for a in args] + [pltpu.SemaphoreType.DMA((len(args),))]
    if held:
        args = tuple(pltpu.with_memory_space_constraint(a, pltpu.HBM) for a in args)
    bytes_moved = sum(math.prod(a.shape) * a.dtype.itemsize for a in args)
    bytes_moved += sum(math.prod(o.shape) * o.dtype.itemsize for o in outs)
    return pl.pallas_call(
        kernel,
        out_shape=outs,
        in_specs=specs,
        out_specs=[pl.BlockSpec(memory_space=pltpu.VMEM)] * len(outs),
        scratch_shapes=scratch,
        cost_estimate=pl.CostEstimate(flops=flops, bytes_accessed=bytes_moved, transcendentals=0),
        compiler_params=pltpu.CompilerParams(vmem_limit_bytes=(HELD_LIMIT if held else 48) * 1024 * 1024),
    )(*args)


def swap(value, axis, mask):
    return lax.ppermute(value, axis, [(i, i ^ mask) for i in range(lax.axis_size(axis))])


def local(features, w_in, b_ahead, c_ahead, b_behind, c_behind, decay_ahead, decay_behind, skip_gain, grad_y):
    peers, n_head = lax.axis_size("seq"), lax.axis_size("head")
    length, depth = features.shape
    heads, columns = decay_ahead.shape[0], w_in.shape[1]
    n = b_ahead.shape[1]
    maps = (b_ahead, c_ahead, b_behind, c_behind)
    decays = (decay_ahead, decay_behind)
    seq_index = lambda: lax.axis_index("seq")
    both_index = lambda: (lax.axis_index("seq"), lax.axis_index("head"))
    shape = jax.ShapeDtypeStruct
    whole = shape((4 * n + GAIN_ROWS, columns), BF16)
    half = shape((2 * n + GAIN_ROWS, columns), BF16)
    prefix = shape((4 * n + 8, columns), F32)

    steps = radices(peers)
    only = len(steps) == 1
    x, own, *sends = call(
        functools.partial(front_kernel, seq_index, only),
        [shape((length, columns), BF16), whole] + [half] * ((steps[0] - 1) if only else 0),
        *decays, grad_y, *maps, features, w_in,
        flops=2 * length * depth * columns,
        held=True,
    )
    gx_local, maps_local, decay_local, factors, turned = call(
        local_kernel,
        [
            shape((length, columns), F32),
            shape((length, 4 * n), F32),
            shape((heads, 2 * length), F32),
            shape((4, length, columns), F32),
            shape((depth, length), BF16),
        ],
        skip_gain, x, grad_y, features, *maps, *decays,
        flops=2 * length * depth * columns,
        scalars=1,
    )
    stride, before = 1, None
    for at, radix in enumerate(steps[:-1]):
        received = [swap(own, "seq", j * stride) for j in range(1, radix)]
        next_last = at == len(steps) - 2
        following = steps[at + 1]
        before, own, *sends = call(
            functools.partial(step_kernel, seq_index, stride, radix, at == 0, next_last, following),
            [prefix, whole] + [half] * ((following - 1) if next_last else 0),
            own, *received, *([] if at == 0 else [before]),
            flops=40 * n * columns,
        )
        stride *= radix
    received = [swap(send, "seq", j * stride) for j, send in enumerate(sends, start=1)]
    rows_out = depth // n_head
    rows_w = depth // peers
    gd_ahead, gd_behind, own_share, *shares = call(
        functools.partial(carry_kernel, both_index, steps[-1], stride, only, peers, n_head),
        [shape((heads, length), F32)] * 2
        + [shape((length, rows_out + 4 * n), F32)]
        + [shape((length, rows_out + 4 * n), BF16)] * (n_head - 1)
        + [shape((peers, rows_w, columns), BF16)],
        own, *received, *([] if only else [before]),
        x, grad_y, turned, w_in, *maps, gx_local, maps_local, decay_local, factors,
        flops=6 * length * depth * columns,
    )
    *head_shares, w_shares = shares
    w_shares = lax.all_to_all(w_shares, "seq", 0, 0)
    head_shares = [swap(s, "head", k) for k, s in enumerate(head_shares, start=1)]
    grad_features, grad_w_in, *grad_maps = call(
        functools.partial(sum_kernel, n_head, 1.0 / math.sqrt(length * peers)),
        [shape((length, rows_out), BF16), shape((rows_w, columns), F32)]
        + [shape((length, n), F32)] * 4,
        own_share, *head_shares, w_shares,
    )
    return (grad_features, grad_w_in, *grad_maps, gd_ahead, gd_behind)


def solution(mesh):
    in_specs = (
        P("seq", None),
        P(None, "head"),
        P("seq", None),
        P("seq", None),
        P("seq", None),
        P("seq", None),
        P("head", "seq"),
        P("head", "seq"),
        P("head"),
        P("seq", "head"),
    )
    out_specs = (
        P("seq", "head"),
        P("seq", "head"),
        P("seq", None),
        P("seq", None),
        P("seq", None),
        P("seq", None),
        P("head", "seq"),
        P("head", "seq"),
    )
    return jax.shard_map(local, mesh=mesh, in_specs=in_specs, out_specs=out_specs, check_vma=False)
```

```python
import functools
import math

import jax
import jax.numpy as jnp
from jax import lax
from jax.experimental import pallas as pl
from jax.experimental.pallas import tpu as pltpu
from jax.sharding import PartitionSpec as P

F32 = jnp.float32
BF16 = jnp.bfloat16
HIGH = lax.Precision.HIGHEST
GAIN_ROWS = 16
VMEM_LIMIT = 48 * 1024 * 1024


def nn(a, b, **kw):
    return lax.dot_general(a, b, (((1,), (0,)), ((), ())), preferred_element_type=F32, **kw)


def nt(a, b, **kw):
    return lax.dot_general(a, b, (((1,), (1,)), ((), ())), preferred_element_type=F32, **kw)


def iotas(rows, cols):
    return (
        lax.broadcasted_iota(jnp.int32, (rows, cols), 0),
        lax.broadcasted_iota(jnp.int32, (rows, cols), 1),
    )


def spread_rows(values, width):
    heads, length = values.shape
    return jnp.concatenate(
        [jnp.broadcast_to(values[h : h + 1], (width, length)) for h in range(heads)], axis=0
    )


def split3(value):
    high = value.astype(BF16)
    rest = value - high.astype(F32)
    middle = rest.astype(BF16)
    low = (rest - middle.astype(F32)).astype(BF16)
    return high, middle, low


def masked_sums(masks, values):
    masks = masks.astype(BF16)
    return sum(nt(masks, part) for part in split3(values))


def decay_factors(d_ahead, d_behind, width):
    length = d_ahead.shape[1]
    row, col = iotas(length, length)
    upto = (col <= row).astype(F32)
    since = (col >= row).astype(F32)
    ahead = masked_sums(
        jnp.concatenate([upto, 1.0 - upto], axis=0), spread_rows(d_ahead, width)
    )
    behind = masked_sums(
        jnp.concatenate([since, 1.0 - since], axis=0), spread_rows(d_behind, width)
    )
    ahead, behind = jnp.exp(ahead), jnp.exp(behind)
    return ahead[:length], ahead[length:], behind[:length], behind[length:]


def radices(peers):
    bits = peers.bit_length() - 1
    return ([2] if bits % 2 else []) + [4] * (bits // 2)


def digit(index, stride, radix):
    return lax.rem(lax.div(index, stride), radix)


def read_gain(block, k=0):
    rows = block.astype(F32)[3 * k : 3 * k + 3]
    return rows[0:1] + rows[1:2] + rows[2:3]


def gain_block(*gains):
    rows = [p.astype(F32) for gain in gains for p in split3(gain)]
    pad = jnp.zeros((GAIN_ROWS - len(rows), gains[0].shape[1]), F32)
    return jnp.concatenate(rows + [pad], axis=0).astype(BF16)


def product_where(conditions, gains):
    result = jnp.ones_like(gains[0])
    for condition, gain in zip(conditions, gains):
        result = jnp.where(condition, result * gain, result)
    return result


def merge_coefficients(me, members, gains_up, gains_down):
    below, above = [], []
    others = range(1, len(members))
    for j in others:
        q = members[j]
        low = product_where(
            [jnp.logical_and(members[i] > q, members[i] < me) for i in others], [gains_up[i] for i in others]
        )
        high = product_where(
            [jnp.logical_and(members[i] < q, members[i] > me) for i in others], [gains_down[i] for i in others]
        )
        below.append(jnp.where(q < me, low, 0.0))
        above.append(jnp.where(q > me, high, 0.0))
    return below, above


def write_whole(out, up, down, gain_up, gain_down):
    n = up.shape[0]
    out[0:n] = up.astype(BF16)
    out[n : 2 * n] = down.astype(BF16)
    out[2 * n :] = gain_block(gain_up, gain_down)


def write_halves(outs, up, down, gain_up, gain_down, me):
    n = up.shape[0]
    blocks = gain_block(gain_up), gain_block(gain_down)
    up, down = up.astype(BF16), down.astype(BF16)
    for j, out in enumerate(outs, start=1):
        upward = (me ^ j) > me
        out[0:n] = jnp.where(upward, up, down)
        out[n:] = jnp.where(upward, *blocks)


def write_chunk(outs, me, last, *chunk):
    if last:
        write_halves(outs, *chunk, me())
    else:
        write_whole(outs[0], *chunk)


def start_copies(sources, targets, sems):
    copies = [pltpu.make_async_copy(s, t, sems.at[k]) for k, (s, t) in enumerate(zip(sources, targets))]
    for copy in copies:
        copy.start()
    return copies


def gradient_kernel(me, last, width, *refs):
    *refs, sems = refs
    sources, outs, held = refs[:5], refs[5:-5], refs[-5:]
    copies = start_copies(sources, held, sems)
    da, db, gy, ca, cb = held
    for copy in copies[:2]:
        copy.wait()
    factors = decay_factors(da[...], db[...], width)
    *sends, factors_out = outs
    for k in range(4):
        factors_out[k] = factors[k]
    grow_a, _, grow_b, _ = factors
    for copy in copies[2:]:
        copy.wait()
    gyf = gy[...].astype(F32)
    up = nn(cb[...].T, (gyf * grow_b).astype(BF16))
    down = nn(ca[...].T, (gyf * grow_a).astype(BF16))
    write_chunk(sends, me, last, up, down, grow_b[0:1], grow_a[gyf.shape[0] - 1 :])


def state_kernel(me, last, *refs):
    *refs, sems = refs
    sources, factors, outs, held = refs[:4], refs[4], refs[5:-4], refs[-4:]
    copies = start_copies(sources, held, sems)
    ba, bb, features, w_in = held
    for copy in copies:
        copy.wait()
    *sends, x_out = outs
    x = nn(features[...], w_in[...]).astype(BF16)
    x_out[...] = x
    xf = x.astype(F32)
    up = nn(ba[...].T, (xf * factors[1]).astype(BF16))
    down = nn(bb[...].T, (xf * factors[3]).astype(BF16))
    write_chunk(sends, me, last, up, down, factors[0, x.shape[0] - 1 :], factors[2, 0:1])


def step_kernel(index, stride, radix, first, next_last, next_radix, *refs):
    refs = list(refs)
    own = refs.pop(0)
    received = [refs.pop(0) for _ in range(radix - 1)]
    before = None if first else refs.pop(0)
    pre_out = refs.pop(0)
    n = (own.shape[0] - GAIN_ROWS) // 2
    seq = index()
    me = digit(seq, stride, radix)
    members = [me ^ j for j in range(radix)]
    loaded = [(ref[0:n].astype(F32), ref[n : 2 * n].astype(F32)) for ref in [own] + received]
    gains = [[read_gain(ref[2 * n :], k) for ref in [own] + received] for k in range(2)]
    coefficients = merge_coefficients(me, members, *gains)
    width = own.shape[1]
    new_grow = []
    totals = []
    for down in range(2):
        total = sum(coefficients[down][j - 1] * loaded[j][down] for j in range(1, radix))
        inside = [(members[j] > me) if down else (members[j] < me) for j in range(1, radix)]
        grow = product_where(inside, gains[down][1:])
        if not first:
            kept = before[2 * n + down : 2 * n + down + 1]
            total = kept * total + before[down * n : (down + 1) * n]
            grow = kept * grow
        pre_out[down * n : (down + 1) * n] = total
        new_grow.append(grow)
        group = 0.0
        for j in range(radix):
            rest = [i for i in range(radix) if i != j]
            outer = [(members[i] < members[j]) if down else (members[i] > members[j]) for i in rest]
            group = group + product_where(outer, [gains[down][i] for i in rest]) * loaded[j][down]
        totals.append(group)
    pre_out[2 * n :] = jnp.concatenate(new_grow + [jnp.zeros((6, width), F32)], axis=0)
    gain = [functools.reduce(lambda a, b: a * b, gains[k]) for k in range(2)]
    write_chunk(refs, lambda: digit(seq, stride * radix, next_radix), next_last, *totals, *gain)


def local_kernel(
    skip, x, gy, features, ba, ca, bb, cb, da, db, gx_out, maps_out, decay_out, turned_out
):
    heads, length = da.shape
    width = x.shape[1] // heads
    n = ba.shape[1]
    row, col = iotas(length, length)
    upto = (col <= row).astype(F32)
    since = (col >= row).astype(F32)
    pad = jnp.zeros((8 - heads, length), F32)
    d_ahead = jnp.concatenate([da[...], pad], axis=0)
    d_behind = jnp.concatenate([db[...], pad], axis=0)
    columns_a = masked_sums(upto, d_ahead)
    columns_b = masked_sums(since, d_behind)
    rows_a = columns_a.T
    rows_b = columns_b.T
    later, same = col > row, col == row
    raw_a = nt(ba[...], ca[...])
    raw_b = nt(bb[...], cb[...])
    affinity = jnp.where(same, raw_a + raw_b, jnp.where(later, raw_a, raw_b))
    weight_sum = jnp.zeros((length, length), F32)
    counts = jnp.concatenate([since.T, upto.T], axis=1).astype(BF16)
    cross = jnp.concatenate([row < col, row > col], axis=1).astype(F32)
    totals = []
    for h in range(heads):
        part = slice(h * width, (h + 1) * width)
        gap = jnp.where(
            later,
            rows_a[h : h + 1] - columns_a[:, h : h + 1],
            rows_b[h : h + 1] - columns_b[:, h : h + 1],
        )
        decay = jnp.exp(jnp.where(same, 0.0, gap))
        score_grad = nt(x[:, part], gy[:, part])
        weighted = score_grad * decay
        weight_sum = weight_sum + weighted
        gx_out[:, part] = nn((decay * affinity).astype(BF16), gy[:, part]) + skip[h] * gy[:, part].astype(F32)
        pieces = nn((weighted * affinity).astype(BF16), counts)
        totals.append(jnp.sum(pieces * cross, axis=0, keepdims=True))
    for h in range(heads):
        decay_out[h : h + 1] = totals[h]
    ahead = jnp.where(col >= row, weight_sum, 0.0).astype(BF16)
    behind = jnp.where(col <= row, weight_sum, 0.0).astype(BF16)
    maps_out[:, 0:n] = nn(ahead, ca[...])
    maps_out[:, n : 2 * n] = nn(ahead.T, ba[...])
    maps_out[:, 2 * n : 3 * n] = nn(behind, cb[...])
    maps_out[:, 3 * n :] = nn(behind.T, bb[...])
    turned_out[...] = features[...].T


def entering(chunks, me, radix, n):
    members = [me ^ j for j in range(radix)]
    results = []
    for received, before in chunks:
        gains = [read_gain(ref[n:]) for ref in received]
        gains = gains[:1] + gains
        coefficients = merge_coefficients(me, members, gains, gains)

        def enter(down, received=received, before=before, coefficients=coefficients):
            total = 0.0
            for coefficient, ref in zip(coefficients[down], received):
                total = total + coefficient * ref[0:n].astype(F32)
            if before is not None:
                total = before[2 * n + down : 2 * n + down + 1] * total + before[down * n : (down + 1) * n]
            return total

        results.append(enter)
    return results


def take_chunks(refs, radix, first, count):
    chunks = []
    for _ in range(count):
        received = [refs.pop(0) for _ in range(radix - 1)]
        chunks.append((received, None if first else refs.pop(0)))
    return chunks


def carry_kernel(index, steps, stride, direct, *refs):
    refs = list(refs)
    chunks = take_chunks(refs, steps[-1], len(steps) == 1, 1)
    turned, ba, bb, gx_local, factors, gx_out = [refs.pop(0) for _ in range(6)]
    seq = index()
    me = digit(seq, stride, steps[-1])
    (gradient,) = entering(chunks, me, steps[-1], ba.shape[1])
    grad_x = gx_local[...]
    for b, grad, left in ((ba, gradient(1), factors[1]), (bb, gradient(0), factors[3])):
        grad_x = grad_x + nn(b[...], grad.astype(BF16)).astype(BF16).astype(F32) * left
    grad_x = grad_x.astype(BF16)
    gx_out[...] = grad_x
    if not direct:
        refs.pop(0)[...] = nn(turned[...], grad_x).astype(BF16)
        return
    rows = refs[0].shape[1]
    for far in (1, 0):
        for j in range(1, steps[0]):
            out = refs.pop(0)
            for k in range(2):
                at = (me ^ (2 * far + k)) * steps[0] + (digit(seq, 1, steps[0]) ^ j)
                at = pl.multiple_of(at * rows, rows)
                out[k] = nn(turned[pl.ds(at, rows), :], grad_x).astype(BF16)


def fold_kernel(index, steps, far, turned, grad_x, *refs):
    received, outs = refs[: steps[0] - 1], refs[-2:]
    rows = received[0].shape[1]
    seq = index()
    for k in range(2):
        at = (digit(seq, steps[0], steps[1]) ^ (2 * far + k)) * steps[0] + digit(seq, 1, steps[0])
        share = nn(turned[pl.ds(pl.multiple_of(at * rows, rows), rows), :], grad_x[...])
        total = sum([ref[k].astype(F32) for ref in received], share)
        outs[k][...] = total.astype(outs[k].dtype)


def share_kernel(index, radix, stride, first, n_head, *refs):
    refs = list(refs)
    chunks = take_chunks(refs, radix, first, 2)
    grad_x, x, gy, w_in, ba, ca, bb, cb = [refs.pop(0) for _ in range(8)]
    maps_local, decay_local, factors = [refs.pop(0) for _ in range(3)]
    gd_a_out, gd_b_out, own_out, send_out, maps_out = refs
    heads = decay_local.shape[0]
    n = ba.shape[1]
    length, columns = x.shape
    width = columns // heads
    seq, head = index()
    gradient, state = entering(chunks, digit(seq, stride, radix), radix, n)
    grow_a, left_a, grow_b, left_b = [factors[k] for k in range(4)]
    xf, gyf = x[...].astype(F32), gy[...].astype(F32)
    row, col = iotas(length, length)
    own_rows, own_cols = iotas(8, columns)
    group = (lax.div(own_cols, width) == own_rows).astype(BF16)
    frame = lax.broadcasted_iota(jnp.int32, (length, 1), 0)

    def direction(state, grad, grow, left, b, c, at_end, later, earlier):
        gain = jnp.sum(jnp.where(frame == at_end, grow, 0.0), axis=0, keepdims=True)
        state_low, grad_low = state.astype(BF16), grad.astype(BF16)
        carried = grow * nn(c[...], state_low)
        through = gain * jnp.sum(state * grad, axis=0, keepdims=True)
        read = gyf * carried + jnp.where(frame == at_end, through, 0.0)
        write = nn(b[...], grad_low).astype(BF16).astype(F32) * left * xf
        reads = nt(group, read.astype(BF16))
        writes = nt(group, write.astype(BF16))
        grad_decay = nn(reads, later, precision=HIGH) + nn(writes, earlier, precision=HIGH)
        grad_c = nt((gyf * grow).astype(BF16), state_low)
        grad_b = nt((xf * left).astype(BF16), grad_low)
        return grad_b, grad_c, grad_decay

    gb_a, gc_a, gd_a = direction(
        state(0), gradient(1), grow_a, left_a, ba, ca, length - 1,
        (row >= col).astype(F32), (row < col).astype(F32),
    )
    gb_b, gc_b, gd_b = direction(
        state(1), gradient(0), grow_b, left_b, bb, cb, 0,
        (row <= col).astype(F32), (row > col).astype(F32),
    )
    gd_a_out[...] = gd_a[:heads] + decay_local[:, 0:length]
    gd_b_out[...] = gd_b[:heads] + decay_local[:, length:]
    maps = maps_local[...] + jnp.concatenate([gb_a, gc_a, gb_b, gc_b], axis=1)
    rows_out = w_in.shape[0] // n_head
    half = n_head // 2 * rows_out
    own_out[:, half:] = maps
    maps_out[...] = maps.astype(BF16)
    for high in range(n_head // 2):
        part = slice(high * rows_out, (high + 1) * rows_out)
        for away in range(2):
            at = pl.multiple_of((high * 2 + (lax.rem(head, 2) ^ away)) * rows_out, rows_out)
            share = nt(grad_x[...], w_in[pl.ds(at, rows_out), :])
            if away:
                send_out[:, part] = share.astype(BF16)
            else:
                own_out[:, part] = share


def pair_kernel(index, stride, rows_out, maps_at, own, received, received_maps, *refs):
    own_out, send_out, maps_out = refs[-3:]
    me = digit(index(), stride, 2)
    half = maps_at // 2
    maps = own[:, maps_at:] + received_maps[...].astype(F32)
    own_out[:, half:] = maps
    maps_out[...] = maps.astype(BF16)
    for high in range(half // rows_out):
        part = slice(high * rows_out, (high + 1) * rows_out)
        for away in range(2):
            at = pl.multiple_of((high * 2 + (me ^ away)) * rows_out, rows_out)
            total = own[:, pl.ds(at, rows_out)] + received[:, pl.ds(at, rows_out)].astype(F32)
            if away:
                send_out[:, part] = total.astype(BF16)
            else:
                own_out[:, part] = total


def head_kernel(own, other, other_maps, gf_out, *map_outs):
    columns, n = gf_out.shape[1], map_outs[0].shape[1]
    gf_out[...] = (own[:, 0:columns] + other[...].astype(F32)).astype(BF16)
    for k, out in enumerate(map_outs):
        at = columns + k * n
        out[...] = own[:, at : at + n] + other_maps[:, k * n : (k + 1) * n].astype(F32)


def weight_kernel(scale, *refs):
    *parts, out = refs
    total = 0.0
    for part in parts:
        piece = part[...].astype(F32)
        total = total + (jnp.sum(piece, axis=0) if piece.ndim == 3 else piece)
    out[...] = total * scale


def call(kernel, outs, *args, flops=0, scalars=0, held=0):
    specs = [pl.BlockSpec(memory_space=pltpu.SMEM)] * scalars
    specs += [pl.BlockSpec(memory_space=pltpu.HBM)] * held
    specs += [pl.BlockSpec(memory_space=pltpu.VMEM)] * (len(args) - scalars - held)
    outs = list(outs) + [jax.ShapeDtypeStruct(a.shape, a.dtype) for a in args[:held]]
    if held:
        args = tuple(pltpu.with_memory_space_constraint(a, pltpu.HBM) for a in args[:held]) + args[held:]
    bytes_moved = sum(math.prod(a.shape) * a.dtype.itemsize for a in args)
    bytes_moved += sum(math.prod(o.shape) * o.dtype.itemsize for o in outs)
    return pl.pallas_call(
        kernel,
        out_shape=outs,
        in_specs=specs,
        out_specs=[pl.BlockSpec(memory_space=pltpu.VMEM)] * len(outs),
        scratch_shapes=[pltpu.SemaphoreType.DMA((held,))] if held else [],
        cost_estimate=pl.CostEstimate(flops=flops, bytes_accessed=bytes_moved, transcendentals=0),
        compiler_params=pltpu.CompilerParams(vmem_limit_bytes=VMEM_LIMIT),
    )(*args)


def swap(value, axis, mask):
    return lax.ppermute(value, axis, [(i, i ^ mask) for i in range(lax.axis_size(axis))])


def far_first(sends, stride):
    jobs = list(enumerate(sends, start=1))
    return [swap(send, "seq", j * stride) for j, send in reversed(jobs)][::-1]


def local(features, w_in, b_ahead, c_ahead, b_behind, c_behind, decay_ahead, decay_behind, skip_gain, grad_y):
    peers, n_head = lax.axis_size("seq"), lax.axis_size("head")
    length, depth = features.shape
    heads, columns = decay_ahead.shape[0], w_in.shape[1]
    n = b_ahead.shape[1]
    seq_index = lambda: lax.axis_index("seq")
    head_index = lambda: lax.axis_index("head")
    both_index = lambda: (lax.axis_index("seq"), lax.axis_index("head"))
    shape = jax.ShapeDtypeStruct
    square = shape((length, columns), BF16)
    whole = shape((2 * n + GAIN_ROWS, columns), BF16)
    half = shape((n + GAIN_ROWS, columns), BF16)
    prefix = shape((2 * n + 8, columns), F32)

    steps = radices(peers)
    only = len(steps) == 1
    chunk_shapes = [half] * (steps[0] - 1) if only else [whole]
    *gradients, factors, da, db, gy, ca, cb = call(
        functools.partial(gradient_kernel, seq_index, only, columns // heads),
        chunk_shapes + [shape((4, length, columns), F32)],
        decay_ahead, decay_behind, grad_y, c_ahead, c_behind,
        flops=4 * length * n * columns,
        held=5,
    )
    *states, x, ba, bb, fs, wi = call(
        functools.partial(state_kernel, seq_index, only),
        chunk_shapes + [square],
        b_ahead, b_behind, features, w_in, factors,
        flops=2 * length * depth * columns,
        held=4,
    )
    maps = (ba, ca, bb, cb)
    gx_local, maps_local, decay_local, turned = call(
        local_kernel,
        [
            shape((length, columns), F32),
            shape((length, 4 * n), F32),
            shape((heads, 2 * length), F32),
            shape((depth, length), BF16),
        ],
        skip_gain, x, gy, fs, *maps, da, db,
        flops=2 * length * depth * columns,
        scalars=1,
    )
    arrived = []
    for chunk in (gradients, states):
        stride, before = 1, None
        for at, radix in enumerate(steps[:-1]):
            received = [swap(chunk[0], "seq", j * stride) for j in range(1, radix)]
            next_last = at == len(steps) - 2
            following = steps[at + 1]
            before, *chunk = call(
                functools.partial(step_kernel, seq_index, stride, radix, at == 0, next_last, following),
                [prefix] + ([half] * (following - 1) if next_last else [whole]),
                chunk[0], *received, *([] if at == 0 else [before]),
                flops=20 * n * columns,
            )
            stride *= radix
        arrived.append(far_first(chunk, stride) + ([] if only else [before]))
    rows_out, rows_w = depth // n_head, depth // peers
    direct = len(steps) == 2 and rows_w % 16 == 0
    pieces = [shape((2, rows_w, columns), BF16)] * (2 * (steps[0] - 1)) if direct else [shape((depth, columns), BF16)]
    grad_x, *sends = call(
        functools.partial(carry_kernel, seq_index, steps, stride, direct),
        [square] + pieces,
        *arrived[0], turned, ba, bb, gx_local, factors,
        flops=length * depth * columns,
    )
    after = []
    if direct:
        received = [swap(send, "seq", 1 + k % (steps[0] - 1)) for k, send in enumerate(sends)]
        block, block_low = shape((rows_w, columns), F32), shape((rows_w, columns), BF16)
        each = len(received) // 2
        fold = lambda distance, outs, *args: call(
            functools.partial(fold_kernel, seq_index, steps, distance),
            outs, turned, grad_x, *args,
            flops=4 * rows_w * length * columns,
        )
        far = fold(1, [block_low, block_low], *received[:each])
        near = fold(0, [block, block_low], *received[each:], far[0])
        weight_parts = [near[0]] + [
            swap(send, "seq", j * stride) for send, j in ((far[1], 3), (far[0], 2), (near[1], 1))
        ]
        after = [near[0]]
    else:
        weight_parts = [lax.all_to_all(sends[0].reshape(peers, rows_w, columns), "seq", 0, 0)]
    def head_shapes(blocks):
        wide = blocks * rows_out
        return [shape((length, wide + 4 * n), F32), shape((length, wide), BF16), shape((length, 4 * n), BF16)]

    mask, blocks = 2, n_head // 2
    gd_ahead, gd_behind, own_share, *sends = call(
        functools.partial(share_kernel, both_index, steps[-1], stride, only, n_head),
        [shape((heads, length), F32)] * 2 + head_shapes(blocks),
        *arrived[0], *arrived[1], grad_x, x, gy, wi, *maps, maps_local, decay_local, factors,
        flops=3 * length * depth * columns,
    )
    others = [swap(send, "head", 1) for send in sends]
    while mask < n_head:
        own_share, *sends = call(
            functools.partial(pair_kernel, head_index, mask, rows_out, blocks * rows_out),
            head_shapes(blocks // 2),
            own_share, *others, *after,
            flops=4 * length * depth,
        )
        others = [swap(send, "head", mask) for send in sends]
        mask, blocks = mask * 2, blocks // 2
    grad_features, *grad_maps = call(
        head_kernel,
        [shape((length, rows_out), BF16)] + [shape((length, n), F32)] * 4,
        own_share, *others,
    )
    (grad_w_in,) = call(
        functools.partial(weight_kernel, 1.0 / math.sqrt(length * peers)),
        [shape((rows_w, columns), F32)],
        *weight_parts,
    )
    return (grad_features, grad_w_in, *grad_maps, gd_ahead, gd_behind)


def solution(mesh):
    in_specs = (
        P("seq", None),
        P(None, "head"),
        P("seq", None),
        P("seq", None),
        P("seq", None),
        P("seq", None),
        P("head", "seq"),
        P("head", "seq"),
        P("head"),
        P("seq", "head"),
    )
    out_specs = (
        P("seq", "head"),
        P("seq", "head"),
        P("seq", None),
        P("seq", None),
        P("seq", None),
        P("seq", None),
        P("head", "seq"),
        P("head", "seq"),
    )
    return jax.shard_map(local, mesh=mesh, in_specs=in_specs, out_specs=out_specs, check_vma=False)
```

```python
import functools
import math

import jax
import jax.numpy as jnp
from jax import lax
from jax.experimental import pallas as pl
from jax.experimental.pallas import tpu as pltpu
from jax.sharding import PartitionSpec as P

F32 = jnp.float32
BF16 = jnp.bfloat16
HIGH = lax.Precision.HIGHEST
GAIN_ROWS = 16
FLOPS_PER_MICRO = 1.15e9
VMEM_LIMIT = 48 * 1024 * 1024


def nn(a, b, **kw):
    return lax.dot_general(a, b, (((1,), (0,)), ((), ())), preferred_element_type=F32, **kw)


def nt(a, b, **kw):
    return lax.dot_general(a, b, (((1,), (1,)), ((), ())), preferred_element_type=F32, **kw)


def iotas(rows, cols):
    return (
        lax.broadcasted_iota(jnp.int32, (rows, cols), 0),
        lax.broadcasted_iota(jnp.int32, (rows, cols), 1),
    )


def spread_rows(values, width):
    heads, length = values.shape
    return jnp.concatenate(
        [jnp.broadcast_to(values[h : h + 1], (width, length)) for h in range(heads)], axis=0
    )


def split3(value):
    high = value.astype(BF16)
    rest = value - high.astype(F32)
    middle = rest.astype(BF16)
    low = (rest - middle.astype(F32)).astype(BF16)
    return high, middle, low


def masked_sums(masks, values):
    masks = masks.astype(BF16)
    return sum(nt(masks, part) for part in split3(values))


def decay_factors(d_ahead, d_behind, width):
    length = d_ahead.shape[1]
    row, col = iotas(length, length)
    upto = (col <= row).astype(F32)
    since = (col >= row).astype(F32)
    ahead = masked_sums(
        jnp.concatenate([upto, 1.0 - upto], axis=0), spread_rows(d_ahead, width)
    )
    behind = masked_sums(
        jnp.concatenate([since, 1.0 - since], axis=0), spread_rows(d_behind, width)
    )
    ahead, behind = jnp.exp(ahead), jnp.exp(behind)
    return ahead[:length], ahead[length:], behind[:length], behind[length:]


def radices(peers):
    bits = peers.bit_length() - 1
    return ([2] if bits % 2 else []) + [4] * (bits // 2)


def digit(index, stride, radix):
    return lax.rem(lax.div(index, stride), radix)


def read_gain(block, k=0):
    rows = block.astype(F32)[3 * k : 3 * k + 3]
    return rows[0:1] + rows[1:2] + rows[2:3]


def gain_block(*gains):
    rows = [p.astype(F32) for gain in gains for p in split3(gain)]
    pad = jnp.zeros((GAIN_ROWS - len(rows), gains[0].shape[1]), F32)
    return jnp.concatenate(rows + [pad], axis=0).astype(BF16)


def product_where(conditions, gains):
    result = jnp.ones_like(gains[0])
    for condition, gain in zip(conditions, gains):
        result = jnp.where(condition, result * gain, result)
    return result


def merge_coefficients(me, members, gains_up, gains_down):
    below, above = [], []
    others = range(1, len(members))
    for j in others:
        q = members[j]
        low = product_where(
            [jnp.logical_and(members[i] > q, members[i] < me) for i in others], [gains_up[i] for i in others]
        )
        high = product_where(
            [jnp.logical_and(members[i] < q, members[i] > me) for i in others], [gains_down[i] for i in others]
        )
        below.append(jnp.where(q < me, low, 0.0))
        above.append(jnp.where(q > me, high, 0.0))
    return below, above


def write_whole(out, up, down, gain_up, gain_down):
    n = up.shape[0]
    out[0:n] = up.astype(BF16)
    out[n : 2 * n] = down.astype(BF16)
    out[2 * n :] = gain_block(gain_up, gain_down)


def write_halves(outs, up, down, gain_up, gain_down, me):
    n = up.shape[0]
    blocks = gain_block(gain_up), gain_block(gain_down)
    up, down = up.astype(BF16), down.astype(BF16)
    for j, out in enumerate(outs, start=1):
        upward = (me ^ j) > me
        out[0:n] = jnp.where(upward, up, down)
        out[n:] = jnp.where(upward, *blocks)


def write_chunk(outs, me, last, *chunk):
    if last:
        write_halves(outs, *chunk, me())
    else:
        write_whole(outs[0], *chunk)


def start_copies(sources, targets, sems):
    copies = [pltpu.make_async_copy(s, t, sems.at[k]) for k, (s, t) in enumerate(zip(sources, targets))]
    for copy in copies:
        copy.start()
    return copies


def gradient_kernel(me, last, width, *refs):
    *refs, sems = refs
    sources, outs, held = refs[:6], refs[6:-6], refs[-6:]
    copies = start_copies(sources, held, sems)
    da, db, gy, ca, cb, _ = held
    for copy in copies[:2]:
        copy.wait()
    factors = decay_factors(da[...], db[...], width)
    *sends, factors_out = outs
    for k in range(4):
        factors_out[k] = factors[k]
    grow_a, _, grow_b, _ = factors
    for copy in copies[2:]:
        copy.wait()
    gyf = gy[...].astype(F32)
    up = nn(cb[...].T, (gyf * grow_b).astype(BF16))
    down = nn(ca[...].T, (gyf * grow_a).astype(BF16))
    write_chunk(sends, me, last, up, down, grow_b[0:1], grow_a[gyf.shape[0] - 1 :])


def state_kernel(me, last, *refs):
    *refs, sems = refs
    sources, factors, outs, held = refs[:4], refs[4], refs[5:-4], refs[-4:]
    copies = start_copies(sources, held, sems)
    ba, bb, features, w_in = held
    for copy in copies:
        copy.wait()
    *sends, x_out = outs
    x = nn(features[...], w_in[...]).astype(BF16)
    x_out[...] = x
    xf = x.astype(F32)
    up = nn(ba[...].T, (xf * factors[1]).astype(BF16))
    down = nn(bb[...].T, (xf * factors[3]).astype(BF16))
    write_chunk(sends, me, last, up, down, factors[0, x.shape[0] - 1 :], factors[2, 0:1])


def step_kernel(index, stride, radix, first, next_last, next_radix, *refs):
    refs = list(refs)
    own = refs.pop(0)
    received = [refs.pop(0) for _ in range(radix - 1)]
    before, outs = refs[0], refs[-(next_radix if next_last else 2) :]
    pre_out, *outs = outs
    n = (own.shape[0] - GAIN_ROWS) // 2
    seq = index()
    me = digit(seq, stride, radix)
    members = [me ^ j for j in range(radix)]
    loaded = [(ref[0:n].astype(F32), ref[n : 2 * n].astype(F32)) for ref in [own] + received]
    gains = [[read_gain(ref[2 * n :], k) for ref in [own] + received] for k in range(2)]
    coefficients = merge_coefficients(me, members, *gains)
    width = own.shape[1]
    new_grow = []
    totals = []
    for down in range(2):
        total = sum(coefficients[down][j - 1] * loaded[j][down] for j in range(1, radix))
        inside = [(members[j] > me) if down else (members[j] < me) for j in range(1, radix)]
        grow = product_where(inside, gains[down][1:])
        if not first:
            kept = before[2 * n + down : 2 * n + down + 1]
            total = kept * total + before[down * n : (down + 1) * n]
            grow = kept * grow
        pre_out[down * n : (down + 1) * n] = total
        new_grow.append(grow)
        group = 0.0
        for j in range(radix):
            rest = [i for i in range(radix) if i != j]
            outer = [(members[i] < members[j]) if down else (members[i] > members[j]) for i in rest]
            group = group + product_where(outer, [gains[down][i] for i in rest]) * loaded[j][down]
        totals.append(group)
    pre_out[2 * n :] = jnp.concatenate(new_grow + [jnp.zeros((6, width), F32)], axis=0)
    gain = [functools.reduce(lambda a, b: a * b, gains[k]) for k in range(2)]
    write_chunk(outs, lambda: digit(seq, stride * radix, next_radix), next_last, *totals, *gain)


def local_kernel(
    skip, x, gy, features, ba, ca, bb, cb, da, db, gx_out, maps_out, decay_out, turned_out
):
    heads, length = da.shape
    width = x.shape[1] // heads
    n = ba.shape[1]
    row, col = iotas(length, length)
    upto = (col <= row).astype(F32)
    since = (col >= row).astype(F32)
    pad = jnp.zeros((8 - heads, length), F32)
    d_ahead = jnp.concatenate([da[...], pad], axis=0)
    d_behind = jnp.concatenate([db[...], pad], axis=0)
    columns_a = masked_sums(upto, d_ahead)
    columns_b = masked_sums(since, d_behind)
    rows_a = columns_a.T
    rows_b = columns_b.T
    later, same = col > row, col == row
    raw_a = nt(ba[...], ca[...])
    raw_b = nt(bb[...], cb[...])
    affinity = jnp.where(same, raw_a + raw_b, jnp.where(later, raw_a, raw_b))
    weight_sum = jnp.zeros((length, length), F32)
    counts = jnp.concatenate([since.T, upto.T], axis=1).astype(BF16)
    cross = jnp.concatenate([row < col, row > col], axis=1).astype(F32)
    totals = []
    for h in range(heads):
        part = slice(h * width, (h + 1) * width)
        gap = jnp.where(
            later,
            rows_a[h : h + 1] - columns_a[:, h : h + 1],
            rows_b[h : h + 1] - columns_b[:, h : h + 1],
        )
        decay = jnp.exp(jnp.where(same, 0.0, gap))
        score_grad = nt(x[:, part], gy[:, part])
        weighted = score_grad * decay
        weight_sum = weight_sum + weighted
        gx_out[:, part] = nn((decay * affinity).astype(BF16), gy[:, part]) + skip[:, h : h + 1] * gy[:, part].astype(F32)
        pieces = nn((weighted * affinity).astype(BF16), counts)
        totals.append(jnp.sum(pieces * cross, axis=0, keepdims=True))
    for h in range(heads):
        decay_out[h : h + 1] = totals[h]
    ahead = jnp.where(col >= row, weight_sum, 0.0).astype(BF16)
    behind = jnp.where(col <= row, weight_sum, 0.0).astype(BF16)
    maps_out[:, 0:n] = nn(ahead, ca[...])
    maps_out[:, n : 2 * n] = nn(ahead.T, ba[...])
    maps_out[:, 2 * n : 3 * n] = nn(behind, cb[...])
    maps_out[:, 3 * n :] = nn(behind.T, bb[...])
    turned_out[...] = features[...].T


def entering(chunks, seq, peers, n):
    results = []
    for received, before in chunks:
        radix = len(received) + 1
        me = digit(seq, peers // radix, radix)
        members = [me ^ j for j in range(radix)]
        gains = [read_gain(ref[n:]) for ref in received]
        gains = gains[:1] + gains
        coefficients = merge_coefficients(me, members, gains, gains)

        def enter(down, received=received, before=before, coefficients=coefficients):
            total = 0.0
            for coefficient, ref in zip(coefficients[down], received):
                total = total + coefficient * ref[0:n].astype(F32)
            if before is not None:
                total = before[2 * n + down : 2 * n + down + 1] * total + before[down * n : (down + 1) * n]
            return total

        results.append(enter)
    return results


def take_chunks(refs, lasts, first):
    chunks = []
    for radix in lasts:
        received = [refs.pop(0) for _ in range(radix - 1)]
        chunks.append((received, None if first else refs.pop(0)))
    return chunks


def carry_kernel(index, steps, stride, direct, *refs):
    refs = list(refs)
    chunks = take_chunks(refs, steps[-1:], len(steps) == 1)
    turned, ba, bb, gx_local, factors = refs[:5]
    gx_out, grad_out, *outs = refs[-steps[0] - 1 :] if direct else refs[-3:]
    seq = index()
    me = digit(seq, stride, steps[-1])
    (gradient,) = entering(chunks, seq, stride * steps[-1], ba.shape[1])
    grad_x = gx_local[...]
    for k, (b, left) in enumerate(((ba, factors[1]), (bb, factors[3]))):
        grad = gradient(1 - k).astype(BF16)
        grad_out[k] = grad
        grad_x = grad_x + nn(b[...], grad).astype(BF16).astype(F32) * left
    grad_x = grad_x.astype(BF16)
    gx_out[...] = grad_x
    if not direct:
        outs[0][...] = nn(turned[...], grad_x).astype(BF16)
        return
    rows = outs[0].shape[1]
    for j, out in enumerate(outs, start=1):
        for k in range(4):
            at = (me ^ k) * steps[0] + (digit(seq, 1, steps[0]) ^ j)
            out[k] = nn(turned[pl.ds(pl.multiple_of(at * rows, rows), rows), :], grad_x).astype(BF16)


def fold_kernel(index, steps, turned, grad_x, *refs):
    received, outs = refs[: steps[0] - 1], refs[-4:]
    rows = received[0].shape[1]
    seq = index()
    for k in range(4):
        at = (digit(seq, steps[0], steps[1]) ^ k) * steps[0] + digit(seq, 1, steps[0])
        share = nn(turned[pl.ds(pl.multiple_of(at * rows, rows), rows), :], grad_x[...])
        total = sum([ref[k].astype(F32) for ref in received], share)
        outs[k][...] = total.astype(outs[k].dtype)


def head_groups(heads, columns):
    rows, cols = iotas(8, columns)
    return (lax.div(cols, columns // heads) == rows).astype(BF16)


def share_kernel(index, n_head, grad_x, grads, x, w_in, ba, bb, maps_local, decay_local, factors, *outs):
    decay_out, own_out, send_out = outs
    heads = decay_local.shape[0]
    n = ba.shape[1]
    length, columns = x.shape
    xf = x[...].astype(F32)
    row, col = iotas(length, length)
    group = head_groups(heads, columns)
    rows_out = w_in.shape[0] // n_head
    half = n_head // 2 * rows_out
    for k, (b, earlier) in enumerate(((ba, row < col), (bb, row > col))):
        left, grad = factors[2 * k + 1], grads[k]
        write = nn(b[...], grad).astype(BF16).astype(F32) * left * xf
        writes = nt(group, write.astype(BF16))
        part = slice(k * length, (k + 1) * length)
        decay_out[:, part] = decay_local[:, part] + nn(writes, earlier.astype(F32), precision=HIGH)[:heads]
        grad_b = maps_local[:, 2 * k * n : (2 * k + 1) * n] + nt((xf * left).astype(BF16), grad)
        at = half + k * n
        own_out[:, at : at + n] = grad_b
        send_out[:, at : at + n] = grad_b.astype(BF16)
    for high in range(n_head // 2):
        part = slice(high * rows_out, (high + 1) * rows_out)
        for away in range(2):
            at = pl.multiple_of((high * 2 + (lax.rem(index(), 2) ^ away)) * rows_out, rows_out)
            share = nt(grad_x[...], w_in[pl.ds(at, rows_out), :])
            if away:
                send_out[:, part] = share.astype(BF16)
            else:
                own_out[:, part] = share


def state_share_kernel(index, radix, first, peers, *refs):
    refs = list(refs)
    chunks = take_chunks(refs, [radix], first)
    grads, gy, ca, cb, maps_local, decay_part, factors = [refs.pop(0) for _ in range(7)]
    gd_outs, own_out, send_out = refs[-4:-2], refs[-2], refs[-1]
    heads = decay_part.shape[0]
    n = ca.shape[1]
    length, columns = gy.shape
    (state,) = entering(chunks, index(), peers, n)
    gyf = gy[...].astype(F32)
    row, col = iotas(length, length)
    group = head_groups(heads, columns)
    frame = lax.broadcasted_iota(jnp.int32, (length, 1), 0)
    for k, (c, at_end, later) in enumerate(((ca, length - 1, row >= col), (cb, 0, row <= col))):
        grow, entered = factors[2 * k], state(k)
        low = entered.astype(BF16)
        gain = grow[at_end : at_end + 1]
        through = gain * jnp.sum(entered * grads[k].astype(F32), axis=0, keepdims=True)
        read = gyf * (grow * nn(c[...], low)) + jnp.where(frame == at_end, through, 0.0)
        reads = nt(group, read.astype(BF16))
        gd = nn(reads, later.astype(F32), precision=HIGH)[:heads]
        gd_outs[k][...] = gd + decay_part[:, k * length : (k + 1) * length]
        grad_c = maps_local[:, (2 * k + 1) * n : (2 * k + 2) * n] + nt((gyf * grow).astype(BF16), low)
        own_out[:, k * n : (k + 1) * n] = grad_c
        send_out[:, k * n : (k + 1) * n] = grad_c.astype(BF16)


def pair_kernel(index, stride, rows_out, maps_at, own, received, *refs):
    own_out, send_out = refs[-2:]
    me = digit(index(), stride, 2)
    half = maps_at // 2
    maps = own[:, maps_at:] + received[:, maps_at:].astype(F32)
    own_out[:, half:] = maps
    send_out[:, half:] = maps.astype(BF16)
    for high in range(half // rows_out):
        part = slice(high * rows_out, (high + 1) * rows_out)
        for away in range(2):
            at = pl.multiple_of((high * 2 + (me ^ away)) * rows_out, rows_out)
            total = own[:, pl.ds(at, rows_out)] + received[:, pl.ds(at, rows_out)].astype(F32)
            if away:
                send_out[:, part] = total.astype(BF16)
            else:
                own_out[:, part] = total


def last_kernel(scale, own, other, own_c, other_c, *refs):
    parts, gf_out, gw_out, map_outs = refs[:-6], refs[-6], refs[-5], refs[-4:]
    columns, n = gf_out.shape[1], map_outs[0].shape[1]
    gf_out[...] = (own[:, 0:columns] + other[:, 0:columns].astype(F32)).astype(BF16)
    for k in range(2):
        at, at_c = columns + k * n, k * n
        map_outs[2 * k][...] = own[:, at : at + n] + other[:, at : at + n].astype(F32)
        map_outs[2 * k + 1][...] = own_c[:, at_c : at_c + n] + other_c[:, at_c : at_c + n].astype(F32)
    total = 0.0
    for part in parts:
        piece = part[...].astype(F32)
        total = total + (jnp.sum(piece, axis=0) if piece.ndim == 3 else piece)
    gw_out[...] = total * scale


def call(kernel, outs, *args, micros=0.0, held=0):
    specs = [pl.BlockSpec(memory_space=pltpu.HBM)] * held
    specs += [pl.BlockSpec(memory_space=pltpu.VMEM)] * (len(args) - held)
    outs = list(outs) + [jax.ShapeDtypeStruct(a.shape, a.dtype) for a in args[:held]]
    if held:
        args = tuple(pltpu.with_memory_space_constraint(a, pltpu.HBM) for a in args[:held]) + args[held:]
    cost = pl.CostEstimate(flops=int(micros * FLOPS_PER_MICRO), bytes_accessed=0, transcendentals=0)
    return pl.pallas_call(
        kernel,
        out_shape=outs,
        in_specs=specs,
        out_specs=[pl.BlockSpec(memory_space=pltpu.VMEM)] * len(outs),
        scratch_shapes=[pltpu.SemaphoreType.DMA((held,))] if held else [],
        cost_estimate=cost,
        compiler_params=pltpu.CompilerParams(vmem_limit_bytes=VMEM_LIMIT),
    )(*args)


def swap(value, axis, mask):
    return lax.ppermute(value, axis, [(i, i ^ mask) for i in range(lax.axis_size(axis))])


def far_first(sends, stride):
    jobs = list(enumerate(sends, start=1))
    return [swap(send, "seq", j * stride) for j, send in reversed(jobs)][::-1]


def local(features, w_in, b_ahead, c_ahead, b_behind, c_behind, decay_ahead, decay_behind, skip_gain, grad_y):
    peers, n_head = lax.axis_size("seq"), lax.axis_size("head")
    length, depth = features.shape
    heads, columns = decay_ahead.shape[0], w_in.shape[1]
    n = b_ahead.shape[1]
    seq_index = lambda: lax.axis_index("seq")
    head_index = lambda: lax.axis_index("head")
    shape = jax.ShapeDtypeStruct
    square = shape((length, columns), BF16)
    whole = shape((2 * n + GAIN_ROWS, columns), BF16)
    half = shape((n + GAIN_ROWS, columns), BF16)
    prefix = shape((2 * n + 8, columns), F32)

    steps = radices(peers)
    only = len(steps) == 1
    chunk_shapes = [half] * (steps[0] - 1) if only else [whole]
    *gradients, factors, da, db, gy, ca, cb, skip = call(
        functools.partial(gradient_kernel, seq_index, only, columns // heads),
        chunk_shapes + [shape((4, length, columns), F32)],
        decay_ahead, decay_behind, grad_y, c_ahead, c_behind, skip_gain.reshape(1, heads),
        micros=1.35,
        held=6,
    )
    *states, x, ba, bb, fs, wi = call(
        functools.partial(state_kernel, seq_index, only),
        chunk_shapes + [square],
        b_ahead, b_behind, features, w_in, factors,
        micros=1.65,
        held=4,
    )
    maps = (ba, ca, bb, cb)
    gx_local, maps_local, decay_local, turned = call(
        local_kernel,
        [
            shape((length, columns), F32),
            shape((length, 4 * n), F32),
            shape((heads, 2 * length), F32),
            shape((depth, length), BF16),
        ],
        skip, x, gy, fs, *maps, da, db,
        micros=0.9,
    )
    def merges(chunk):
        stride, before = 1, None
        for at, radix in enumerate(steps[:-1]):
            received = [swap(chunk[0], "seq", j * stride) for j in range(1, radix)]
            next_last = at == len(steps) - 2
            following = steps[at + 1]
            count = (following - 1) if next_last else 1
            before, *chunk = call(
                functools.partial(step_kernel, seq_index, stride, radix, at == 0, next_last, following),
                [prefix] + ([half] if next_last else [whole]) * count,
                chunk[0], *received, *([] if at == 0 else [before]),
                micros=0.15,
            )
            stride *= radix
        return far_first(chunk, stride) + ([] if only else [before])

    stride = peers // steps[-1]
    gradient_in = merges(gradients)
    state_in = merges(states)
    rows_out, rows_w = depth // n_head, depth // peers
    direct = len(steps) == 2 and rows_w % 16 == 0
    pieces = [shape((4, rows_w, columns), BF16)] * (steps[0] - 1) if direct else [shape((depth, columns), BF16)]
    grad_x, grads, *sends = call(
        functools.partial(carry_kernel, seq_index, steps, stride, direct),
        [square, shape((2, n, columns), BF16)] + pieces,
        *gradient_in, turned, ba, bb, gx_local, factors,
        micros=0.5,
    )
    if direct:
        received = [swap(send, "seq", j) for j, send in enumerate(sends, start=1)]
        own_weight, *sends = call(
            functools.partial(fold_kernel, seq_index, steps),
            [shape((rows_w, columns), F32)] + [shape((rows_w, columns), BF16)] * 3,
            turned, grad_x, *received,
            micros=0.22,
        )
        weight_parts = [own_weight] + far_first(sends, stride)
    else:
        weight_parts = [lax.all_to_all(sends[0].reshape(peers, rows_w, columns), "seq", 0, 0)]
    def head_shapes(blocks):
        wide = (length, blocks * rows_out + 2 * n)
        return [shape(wide, F32), shape(wide, BF16)]

    def head_sums(own, send, blocks):
        other, mask = swap(send, "head", 1), 2
        while mask < n_head:
            own, send = call(
                functools.partial(pair_kernel, head_index, mask, rows_out, blocks * rows_out),
                head_shapes(blocks // 2),
                own, other,
                micros=0.2,
            )
            other = swap(send, "head", mask)
            mask, blocks = mask * 2, blocks // 2
        return own, other

    decay_part, *shares = call(
        functools.partial(share_kernel, head_index, n_head),
        [shape((heads, 2 * length), F32)] + head_shapes(n_head // 2),
        grad_x, grads, x, wi, ba, bb, maps_local, decay_local, factors,
        micros=1.0,
    )
    shares = head_sums(*shares, n_head // 2)
    gd_ahead, gd_behind, *shares_c = call(
        functools.partial(state_share_kernel, seq_index, steps[-1], only, peers),
        [shape((heads, length), F32)] * 2 + head_shapes(0),
        *state_in, grads, gy, ca, cb, maps_local, decay_part, factors,
        micros=1.4,
    )
    shares_c = head_sums(*shares_c, 0)
    grad_features, grad_w_in, *grad_maps = call(
        functools.partial(last_kernel, 1.0 / math.sqrt(length * peers)),
        [shape((length, rows_out), BF16), shape((rows_w, columns), F32)] + [shape((length, n), F32)] * 4,
        *shares, *shares_c, *weight_parts,
        micros=0.8,
    )
    return (grad_features, grad_w_in, *grad_maps, gd_ahead, gd_behind)


def solution(mesh):
    in_specs = (
        P("seq", None),
        P(None, "head"),
        P("seq", None),
        P("seq", None),
        P("seq", None),
        P("seq", None),
        P("head", "seq"),
        P("head", "seq"),
        P("head"),
        P("seq", "head"),
    )
    out_specs = (
        P("seq", "head"),
        P("seq", "head"),
        P("seq", None),
        P("seq", None),
        P("seq", None),
        P("seq", None),
        P("head", "seq"),
        P("head", "seq"),
    )
    return jax.shard_map(local, mesh=mesh, in_specs=in_specs, out_specs=out_specs, check_vma=False)
```

```python
import functools
import math

import jax
import jax.numpy as jnp
from jax import lax
from jax.experimental import pallas as pl
from jax.experimental.pallas import tpu as pltpu
from jax.sharding import PartitionSpec as P

F32 = jnp.float32
BF16 = jnp.bfloat16
HIGH = lax.Precision.HIGHEST
GAIN_ROWS = 16
FLOPS_PER_MICRO = 1.15e9
VMEM_LIMIT = 48 * 1024 * 1024


def nn(a, b, **kw):
    return lax.dot_general(a, b, (((1,), (0,)), ((), ())), preferred_element_type=F32, **kw)


def nt(a, b, **kw):
    return lax.dot_general(a, b, (((1,), (1,)), ((), ())), preferred_element_type=F32, **kw)


def iotas(rows, cols):
    return (
        lax.broadcasted_iota(jnp.int32, (rows, cols), 0),
        lax.broadcasted_iota(jnp.int32, (rows, cols), 1),
    )


def spread_rows(values, width):
    heads, length = values.shape
    return jnp.concatenate(
        [jnp.broadcast_to(values[h : h + 1], (width, length)) for h in range(heads)], axis=0
    )


def split3(value):
    high = value.astype(BF16)
    rest = value - high.astype(F32)
    middle = rest.astype(BF16)
    low = (rest - middle.astype(F32)).astype(BF16)
    return high, middle, low


def masked_sums(masks, values):
    masks = masks.astype(BF16)
    return sum(nt(masks, part) for part in split3(values))


def decay_factors(d_ahead, d_behind, width):
    length = d_ahead.shape[1]
    row, col = iotas(length, length)
    upto = (col <= row).astype(F32)
    since = (col >= row).astype(F32)
    ahead = masked_sums(
        jnp.concatenate([upto, 1.0 - upto], axis=0), spread_rows(d_ahead, width)
    )
    behind = masked_sums(
        jnp.concatenate([since, 1.0 - since], axis=0), spread_rows(d_behind, width)
    )
    ahead, behind = jnp.exp(ahead), jnp.exp(behind)
    return ahead[:length], ahead[length:], behind[:length], behind[length:]


def radices(peers):
    bits = peers.bit_length() - 1
    return ([2] if bits % 2 else []) + [4] * (bits // 2)


def digit(index, stride, radix):
    return lax.rem(lax.div(index, stride), radix)


def read_gain(block, k=0):
    rows = block.astype(F32)[3 * k : 3 * k + 3]
    return rows[0:1] + rows[1:2] + rows[2:3]


def gain_block(*gains):
    rows = [p.astype(F32) for gain in gains for p in split3(gain)]
    pad = jnp.zeros((GAIN_ROWS - len(rows), gains[0].shape[1]), F32)
    return jnp.concatenate(rows + [pad], axis=0).astype(BF16)


def product_where(conditions, gains):
    result = jnp.ones_like(gains[0])
    for condition, gain in zip(conditions, gains):
        result = jnp.where(condition, result * gain, result)
    return result


def merge_coefficients(me, members, gains_up, gains_down):
    below, above = [], []
    others = range(1, len(members))
    for j in others:
        q = members[j]
        low = product_where(
            [jnp.logical_and(members[i] > q, members[i] < me) for i in others], [gains_up[i] for i in others]
        )
        high = product_where(
            [jnp.logical_and(members[i] < q, members[i] > me) for i in others], [gains_down[i] for i in others]
        )
        below.append(jnp.where(q < me, low, 0.0))
        above.append(jnp.where(q > me, high, 0.0))
    return below, above


def write_whole(out, up, down, gain_up, gain_down):
    n = up.shape[0]
    out[0:n] = up.astype(BF16)
    out[n : 2 * n] = down.astype(BF16)
    out[2 * n :] = gain_block(gain_up, gain_down)


def write_halves(outs, up, down, gain_up, gain_down, me):
    n = up.shape[0]
    blocks = gain_block(gain_up), gain_block(gain_down)
    up, down = up.astype(BF16), down.astype(BF16)
    for j, out in enumerate(outs, start=1):
        upward = (me ^ j) > me
        out[0:n] = jnp.where(upward, up, down)
        out[n:] = jnp.where(upward, *blocks)


def write_chunk(outs, me, last, *chunk):
    if last:
        write_halves(outs, *chunk, me())
    else:
        write_whole(outs[0], *chunk)


def start_copies(sources, targets, sems):
    copies = [pltpu.make_async_copy(s, t, sems.at[k]) for k, (s, t) in enumerate(zip(sources, targets))]
    for copy in copies:
        copy.start()
    return copies


def gradient_kernel(me, last, width, *refs):
    *refs, sems = refs
    sources, outs, held = refs[:6], refs[6:-6], refs[-6:]
    copies = start_copies(sources, held, sems)
    da, db, gy, ca, cb, _ = held
    for copy in copies[:2]:
        copy.wait()
    factors = decay_factors(da[...], db[...], width)
    *sends, factors_out = outs
    for k in range(4):
        factors_out[k] = factors[k]
    grow_a, _, grow_b, _ = factors
    for copy in copies[2:]:
        copy.wait()
    gyf = gy[...].astype(F32)
    up = nn(cb[...].T, (gyf * grow_b).astype(BF16))
    down = nn(ca[...].T, (gyf * grow_a).astype(BF16))
    write_chunk(sends, me, last, up, down, grow_b[0:1], grow_a[gyf.shape[0] - 1 :])


def state_kernel(me, last, *refs):
    *refs, sems = refs
    sources, factors, outs, held = refs[:4], refs[4], refs[5:-4], refs[-4:]
    copies = start_copies(sources, held, sems)
    ba, bb, features, w_in = held
    for copy in copies:
        copy.wait()
    *sends, x_out = outs
    x = nn(features[...], w_in[...]).astype(BF16)
    x_out[...] = x
    xf = x.astype(F32)
    up = nn(ba[...].T, (xf * factors[1]).astype(BF16))
    down = nn(bb[...].T, (xf * factors[3]).astype(BF16))
    write_chunk(sends, me, last, up, down, factors[0, x.shape[0] - 1 :], factors[2, 0:1])


def step_kernel(index, stride, radix, first, next_last, next_radix, *refs):
    refs = list(refs)
    own = refs.pop(0)
    received = [refs.pop(0) for _ in range(radix - 1)]
    before, outs = refs[0], refs[-(next_radix if next_last else 2) :]
    pre_out, *outs = outs
    n = (own.shape[0] - GAIN_ROWS) // 2
    seq = index()
    me = digit(seq, stride, radix)
    members = [me ^ j for j in range(radix)]
    loaded = [(ref[0:n].astype(F32), ref[n : 2 * n].astype(F32)) for ref in [own] + received]
    gains = [[read_gain(ref[2 * n :], k) for ref in [own] + received] for k in range(2)]
    coefficients = merge_coefficients(me, members, *gains)
    width = own.shape[1]
    new_grow = []
    totals = []
    for down in range(2):
        total = sum(coefficients[down][j - 1] * loaded[j][down] for j in range(1, radix))
        inside = [(members[j] > me) if down else (members[j] < me) for j in range(1, radix)]
        grow = product_where(inside, gains[down][1:])
        if not first:
            kept = before[2 * n + down : 2 * n + down + 1]
            total = kept * total + before[down * n : (down + 1) * n]
            grow = kept * grow
        pre_out[down * n : (down + 1) * n] = total
        new_grow.append(grow)
        group = 0.0
        for j in range(radix):
            rest = [i for i in range(radix) if i != j]
            outer = [(members[i] < members[j]) if down else (members[i] > members[j]) for i in rest]
            group = group + product_where(outer, [gains[down][i] for i in rest]) * loaded[j][down]
        totals.append(group)
    pre_out[2 * n :] = jnp.concatenate(new_grow + [jnp.zeros((6, width), F32)], axis=0)
    gain = [functools.reduce(lambda a, b: a * b, gains[k]) for k in range(2)]
    write_chunk(outs, lambda: digit(seq, stride * radix, next_radix), next_last, *totals, *gain)


def local_kernel(
    skip, x, gy, features, ba, ca, bb, cb, da, db, gx_out, maps_out, decay_out, turned_out
):
    heads, length = da.shape
    width = x.shape[1] // heads
    n = ba.shape[1]
    row, col = iotas(length, length)
    upto = (col <= row).astype(F32)
    since = (col >= row).astype(F32)
    pad = jnp.zeros((8 - heads, length), F32)
    d_ahead = jnp.concatenate([da[...], pad], axis=0)
    d_behind = jnp.concatenate([db[...], pad], axis=0)
    columns_a = masked_sums(upto, d_ahead)
    columns_b = masked_sums(since, d_behind)
    rows_a = columns_a.T
    rows_b = columns_b.T
    later, same = col > row, col == row
    raw_a = nt(ba[...], ca[...])
    raw_b = nt(bb[...], cb[...])
    affinity = jnp.where(same, raw_a + raw_b, jnp.where(later, raw_a, raw_b))
    weight_sum = jnp.zeros((length, length), F32)
    counts = jnp.concatenate([since.T, upto.T], axis=1).astype(BF16)
    cross = jnp.concatenate([row < col, row > col], axis=1).astype(F32)
    totals = []
    for h in range(heads):
        part = slice(h * width, (h + 1) * width)
        gap = jnp.where(
            later,
            rows_a[h : h + 1] - columns_a[:, h : h + 1],
            rows_b[h : h + 1] - columns_b[:, h : h + 1],
        )
        decay = jnp.exp(jnp.where(same, 0.0, gap))
        score_grad = nt(x[:, part], gy[:, part])
        weighted = score_grad * decay
        weight_sum = weight_sum + weighted
        gx_out[:, part] = nn((decay * affinity).astype(BF16), gy[:, part]) + skip[:, h : h + 1] * gy[:, part].astype(F32)
        pieces = nn((weighted * affinity).astype(BF16), counts)
        totals.append(jnp.sum(pieces * cross, axis=0, keepdims=True))
    for h in range(heads):
        decay_out[h : h + 1] = totals[h]
    ahead = jnp.where(col >= row, weight_sum, 0.0).astype(BF16)
    behind = jnp.where(col <= row, weight_sum, 0.0).astype(BF16)
    maps_out[:, 0:n] = nn(ahead, ca[...])
    maps_out[:, n : 2 * n] = nn(ahead.T, ba[...])
    maps_out[:, 2 * n : 3 * n] = nn(behind, cb[...])
    maps_out[:, 3 * n :] = nn(behind.T, bb[...])
    turned_out[...] = features[...].T


def entering(chunks, seq, peers, n):
    results = []
    for received, before in chunks:
        radix = len(received) + 1
        me = digit(seq, peers // radix, radix)
        members = [me ^ j for j in range(radix)]
        gains = [read_gain(ref[n:]) for ref in received]
        gains = gains[:1] + gains
        coefficients = merge_coefficients(me, members, gains, gains)

        def enter(down, received=received, before=before, coefficients=coefficients):
            total = 0.0
            for coefficient, ref in zip(coefficients[down], received):
                total = total + coefficient * ref[0:n].astype(F32)
            if before is not None:
                total = before[2 * n + down : 2 * n + down + 1] * total + before[down * n : (down + 1) * n]
            return total

        results.append(enter)
    return results


def take_chunks(refs, lasts, first):
    chunks = []
    for radix in lasts:
        received = [refs.pop(0) for _ in range(radix - 1)][::-1]
        chunks.append((received, None if first else refs.pop(0)))
    return chunks


def carry_kernel(index, steps, stride, direct, *refs):
    refs = list(refs)
    chunks = take_chunks(refs, steps[-1:], len(steps) == 1)
    turned, ba, bb, gx_local, factors = refs[:5]
    gx_out, grad_out, *outs = refs[-steps[0] - 1 :] if direct else refs[-3:]
    seq = index()
    me = digit(seq, stride, steps[-1])
    (gradient,) = entering(chunks, seq, stride * steps[-1], ba.shape[1])
    grad_x = gx_local[...]
    for k, (b, left) in enumerate(((ba, factors[1]), (bb, factors[3]))):
        grad = gradient(1 - k).astype(BF16)
        grad_out[k] = grad
        grad_x = grad_x + nn(b[...], grad).astype(BF16).astype(F32) * left
    grad_x = grad_x.astype(BF16)
    gx_out[...] = grad_x
    if not direct:
        outs[0][...] = nn(turned[...], grad_x).astype(BF16)
        return
    rows = outs[0].shape[1]
    for j, out in enumerate(outs, start=1):
        for k in range(4):
            at = (me ^ k) * steps[0] + (digit(seq, 1, steps[0]) ^ j)
            out[k] = nn(turned[pl.ds(pl.multiple_of(at * rows, rows), rows), :], grad_x).astype(BF16)


def fold_kernel(index, steps, turned, grad_x, *refs):
    received, outs = refs[: steps[0] - 1], refs[-4:]
    rows = received[0].shape[1]
    seq = index()
    for k in range(4):
        at = (digit(seq, steps[0], steps[1]) ^ k) * steps[0] + digit(seq, 1, steps[0])
        share = nn(turned[pl.ds(pl.multiple_of(at * rows, rows), rows), :], grad_x[...])
        total = sum([ref[k].astype(F32) for ref in received], share)
        outs[k][...] = total.astype(outs[k].dtype)


def head_groups(heads, columns):
    rows, cols = iotas(8, columns)
    return (lax.div(cols, columns // heads) == rows).astype(BF16)


def share_kernel(index, n_head, grad_x, grads, x, w_in, ba, bb, maps_local, decay_local, factors, *outs):
    decay_out, own_out, send_out = outs
    heads = decay_local.shape[0]
    n = ba.shape[1]
    length, columns = x.shape
    xf = x[...].astype(F32)
    row, col = iotas(length, length)
    group = head_groups(heads, columns)
    rows_out = w_in.shape[0] // n_head
    half = n_head // 2 * rows_out
    for k, (b, earlier) in enumerate(((ba, row < col), (bb, row > col))):
        left, grad = factors[2 * k + 1], grads[k]
        write = nn(b[...], grad).astype(BF16).astype(F32) * left * xf
        writes = nt(group, write.astype(BF16))
        part = slice(k * length, (k + 1) * length)
        decay_out[:, part] = decay_local[:, part] + nn(writes, earlier.astype(F32), precision=HIGH)[:heads]
        grad_b = maps_local[:, 2 * k * n : (2 * k + 1) * n] + nt((xf * left).astype(BF16), grad)
        at = half + k * n
        own_out[:, at : at + n] = grad_b
        send_out[:, at : at + n] = grad_b.astype(BF16)
    for high in range(n_head // 2):
        part = slice(high * rows_out, (high + 1) * rows_out)
        for away in range(2):
            at = pl.multiple_of((high * 2 + (lax.rem(index(), 2) ^ away)) * rows_out, rows_out)
            share = nt(grad_x[...], w_in[pl.ds(at, rows_out), :])
            if away:
                send_out[:, part] = share.astype(BF16)
            else:
                own_out[:, part] = share


def state_share_kernel(index, steps, peers, *refs):
    refs = list(refs)
    chunks = take_chunks(refs, steps[-1:], len(steps) == 1)
    grads, gy, ca, cb, maps_local, decay_part, factors = [refs.pop(0) for _ in range(7)]
    *gd_outs, own_out, send_out = refs
    heads = decay_part.shape[0]
    n = ca.shape[1]
    length, columns = gy.shape
    (state,) = entering(chunks, index(), peers, n)
    gyf = gy[...].astype(F32)
    row, col = iotas(length, length)
    group = head_groups(heads, columns)
    frame = lax.broadcasted_iota(jnp.int32, (length, 1), 0)
    for k, (c, at_end, later) in enumerate(((ca, length - 1, row >= col), (cb, 0, row <= col))):
        grow, entered = factors[2 * k], state(k)
        low = entered.astype(BF16)
        gain = grow[at_end : at_end + 1]
        through = gain * jnp.sum(entered * grads[k].astype(F32), axis=0, keepdims=True)
        read = gyf * (grow * nn(c[...], low)) + jnp.where(frame == at_end, through, 0.0)
        reads = nt(group, read.astype(BF16))
        gd = nn(reads, later.astype(F32), precision=HIGH)[:heads]
        gd_outs[k][...] = gd + decay_part[:, k * length : (k + 1) * length]
        grad_c = maps_local[:, (2 * k + 1) * n : (2 * k + 2) * n] + nt((gyf * grow).astype(BF16), low)
        own_out[:, k * n : (k + 1) * n] = grad_c
        send_out[:, k * n : (k + 1) * n] = grad_c.astype(BF16)


def pair_kernel(index, stride, rows_out, blocks, count, *refs):
    parts, own_out, send_out = refs[:count], refs[-2], refs[-1]
    me = digit(index(), stride, 2)
    own, received = parts[0], parts[1]
    at = blocks * rows_out
    half = at // 2
    maps = []
    for mine, other in zip(parts[0::2], parts[1::2]):
        maps.append(mine[:, at:] + other[:, at:].astype(F32))
        at = 0
    maps = jnp.concatenate(maps, axis=1)
    own_out[:, half:] = maps
    send_out[:, half:] = maps.astype(BF16)
    for high in range(blocks // 2):
        part = slice(high * rows_out, (high + 1) * rows_out)
        for away in range(2):
            at = pl.multiple_of((high * 2 + (me ^ away)) * rows_out, rows_out)
            total = own[:, pl.ds(at, rows_out)] + received[:, pl.ds(at, rows_out)].astype(F32)
            if away:
                send_out[:, part] = total.astype(BF16)
            else:
                own_out[:, part] = total


def last_kernel(scale, own, other, *refs):
    parts, gf_out, gw_out, map_outs = refs[:-6], refs[-6], refs[-5], refs[-4:]
    columns, n = gf_out.shape[1], map_outs[0].shape[1]
    gf_out[...] = (own[:, 0:columns] + other[:, 0:columns].astype(F32)).astype(BF16)
    for k, out in enumerate((map_outs[0], map_outs[2], map_outs[1], map_outs[3])):
        at = columns + k * n
        out[...] = own[:, at : at + n] + other[:, at : at + n].astype(F32)
    total = 0.0
    for part in parts:
        piece = part[...].astype(F32)
        total = total + (jnp.sum(piece, axis=0) if piece.ndim == 3 else piece)
    gw_out[...] = total * scale


def call(kernel, outs, *args, micros=0.0, held=0):
    specs = [pl.BlockSpec(memory_space=pltpu.HBM)] * held
    specs += [pl.BlockSpec(memory_space=pltpu.VMEM)] * (len(args) - held)
    outs = list(outs) + [jax.ShapeDtypeStruct(a.shape, a.dtype) for a in args[:held]]
    if held:
        args = tuple(pltpu.with_memory_space_constraint(a, pltpu.HBM) for a in args[:held]) + args[held:]
    cost = pl.CostEstimate(flops=int(micros * FLOPS_PER_MICRO), bytes_accessed=0, transcendentals=0)
    return pl.pallas_call(
        kernel,
        out_shape=outs,
        in_specs=specs,
        out_specs=[pl.BlockSpec(memory_space=pltpu.VMEM)] * len(outs),
        scratch_shapes=[pltpu.SemaphoreType.DMA((held,))] if held else [],
        cost_estimate=cost,
        compiler_params=pltpu.CompilerParams(vmem_limit_bytes=VMEM_LIMIT),
    )(*args)


def swap(value, axis, mask):
    return lax.ppermute(value, axis, [(i, i ^ mask) for i in range(lax.axis_size(axis))])


def far_first(sends, stride):
    jobs = list(enumerate(sends, start=1))
    return [swap(send, "seq", j * stride) for j, send in reversed(jobs)]


def local(features, w_in, b_ahead, c_ahead, b_behind, c_behind, decay_ahead, decay_behind, skip_gain, grad_y):
    peers, n_head = lax.axis_size("seq"), lax.axis_size("head")
    length, depth = features.shape
    heads, columns = decay_ahead.shape[0], w_in.shape[1]
    n = b_ahead.shape[1]
    seq_index = lambda: lax.axis_index("seq")
    head_index = lambda: lax.axis_index("head")
    shape = jax.ShapeDtypeStruct
    square = shape((length, columns), BF16)
    whole = shape((2 * n + GAIN_ROWS, columns), BF16)
    half = shape((n + GAIN_ROWS, columns), BF16)
    prefix = shape((2 * n + 8, columns), F32)

    steps = radices(peers)
    only = len(steps) == 1
    chunk_shapes = [half] * (steps[0] - 1) if only else [whole]
    *gradients, factors, da, db, gy, ca, cb, skip = call(
        functools.partial(gradient_kernel, seq_index, only, columns // heads),
        chunk_shapes + [shape((4, length, columns), F32)],
        decay_ahead, decay_behind, grad_y, c_ahead, c_behind, skip_gain.reshape(1, heads),
        micros=1.35,
        held=6,
    )
    *states, x, ba, bb, fs, wi = call(
        functools.partial(state_kernel, seq_index, only),
        chunk_shapes + [square],
        b_ahead, b_behind, features, w_in, factors,
        micros=1.65,
        held=4,
    )
    maps = (ba, ca, bb, cb)
    gx_local, maps_local, decay_local, turned = call(
        local_kernel,
        [
            shape((length, columns), F32),
            shape((length, 4 * n), F32),
            shape((heads, 2 * length), F32),
            shape((depth, length), BF16),
        ],
        skip, x, gy, fs, *maps, da, db,
        micros=0.9,
    )
    def merges(chunk):
        stride, before = 1, None
        for at, radix in enumerate(steps[:-1]):
            received = [swap(chunk[0], "seq", j * stride) for j in range(1, radix)]
            next_last = at == len(steps) - 2
            following = steps[at + 1]
            count = (following - 1) if next_last else 1
            before, *chunk = call(
                functools.partial(step_kernel, seq_index, stride, radix, at == 0, next_last, following),
                [prefix] + ([half] if next_last else [whole]) * count,
                chunk[0], *received, *([] if at == 0 else [before]),
                micros=0.15,
            )
            stride *= radix
        return far_first(chunk, stride) + ([] if only else [before])

    stride = peers // steps[-1]
    gradient_in = merges(gradients)
    state_in = merges(states)
    rows_out, rows_w = depth // n_head, depth // peers
    direct = len(steps) == 2 and rows_w % 16 == 0
    pieces = [shape((4, rows_w, columns), BF16)] * (steps[0] - 1) if direct else [shape((depth, columns), BF16)]
    grad_x, grads, *sends = call(
        functools.partial(carry_kernel, seq_index, steps, stride, direct),
        [square, shape((2, n, columns), BF16)] + pieces,
        *gradient_in, turned, ba, bb, gx_local, factors,
        micros=0.5,
    )
    def head_shapes(blocks, maps):
        wide = (length, blocks * rows_out + maps * n)
        return [shape(wide, F32), shape(wide, BF16)]

    decay_part, own, send = call(
        functools.partial(share_kernel, head_index, n_head),
        [shape((heads, 2 * length), F32)] + head_shapes(n_head // 2, 2),
        grad_x, grads, x, wi, ba, bb, maps_local, decay_local, factors,
        micros=1.0,
    )
    shares = [own, swap(send, "head", 1)]
    received = [swap(send, "seq", j) for j, send in enumerate(sends, start=1)] if direct else []
    gd_ahead, gd_behind, own, send = call(
        functools.partial(state_share_kernel, seq_index, steps, peers),
        [shape((heads, length), F32)] * 2 + head_shapes(0, 2),
        *state_in, grads, gy, ca, cb, maps_local, decay_part, factors,
        micros=1.4,
    )
    shares += [own, swap(send, "head", 1)]
    after = []
    if direct:
        own_weight, *sends = call(
            functools.partial(fold_kernel, seq_index, steps),
            [shape((rows_w, columns), F32)] + [shape((rows_w, columns), BF16)] * 3,
            turned, grad_x, *received, own,
            micros=0.22,
        )
        weight_parts = [own_weight] + far_first(sends, stride)
        after = [own_weight]
    else:
        weight_parts = [lax.all_to_all(sends[0].reshape(peers, rows_w, columns), "seq", 0, 0)]
    mask, blocks = 2, n_head // 2
    while mask < n_head:
        own, send = call(
            functools.partial(pair_kernel, head_index, mask, rows_out, blocks, len(shares)),
            head_shapes(blocks // 2, 4),
            *shares, *after,
            micros=0.25,
        )
        shares = [own, swap(send, "head", mask)]
        mask, blocks = mask * 2, blocks // 2
    grad_features, grad_w_in, *grad_maps = call(
        functools.partial(last_kernel, 1.0 / math.sqrt(length * peers)),
        [shape((length, rows_out), BF16), shape((rows_w, columns), F32)] + [shape((length, n), F32)] * 4,
        *shares, *weight_parts,
        micros=0.8,
    )
    return (grad_features, grad_w_in, *grad_maps, gd_ahead, gd_behind)


def solution(mesh):
    in_specs = (
        P("seq", None),
        P(None, "head"),
        P("seq", None),
        P("seq", None),
        P("seq", None),
        P("seq", None),
        P("head", "seq"),
        P("head", "seq"),
        P("head"),
        P("seq", "head"),
    )
    out_specs = (
        P("seq", "head"),
        P("seq", "head"),
        P("seq", None),
        P("seq", None),
        P("seq", None),
        P("seq", None),
        P("head", "seq"),
        P("head", "seq"),
    )
    return jax.shard_map(local, mesh=mesh, in_specs=in_specs, out_specs=out_specs, check_vma=False)
```

```python
import functools
import math

import jax
import jax.numpy as jnp
from jax import lax
from jax.experimental import pallas as pl
from jax.experimental.pallas import tpu as pltpu
from jax.sharding import PartitionSpec as P

F32 = jnp.float32
BF16 = jnp.bfloat16
HIGH = lax.Precision.HIGHEST
GAIN_ROWS = 16
FLOPS_PER_MICRO = 1.15e9
VMEM_LIMIT = 48 * 1024 * 1024


def nn(a, b, **kw):
    return lax.dot_general(a, b, (((1,), (0,)), ((), ())), preferred_element_type=F32, **kw)


def nt(a, b, **kw):
    return lax.dot_general(a, b, (((1,), (1,)), ((), ())), preferred_element_type=F32, **kw)


def iotas(rows, cols):
    return (
        lax.broadcasted_iota(jnp.int32, (rows, cols), 0),
        lax.broadcasted_iota(jnp.int32, (rows, cols), 1),
    )


def spread_rows(values, width):
    heads, length = values.shape
    return jnp.concatenate(
        [jnp.broadcast_to(values[h : h + 1], (width, length)) for h in range(heads)], axis=0
    )


def split3(value):
    high = value.astype(BF16)
    rest = value - high.astype(F32)
    middle = rest.astype(BF16)
    low = (rest - middle.astype(F32)).astype(BF16)
    return high, middle, low


def masked_sums(masks, values):
    masks = masks.astype(BF16)
    return sum(nt(masks, part) for part in split3(values))


def decay_factors(d_ahead, d_behind, width):
    length = d_ahead.shape[1]
    row, col = iotas(length, length)
    upto = (col <= row).astype(F32)
    since = (col >= row).astype(F32)
    ahead = masked_sums(
        jnp.concatenate([upto, 1.0 - upto], axis=0), spread_rows(d_ahead, width)
    )
    behind = masked_sums(
        jnp.concatenate([since, 1.0 - since], axis=0), spread_rows(d_behind, width)
    )
    ahead, behind = jnp.exp(ahead), jnp.exp(behind)
    return ahead[:length], ahead[length:], behind[:length], behind[length:]


def radices(peers):
    bits = peers.bit_length() - 1
    return ([2] if bits % 2 else []) + [4] * (bits // 2)


def digit(index, stride, radix):
    return lax.rem(lax.div(index, stride), radix)


def read_gain(block, k=0):
    rows = block.astype(F32)[3 * k : 3 * k + 3]
    return rows[0:1] + rows[1:2] + rows[2:3]


def gain_block(*gains):
    rows = [p.astype(F32) for gain in gains for p in split3(gain)]
    pad = jnp.zeros((GAIN_ROWS - len(rows), gains[0].shape[1]), F32)
    return jnp.concatenate(rows + [pad], axis=0).astype(BF16)


def product_where(conditions, gains):
    result = jnp.ones_like(gains[0])
    for condition, gain in zip(conditions, gains):
        result = jnp.where(condition, result * gain, result)
    return result


def merge_coefficients(me, members, gains_up, gains_down):
    below, above = [], []
    others = range(1, len(members))
    for j in others:
        q = members[j]
        low = product_where(
            [jnp.logical_and(members[i] > q, members[i] < me) for i in others], [gains_up[i] for i in others]
        )
        high = product_where(
            [jnp.logical_and(members[i] < q, members[i] > me) for i in others], [gains_down[i] for i in others]
        )
        below.append(jnp.where(q < me, low, 0.0))
        above.append(jnp.where(q > me, high, 0.0))
    return below, above


def write_whole(out, up, down, gains):
    n = up.shape[0]
    out[0:n] = up.astype(BF16)
    out[n : 2 * n] = down.astype(BF16)
    if gains:
        out[2 * n :] = gain_block(*gains)


def write_halves(outs, up, down, gains, me):
    n = up.shape[0]
    up, down = up.astype(BF16), down.astype(BF16)
    for j, out in enumerate(outs, start=1):
        out[0:n] = jnp.where((me ^ j) > me, up, down)
        if gains:
            out[n:] = gain_block(*gains)


def write_chunk(outs, me, last, *chunk):
    if last:
        write_halves(outs, *chunk, me())
    else:
        write_whole(outs[0], *chunk)


def start_copies(sources, targets, sems):
    copies = [pltpu.make_async_copy(s, t, sems.at[k]) for k, (s, t) in enumerate(zip(sources, targets))]
    for copy in copies:
        copy.start()
    return copies


def gradient_kernel(me, last, width, *refs):
    *refs, sems = refs
    sources, outs, held = refs[:6], refs[6:-6], refs[-6:]
    copies = start_copies(sources, held, sems)
    da, db, gy, ca, cb, _ = held
    for copy in copies[:2]:
        copy.wait()
    factors = decay_factors(da[...], db[...], width)
    *sends, factors_out = outs
    for k in range(4):
        factors_out[k] = factors[k]
    grow_a, _, grow_b, _ = factors
    for copy in copies[2:]:
        copy.wait()
    gyf = gy[...].astype(F32)
    up = nn(cb[...].T, (gyf * grow_b).astype(BF16))
    down = nn(ca[...].T, (gyf * grow_a).astype(BF16))
    write_chunk(sends, me, last, up, down, (grow_a[gyf.shape[0] - 1 :], grow_b[0:1]))


def state_kernel(me, last, *refs):
    *refs, sems = refs
    sources, factors, outs, held = refs[:4], refs[4], refs[5:-4], refs[-4:]
    copies = start_copies(sources, held, sems)
    ba, bb, features, w_in = held
    for copy in copies:
        copy.wait()
    *sends, x_out = outs
    x = nn(features[...], w_in[...]).astype(BF16)
    x_out[...] = x
    xf = x.astype(F32)
    up = nn(ba[...].T, (xf * factors[1]).astype(BF16))
    down = nn(bb[...].T, (xf * factors[3]).astype(BF16))
    write_chunk(sends, me, last, up, down, ())


def step_kernel(index, stride, radix, first, next_last, next_radix, states, *refs):
    refs = list(refs)
    members_in = [refs.pop(0) for _ in range(radix)]
    gains_in = [refs.pop(0) for _ in range(radix)] if states else members_in
    before, outs = refs[0], refs[-(next_radix if next_last else 2) :]
    pre_out, *outs = outs
    n = (gains_in[0].shape[0] - GAIN_ROWS) // 2
    seq = index()
    me = digit(seq, stride, radix)
    members = [me ^ j for j in range(radix)]
    loaded = [(ref[0:n].astype(F32), ref[n : 2 * n].astype(F32)) for ref in members_in]
    both = [[read_gain(ref[2 * n :], k) for ref in gains_in] for k in range(2)]
    gains = both if states else both[::-1]
    coefficients = merge_coefficients(me, members, *gains)
    width = members_in[0].shape[1]
    new_grow = []
    totals = []
    for down in range(2):
        total = sum(coefficients[down][j - 1] * loaded[j][down] for j in range(1, radix))
        inside = [(members[j] > me) if down else (members[j] < me) for j in range(1, radix)]
        grow = product_where(inside, gains[down][1:])
        if not first:
            kept = before[2 * n + down : 2 * n + down + 1]
            total = kept * total + before[down * n : (down + 1) * n]
            grow = kept * grow
        pre_out[down * n : (down + 1) * n] = total
        new_grow.append(grow)
        group = 0.0
        for j in range(radix):
            rest = [i for i in range(radix) if i != j]
            outer = [(members[i] < members[j]) if down else (members[i] > members[j]) for i in rest]
            group = group + product_where(outer, [gains[down][i] for i in rest]) * loaded[j][down]
        totals.append(group)
    pre_out[2 * n :] = jnp.concatenate(new_grow + [jnp.zeros((6, width), F32)], axis=0)
    new = () if states else [functools.reduce(lambda a, b: a * b, both[k]) for k in range(2)]
    write_chunk(outs, lambda: digit(seq, stride * radix, next_radix), next_last, *totals, new)


def local_kernel(
    skip, x, gy, features, ba, ca, bb, cb, da, db, gx_out, maps_out, decay_out, turned_out
):
    heads, length = da.shape
    width = x.shape[1] // heads
    n = ba.shape[1]
    row, col = iotas(length, length)
    upto = (col <= row).astype(F32)
    since = (col >= row).astype(F32)
    pad = jnp.zeros((8 - heads, length), F32)
    d_ahead = jnp.concatenate([da[...], pad], axis=0)
    d_behind = jnp.concatenate([db[...], pad], axis=0)
    columns_a = masked_sums(upto, d_ahead)
    columns_b = masked_sums(since, d_behind)
    rows_a = columns_a.T
    rows_b = columns_b.T
    later, same = col > row, col == row
    raw_a = nt(ba[...], ca[...])
    raw_b = nt(bb[...], cb[...])
    affinity = jnp.where(same, raw_a + raw_b, jnp.where(later, raw_a, raw_b))
    weight_sum = jnp.zeros((length, length), F32)
    counts = jnp.concatenate([since.T, upto.T], axis=1).astype(BF16)
    cross = jnp.concatenate([row < col, row > col], axis=1).astype(F32)
    totals = []
    for h in range(heads):
        part = slice(h * width, (h + 1) * width)
        gap = jnp.where(
            later,
            rows_a[h : h + 1] - columns_a[:, h : h + 1],
            rows_b[h : h + 1] - columns_b[:, h : h + 1],
        )
        decay = jnp.exp(jnp.where(same, 0.0, gap))
        score_grad = nt(x[:, part], gy[:, part])
        weighted = score_grad * decay
        weight_sum = weight_sum + weighted
        gx_out[:, part] = nn((decay * affinity).astype(BF16), gy[:, part]) + skip[:, h : h + 1] * gy[:, part].astype(F32)
        pieces = nn((weighted * affinity).astype(BF16), counts)
        totals.append(jnp.sum(pieces * cross, axis=0, keepdims=True))
    for h in range(heads):
        decay_out[h : h + 1] = totals[h]
    ahead = jnp.where(col >= row, weight_sum, 0.0).astype(BF16)
    behind = jnp.where(col <= row, weight_sum, 0.0).astype(BF16)
    maps_out[:, 0:n] = nn(ahead, ca[...])
    maps_out[:, n : 2 * n] = nn(ahead.T, ba[...])
    maps_out[:, 2 * n : 3 * n] = nn(behind, cb[...])
    maps_out[:, 3 * n :] = nn(behind.T, bb[...])
    turned_out[...] = features[...].T


def entering(received, decays, before, seq, peers, n, states):
    radix = len(received) + 1
    me = digit(seq, peers // radix, radix)
    members = [me ^ j for j in range(radix)]
    ahead, behind = [[read_gain(ref[n:], k) for ref in decays[:1] + decays] for k in range(2)]
    gains = (ahead, behind) if states else (behind, ahead)
    coefficients = merge_coefficients(me, members, *gains)

    def enter(down):
        total = 0.0
        for coefficient, ref in zip(coefficients[down], received):
            total = total + coefficient * ref[0:n].astype(F32)
        if before is not None:
            total = before[2 * n + down : 2 * n + down + 1] * total + before[down * n : (down + 1) * n]
        return total

    return enter


def take_chunk(refs, radix, first):
    received = [refs.pop(0) for _ in range(radix - 1)][::-1]
    return received, None if first else refs.pop(0)


def carry_kernel(index, steps, stride, direct, *refs):
    refs = list(refs)
    received, before = take_chunk(refs, steps[-1], len(steps) == 1)
    turned, ba, bb, gx_local, factors = [refs.pop(0) for _ in range(5)]
    gx_out, grad_out, *outs = refs
    seq = index()
    me = digit(seq, stride, steps[-1])
    gradient = entering(received, received, before, seq, stride * steps[-1], ba.shape[1], False)
    grad_x = gx_local[...]
    for k, (b, left) in enumerate(((ba, factors[1]), (bb, factors[3]))):
        grad = gradient(1 - k).astype(BF16)
        grad_out[k] = grad
        grad_x = grad_x + nn(b[...], grad).astype(BF16).astype(F32) * left
    grad_x = grad_x.astype(BF16)
    gx_out[...] = grad_x
    if not direct:
        outs[0][...] = nn(turned[...], grad_x).astype(BF16)
        return
    rows = outs[0].shape[1]
    for j, out in enumerate(outs, start=1):
        for k in range(4):
            at = (me ^ k) * steps[0] + (digit(seq, 1, steps[0]) ^ j)
            out[k] = nn(turned[pl.ds(pl.multiple_of(at * rows, rows), rows), :], grad_x).astype(BF16)


def fold_kernel(index, steps, turned, grad_x, *refs):
    received, outs = refs[: steps[0] - 1], refs[-4:]
    rows = received[0].shape[1]
    seq = index()
    for k in range(4):
        at = (digit(seq, steps[0], steps[1]) ^ k) * steps[0] + digit(seq, 1, steps[0])
        share = nn(turned[pl.ds(pl.multiple_of(at * rows, rows), rows), :], grad_x[...])
        total = sum([ref[k].astype(F32) for ref in received], share)
        outs[k][...] = total.astype(outs[k].dtype)


def head_groups(heads, columns):
    rows, cols = iotas(8, columns)
    return (lax.div(cols, columns // heads) == rows).astype(BF16)


def share_kernel(index, n_head, grad_x, grads, x, w_in, ba, bb, maps_local, decay_local, factors, *outs):
    decay_out, maps_out, own_out, send_out = outs
    heads = decay_local.shape[0]
    n = ba.shape[1]
    length, columns = x.shape
    xf = x[...].astype(F32)
    row, col = iotas(length, length)
    group = head_groups(heads, columns)
    rows_out = w_in.shape[0] // n_head
    for k, (b, earlier) in enumerate(((ba, row < col), (bb, row > col))):
        left, grad = factors[2 * k + 1], grads[k]
        write = nn(b[...], grad).astype(BF16).astype(F32) * left * xf
        writes = nt(group, write.astype(BF16))
        part = slice(k * length, (k + 1) * length)
        decay_out[:, part] = decay_local[:, part] + nn(writes, earlier.astype(F32), precision=HIGH)[:heads]
        grad_b = maps_local[:, 2 * k * n : (2 * k + 1) * n] + nt((xf * left).astype(BF16), grad)
        maps_out[:, k * n : (k + 1) * n] = grad_b
    for high in range(n_head // 2):
        part = slice(high * rows_out, (high + 1) * rows_out)
        for away in range(2):
            at = pl.multiple_of((high * 2 + (lax.rem(index(), 2) ^ away)) * rows_out, rows_out)
            share = nt(grad_x[...], w_in[pl.ds(at, rows_out), :])
            if away:
                send_out[:, part] = share.astype(BF16)
            else:
                own_out[:, part] = share


def state_share_kernel(index, steps, peers, *refs):
    refs = list(refs)
    received, before = take_chunk(refs, steps[-1], len(steps) == 1)
    decays, _ = take_chunk(refs, steps[-1], True)
    grads, gy, ca, cb, maps_local, maps_b, decay_part, factors = [refs.pop(0) for _ in range(8)]
    *gd_outs, own_out, send_out = refs
    heads = decay_part.shape[0]
    n = ca.shape[1]
    length, columns = gy.shape
    state = entering(received, decays, before, index(), peers, n, True)
    gyf = gy[...].astype(F32)
    row, col = iotas(length, length)
    group = head_groups(heads, columns)
    frame = lax.broadcasted_iota(jnp.int32, (length, 1), 0)
    for k, (c, at_end, later) in enumerate(((ca, length - 1, row >= col), (cb, 0, row <= col))):
        grow, entered = factors[2 * k], state(k)
        low = entered.astype(BF16)
        gain = grow[at_end : at_end + 1]
        through = gain * jnp.sum(entered * grads[k].astype(F32), axis=0, keepdims=True)
        read = gyf * (grow * nn(c[...], low)) + jnp.where(frame == at_end, through, 0.0)
        reads = nt(group, read.astype(BF16))
        gd = nn(reads, later.astype(F32), precision=HIGH)[:heads]
        gd_outs[k][...] = gd + decay_part[:, k * length : (k + 1) * length]
        grad_c = maps_local[:, (2 * k + 1) * n : (2 * k + 2) * n] + nt((gyf * grow).astype(BF16), low)
        for at, value in ((2 * k, maps_b[:, k * n : (k + 1) * n]), (2 * k + 1, grad_c)):
            own_out[:, at * n : (at + 1) * n] = value
            send_out[:, at * n : (at + 1) * n] = value.astype(BF16)


def pair_kernel(index, stride, rows_out, blocks, count, *refs):
    parts, own_out, send_out = refs[:count], refs[-2], refs[-1]
    me = digit(index(), stride, 2)
    own, received = parts[0], parts[1]
    at = blocks * rows_out
    half = at // 2
    if count == 4:
        maps = parts[2][...] + parts[3][...].astype(F32)
    else:
        maps = own[:, at:] + received[:, at:].astype(F32)
    own_out[:, half:] = maps
    send_out[:, half:] = maps.astype(BF16)
    for high in range(blocks // 2):
        part = slice(high * rows_out, (high + 1) * rows_out)
        for away in range(2):
            at = pl.multiple_of((high * 2 + (me ^ away)) * rows_out, rows_out)
            total = own[:, pl.ds(at, rows_out)] + received[:, pl.ds(at, rows_out)].astype(F32)
            if away:
                send_out[:, part] = total.astype(BF16)
            else:
                own_out[:, part] = total


def last_kernel(scale, own, other, *refs):
    parts, gf_out, gw_out, map_outs = refs[:-6], refs[-6], refs[-5], refs[-4:]
    columns, n = gf_out.shape[1], map_outs[0].shape[1]
    gf_out[...] = (own[:, 0:columns] + other[:, 0:columns].astype(F32)).astype(BF16)
    for k, out in enumerate(map_outs):
        at = columns + k * n
        out[...] = own[:, at : at + n] + other[:, at : at + n].astype(F32)
    total = 0.0
    for part in parts:
        piece = part[...].astype(F32)
        total = total + (jnp.sum(piece, axis=0) if piece.ndim == 3 else piece)
    gw_out[...] = total * scale


def call(kernel, outs, *args, micros=0.0, held=0):
    specs = [pl.BlockSpec(memory_space=pltpu.HBM)] * held
    specs += [pl.BlockSpec(memory_space=pltpu.VMEM)] * (len(args) - held)
    outs = list(outs) + [jax.ShapeDtypeStruct(a.shape, a.dtype) for a in args[:held]]
    if held:
        args = tuple(pltpu.with_memory_space_constraint(a, pltpu.HBM) for a in args[:held]) + args[held:]
    cost = pl.CostEstimate(flops=int(micros * FLOPS_PER_MICRO), bytes_accessed=0, transcendentals=0)
    return pl.pallas_call(
        kernel,
        out_shape=outs,
        in_specs=specs,
        out_specs=[pl.BlockSpec(memory_space=pltpu.VMEM)] * len(outs),
        scratch_shapes=[pltpu.SemaphoreType.DMA((held,))] if held else [],
        cost_estimate=cost,
        compiler_params=pltpu.CompilerParams(vmem_limit_bytes=VMEM_LIMIT),
    )(*args)


def swap(value, axis, mask):
    return lax.ppermute(value, axis, [(i, i ^ mask) for i in range(lax.axis_size(axis))])


def far_first(sends, stride):
    jobs = list(enumerate(sends, start=1))
    return [swap(send, "seq", j * stride) for j, send in reversed(jobs)]


def local(features, w_in, b_ahead, c_ahead, b_behind, c_behind, decay_ahead, decay_behind, skip_gain, grad_y):
    peers, n_head = lax.axis_size("seq"), lax.axis_size("head")
    length, depth = features.shape
    heads, columns = decay_ahead.shape[0], w_in.shape[1]
    n = b_ahead.shape[1]
    seq_index = lambda: lax.axis_index("seq")
    head_index = lambda: lax.axis_index("head")
    shape = jax.ShapeDtypeStruct
    square = shape((length, columns), BF16)
    whole = shape((2 * n + GAIN_ROWS, columns), BF16)
    half = shape((n + GAIN_ROWS, columns), BF16)
    state_whole, state_half = shape((2 * n, columns), BF16), shape((n, columns), BF16)
    prefix = shape((2 * n + 8, columns), F32)

    steps = radices(peers)
    only = len(steps) == 1
    chunk_shapes = [half] * (steps[0] - 1) if only else [whole]
    *gradients, factors, da, db, gy, ca, cb, skip = call(
        functools.partial(gradient_kernel, seq_index, only, columns // heads),
        chunk_shapes + [shape((4, length, columns), F32)],
        decay_ahead, decay_behind, grad_y, c_ahead, c_behind, skip_gain.reshape(1, heads),
        micros=1.35,
        held=6,
    )
    *states, x, ba, bb, fs, wi = call(
        functools.partial(state_kernel, seq_index, only),
        ([state_half] * (steps[0] - 1) if only else [state_whole]) + [square],
        b_ahead, b_behind, features, w_in, factors,
        micros=1.65,
        held=4,
    )
    maps = (ba, ca, bb, cb)
    gx_local, maps_local, decay_local, turned = call(
        local_kernel,
        [
            shape((length, columns), F32),
            shape((length, 4 * n), F32),
            shape((heads, 2 * length), F32),
            shape((depth, length), BF16),
        ],
        skip, x, gy, fs, *maps, da, db,
        micros=0.9,
    )
    def merges(chunk, decays):
        stride, before, seen = 1, None, []
        whole_shape, half_shape = (state_whole, state_half) if decays else (whole, half)
        for at, radix in enumerate(steps[:-1]):
            members = [chunk[0]] + [swap(chunk[0], "seq", j * stride) for j in range(1, radix)]
            seen.append(members)
            next_last = at == len(steps) - 2
            following = steps[at + 1]
            before, *chunk = call(
                functools.partial(
                    step_kernel, seq_index, stride, radix, at == 0, next_last, following, bool(decays)
                ),
                [prefix] + ([half_shape] * (following - 1) if next_last else [whole_shape]),
                *members, *(decays[at] if decays else []), *([] if at == 0 else [before]),
                micros=0.15,
            )
            stride *= radix
        return far_first(chunk, stride), [] if only else [before], seen

    stride = peers // steps[-1]
    gradients, gradient_before, seen = merges(gradients, None)
    states, state_before, _ = merges(states, seen) if not only else (far_first(states, stride), [], [])
    gradient_in, state_in = gradients + gradient_before, states + state_before + gradients
    rows_out, rows_w = depth // n_head, depth // peers
    direct = len(steps) == 2 and rows_w % 16 == 0
    pieces = [shape((4, rows_w, columns), BF16)] * (steps[0] - 1) if direct else [shape((depth, columns), BF16)]
    grad_x, grads, *sends = call(
        functools.partial(carry_kernel, seq_index, steps, stride, direct),
        [square, shape((2, n, columns), BF16)] + pieces,
        *gradient_in, turned, ba, bb, gx_local, factors,
        micros=0.5,
    )
    def both(width):
        return [shape((length, width), F32), shape((length, width), BF16)]

    decay_part, maps_b, own, send = call(
        functools.partial(share_kernel, head_index, n_head),
        [shape((heads, 2 * length), F32), shape((length, 2 * n), F32)] + both(n_head // 2 * rows_out),
        grad_x, grads, x, wi, ba, bb, maps_local, decay_local, factors,
        micros=1.0,
    )
    shares = [own, swap(send, "head", 1)]
    gd_ahead, gd_behind, own, send = call(
        functools.partial(state_share_kernel, seq_index, steps, peers),
        [shape((heads, length), F32)] * 2 + both(4 * n),
        *state_in, grads, gy, ca, cb, maps_local, maps_b, decay_part, factors,
        micros=1.4,
    )
    shares += [own, swap(send, "head", 1)]
    after = []
    if direct:
        received = [swap(send, "seq", j) for j, send in enumerate(sends, start=1)]
        own_weight, *sends = call(
            functools.partial(fold_kernel, seq_index, steps),
            [shape((rows_w, columns), F32)] + [shape((rows_w, columns), BF16)] * 3,
            turned, grad_x, *received, own,
            micros=0.22,
        )
        weight_parts = far_first(sends, stride) + [own_weight]
        after = [own_weight]
    else:
        weight_parts = [lax.all_to_all(sends[0].reshape(peers, rows_w, columns), "seq", 0, 0)]
    mask, blocks = 2, n_head // 2
    while mask < n_head:
        own, send = call(
            functools.partial(pair_kernel, head_index, mask, rows_out, blocks, len(shares)),
            both(blocks // 2 * rows_out + 4 * n),
            *shares, *after,
            micros=0.25,
        )
        shares = [own, swap(send, "head", mask)]
        mask, blocks = mask * 2, blocks // 2
    grad_features, grad_w_in, *grad_maps = call(
        functools.partial(last_kernel, 1.0 / math.sqrt(length * peers)),
        [shape((length, rows_out), BF16), shape((rows_w, columns), F32)] + [shape((length, n), F32)] * 4,
        *shares, *weight_parts,
        micros=0.8,
    )
    return (grad_features, grad_w_in, *grad_maps, gd_ahead, gd_behind)


def solution(mesh):
    in_specs = (
        P("seq", None),
        P(None, "head"),
        P("seq", None),
        P("seq", None),
        P("seq", None),
        P("seq", None),
        P("head", "seq"),
        P("head", "seq"),
        P("head"),
        P("seq", "head"),
    )
    out_specs = (
        P("seq", "head"),
        P("seq", "head"),
        P("seq", None),
        P("seq", None),
        P("seq", None),
        P("seq", None),
        P("head", "seq"),
        P("head", "seq"),
    )
    return jax.shard_map(local, mesh=mesh, in_specs=in_specs, out_specs=out_specs, check_vma=False)
```

```python
import functools
import math

import jax
import jax.numpy as jnp
from jax import lax
from jax.experimental import pallas as pl
from jax.experimental.pallas import tpu as pltpu
from jax.sharding import PartitionSpec as P

F32 = jnp.float32
BF16 = jnp.bfloat16
HIGH = lax.Precision.HIGHEST
GAIN_ROWS = 16
FLOPS_PER_MICRO = 1.15e9
VMEM_LIMIT = 48 * 1024 * 1024


def nn(a, b, **kw):
    return lax.dot_general(a, b, (((1,), (0,)), ((), ())), preferred_element_type=F32, **kw)


def nt(a, b, **kw):
    return lax.dot_general(a, b, (((1,), (1,)), ((), ())), preferred_element_type=F32, **kw)


def iotas(rows, cols):
    return (
        lax.broadcasted_iota(jnp.int32, (rows, cols), 0),
        lax.broadcasted_iota(jnp.int32, (rows, cols), 1),
    )


def spread_rows(values, width):
    heads, length = values.shape
    return jnp.concatenate(
        [jnp.broadcast_to(values[h : h + 1], (width, length)) for h in range(heads)], axis=0
    )


def split3(value):
    high = value.astype(BF16)
    rest = value - high.astype(F32)
    middle = rest.astype(BF16)
    low = (rest - middle.astype(F32)).astype(BF16)
    return high, middle, low


def masked_sums(masks, values):
    masks = masks.astype(BF16)
    return sum(nt(masks, part) for part in split3(values))


def decay_factors(d_ahead, d_behind, width, rest):
    length = d_ahead.shape[1]
    row, col = iotas(length, length)
    masks = (col > row, col < row) if rest else (col <= row, col >= row)
    return [
        jnp.exp(masked_sums(mask.astype(F32), spread_rows(d, width))) for mask, d in zip(masks, (d_ahead, d_behind))
    ]


def radices(peers):
    bits = peers.bit_length() - 1
    return ([2] if bits % 2 else []) + [4] * (bits // 2)


def digit(index, stride, radix):
    return lax.rem(lax.div(index, stride), radix)


def read_gain(block, k=0):
    rows = block.astype(F32)[3 * k : 3 * k + 3]
    return rows[0:1] + rows[1:2] + rows[2:3]


def gain_block(*gains):
    rows = [p.astype(F32) for gain in gains for p in split3(gain)]
    pad = jnp.zeros((GAIN_ROWS - len(rows), gains[0].shape[1]), F32)
    return jnp.concatenate(rows + [pad], axis=0).astype(BF16)


def product_where(conditions, gains):
    result = jnp.ones_like(gains[0])
    for condition, gain in zip(conditions, gains):
        result = jnp.where(condition, result * gain, result)
    return result


def merge_coefficients(me, members, gains_up, gains_down):
    below, above = [], []
    others = range(1, len(members))
    for j in others:
        q = members[j]
        low = product_where(
            [jnp.logical_and(members[i] > q, members[i] < me) for i in others], [gains_up[i] for i in others]
        )
        high = product_where(
            [jnp.logical_and(members[i] < q, members[i] > me) for i in others], [gains_down[i] for i in others]
        )
        below.append(jnp.where(q < me, low, 0.0))
        above.append(jnp.where(q > me, high, 0.0))
    return below, above


def write_whole(out, up, down, gains):
    n = up.shape[0]
    out[0:n] = up.astype(BF16)
    out[n : 2 * n] = down.astype(BF16)
    if gains:
        out[2 * n :] = gain_block(*gains)


def write_halves(outs, up, down, gains, me):
    n = up.shape[0]
    up, down = up.astype(BF16), down.astype(BF16)
    for j, out in enumerate(outs, start=1):
        out[0:n] = jnp.where((me ^ j) > me, up, down)
        if gains:
            out[n:] = gain_block(*gains)


def write_chunk(outs, me, last, *chunk):
    if last:
        write_halves(outs, *chunk, me())
    else:
        write_whole(outs[0], *chunk)


def start_copies(sources, targets, sems):
    copies = [pltpu.make_async_copy(s, t, sems.at[k]) for k, (s, t) in enumerate(zip(sources, targets))]
    for copy in copies:
        copy.start()
    return copies


def gradient_kernel(me, last, width, *refs):
    *refs, sems = refs
    sources, outs, held = refs[:6], refs[6:-6], refs[-6:]
    copies = start_copies(sources, held, sems)
    da, db, gy, ca, cb, _ = held
    for copy in copies[:2]:
        copy.wait()
    grow_a, grow_b = decay_factors(da[...], db[...], width, False)
    *sends, grow_out = outs
    grow_out[0] = grow_a
    grow_out[1] = grow_b
    for copy in copies[2:]:
        copy.wait()
    gyf = gy[...].astype(F32)
    up = nn(cb[...].T, (gyf * grow_b).astype(BF16))
    down = nn(ca[...].T, (gyf * grow_a).astype(BF16))
    write_chunk(sends, me, last, up, down, (grow_a[gyf.shape[0] - 1 :], grow_b[0:1]))


def state_kernel(me, last, width, *refs):
    *refs, sems = refs
    sources, da, db, outs, held = refs[:4], refs[4], refs[5], refs[6:-4], refs[-4:]
    copies = start_copies(sources, held, sems)
    ba, bb, features, w_in = held
    *sends, x_out, left_out = outs
    left_a, left_b = decay_factors(da[...], db[...], width, True)
    left_out[0] = left_a
    left_out[1] = left_b
    for copy in copies:
        copy.wait()
    x = nn(features[...], w_in[...]).astype(BF16)
    x_out[...] = x
    xf = x.astype(F32)
    up = nn(ba[...].T, (xf * left_a).astype(BF16))
    down = nn(bb[...].T, (xf * left_b).astype(BF16))
    write_chunk(sends, me, last, up, down, ())


def step_kernel(index, stride, radix, first, next_last, next_radix, states, *refs):
    refs = list(refs)
    members_in = [refs.pop(0) for _ in range(radix)]
    gains_in = [refs.pop(0) for _ in range(radix)] if states else members_in
    before, outs = refs[0], refs[-(next_radix if next_last else 2) :]
    pre_out, *outs = outs
    n = (gains_in[0].shape[0] - GAIN_ROWS) // 2
    seq = index()
    me = digit(seq, stride, radix)
    members = [me ^ j for j in range(radix)]
    loaded = [(ref[0:n].astype(F32), ref[n : 2 * n].astype(F32)) for ref in members_in]
    both = [[read_gain(ref[2 * n :], k) for ref in gains_in] for k in range(2)]
    gains = both if states else both[::-1]
    coefficients = merge_coefficients(me, members, *gains)
    width = members_in[0].shape[1]
    new_grow = []
    totals = []
    for down in range(2):
        total = sum(coefficients[down][j - 1] * loaded[j][down] for j in range(1, radix))
        inside = [(members[j] > me) if down else (members[j] < me) for j in range(1, radix)]
        grow = product_where(inside, gains[down][1:])
        if not first:
            kept = before[2 * n + down : 2 * n + down + 1]
            total = kept * total + before[down * n : (down + 1) * n]
            grow = kept * grow
        pre_out[down * n : (down + 1) * n] = total
        new_grow.append(grow)
        group = 0.0
        for j in range(radix):
            rest = [i for i in range(radix) if i != j]
            outer = [(members[i] < members[j]) if down else (members[i] > members[j]) for i in rest]
            group = group + product_where(outer, [gains[down][i] for i in rest]) * loaded[j][down]
        totals.append(group)
    pre_out[2 * n :] = jnp.concatenate(new_grow + [jnp.zeros((6, width), F32)], axis=0)
    new = () if states else [functools.reduce(lambda a, b: a * b, both[k]) for k in range(2)]
    write_chunk(outs, lambda: digit(seq, stride * radix, next_radix), next_last, *totals, new)


def local_kernel(
    skip, x, gy, features, ba, ca, bb, cb, da, db, gx_out, maps_out, decay_out, turned_out
):
    heads, length = da.shape
    width = x.shape[1] // heads
    n = ba.shape[1]
    row, col = iotas(length, length)
    upto = (col <= row).astype(F32)
    since = (col >= row).astype(F32)
    pad = jnp.zeros((8 - heads, length), F32)
    d_ahead = jnp.concatenate([da[...], pad], axis=0)
    d_behind = jnp.concatenate([db[...], pad], axis=0)
    columns_a = masked_sums(upto, d_ahead)
    columns_b = masked_sums(since, d_behind)
    rows_a = columns_a.T
    rows_b = columns_b.T
    later, same = col > row, col == row
    raw_a = nt(ba[...], ca[...])
    raw_b = nt(bb[...], cb[...])
    affinity = jnp.where(same, raw_a + raw_b, jnp.where(later, raw_a, raw_b))
    weight_sum = jnp.zeros((length, length), F32)
    counts = jnp.concatenate([since.T, upto.T], axis=1).astype(BF16)
    cross = jnp.concatenate([row < col, row > col], axis=1).astype(F32)
    totals = []
    for h in range(heads):
        part = slice(h * width, (h + 1) * width)
        gap = jnp.where(
            later,
            rows_a[h : h + 1] - columns_a[:, h : h + 1],
            rows_b[h : h + 1] - columns_b[:, h : h + 1],
        )
        decay = jnp.exp(jnp.where(same, 0.0, gap))
        score_grad = nt(x[:, part], gy[:, part])
        weighted = score_grad * decay
        weight_sum = weight_sum + weighted
        gx_out[:, part] = nn((decay * affinity).astype(BF16), gy[:, part]) + skip[:, h : h + 1] * gy[:, part].astype(F32)
        pieces = nn((weighted * affinity).astype(BF16), counts)
        totals.append(jnp.sum(pieces * cross, axis=0, keepdims=True))
    for h in range(heads):
        decay_out[h : h + 1] = totals[h]
    ahead = jnp.where(col >= row, weight_sum, 0.0).astype(BF16)
    behind = jnp.where(col <= row, weight_sum, 0.0).astype(BF16)
    maps_out[:, 0:n] = nn(ahead, ca[...])
    maps_out[:, n : 2 * n] = nn(ahead.T, ba[...])
    maps_out[:, 2 * n : 3 * n] = nn(behind, cb[...])
    maps_out[:, 3 * n :] = nn(behind.T, bb[...])
    turned_out[...] = features[...].T


def entering(received, decays, before, seq, peers, n, states):
    radix = len(received) + 1
    me = digit(seq, peers // radix, radix)
    members = [me ^ j for j in range(radix)]
    ahead, behind = [[read_gain(ref[n:], k) for ref in decays[:1] + decays] for k in range(2)]
    gains = (ahead, behind) if states else (behind, ahead)
    coefficients = merge_coefficients(me, members, *gains)

    def enter(down):
        total = 0.0
        for coefficient, ref in zip(coefficients[down], received):
            total = total + coefficient * ref[0:n].astype(F32)
        if before is not None:
            total = before[2 * n + down : 2 * n + down + 1] * total + before[down * n : (down + 1) * n]
        return total

    return enter


def take_chunk(refs, radix, first):
    received = [refs.pop(0) for _ in range(radix - 1)][::-1]
    return received, None if first else refs.pop(0)


def carry_kernel(index, steps, stride, direct, *refs):
    refs = list(refs)
    received, before = take_chunk(refs, steps[-1], len(steps) == 1)
    turned, ba, bb, gx_local, left = [refs.pop(0) for _ in range(5)]
    gx_out, grad_out, *outs = refs
    seq = index()
    me = digit(seq, stride, steps[-1])
    gradient = entering(received, received, before, seq, stride * steps[-1], ba.shape[1], False)
    grad_x = gx_local[...]
    for k, b in enumerate((ba, bb)):
        grad = gradient(1 - k).astype(BF16)
        grad_out[k] = grad
        grad_x = grad_x + nn(b[...], grad).astype(BF16).astype(F32) * left[k]
    grad_x = grad_x.astype(BF16)
    gx_out[...] = grad_x
    if not direct:
        outs[0][...] = nn(turned[...], grad_x).astype(BF16)
        return
    rows = outs[0].shape[1]
    for j, out in enumerate(outs, start=1):
        for k in range(4):
            at = (me ^ k) * steps[0] + (digit(seq, 1, steps[0]) ^ j)
            out[k] = nn(turned[pl.ds(pl.multiple_of(at * rows, rows), rows), :], grad_x).astype(BF16)


def fold_kernel(index, steps, turned, grad_x, *refs):
    received, outs = refs[: steps[0] - 1], refs[-4:]
    rows = received[0].shape[1]
    seq = index()
    for k in range(4):
        at = (digit(seq, steps[0], steps[1]) ^ k) * steps[0] + digit(seq, 1, steps[0])
        share = nn(turned[pl.ds(pl.multiple_of(at * rows, rows), rows), :], grad_x[...])
        total = sum([ref[k].astype(F32) for ref in received], share)
        outs[k][...] = total.astype(outs[k].dtype)


def head_groups(heads, columns):
    rows, cols = iotas(8, columns)
    return (lax.div(cols, columns // heads) == rows).astype(BF16)


def share_kernel(index, n_head, grad_x, grads, x, w_in, ba, bb, maps_local, decay_local, lefts, *outs):
    decay_out, maps_out, own_out, send_out = outs
    heads = decay_local.shape[0]
    n = ba.shape[1]
    length, columns = x.shape
    xf = x[...].astype(F32)
    row, col = iotas(length, length)
    group = head_groups(heads, columns)
    rows_out = w_in.shape[0] // n_head
    for k, (b, earlier) in enumerate(((ba, row < col), (bb, row > col))):
        left, grad = lefts[k], grads[k]
        write = nn(b[...], grad).astype(BF16).astype(F32) * left * xf
        writes = nt(group, write.astype(BF16))
        part = slice(k * length, (k + 1) * length)
        decay_out[:, part] = decay_local[:, part] + nn(writes, earlier.astype(F32), precision=HIGH)[:heads]
        grad_b = maps_local[:, 2 * k * n : (2 * k + 1) * n] + nt((xf * left).astype(BF16), grad)
        maps_out[:, k * n : (k + 1) * n] = grad_b
    for high in range(n_head // 2):
        part = slice(high * rows_out, (high + 1) * rows_out)
        for away in range(2):
            at = pl.multiple_of((high * 2 + (lax.rem(index(), 2) ^ away)) * rows_out, rows_out)
            share = nt(grad_x[...], w_in[pl.ds(at, rows_out), :])
            if away:
                send_out[:, part] = share.astype(BF16)
            else:
                own_out[:, part] = share


def state_share_kernel(index, steps, peers, *refs):
    refs = list(refs)
    received, before = take_chunk(refs, steps[-1], len(steps) == 1)
    decays, _ = take_chunk(refs, steps[-1], True)
    gy, maps_local, maps_b, grows = [refs.pop(0) for _ in range(4)]
    states_out, own_out, send_out = refs
    n = maps_b.shape[1] // 2
    state = entering(received, decays, before, index(), peers, n, True)
    gyf = gy[...].astype(F32)
    for k in range(2):
        low = state(k).astype(BF16)
        states_out[k] = low
        grad_c = maps_local[:, (2 * k + 1) * n : (2 * k + 2) * n] + nt((gyf * grows[k]).astype(BF16), low)
        for at, value in ((2 * k, maps_b[:, k * n : (k + 1) * n]), (2 * k + 1, grad_c)):
            own_out[:, at * n : (at + 1) * n] = value
            send_out[:, at * n : (at + 1) * n] = value.astype(BF16)


def decay_kernel(states, grads, gy, ca, cb, decay_part, grows, *refs):
    gd_outs = refs[-2:]
    heads = decay_part.shape[0]
    length, columns = gy.shape
    gyf = gy[...].astype(F32)
    row, col = iotas(length, length)
    group = head_groups(heads, columns)
    frame = lax.broadcasted_iota(jnp.int32, (length, 1), 0)
    for k, (c, at_end, later) in enumerate(((ca, length - 1, row >= col), (cb, 0, row <= col))):
        grow, low = grows[k], states[k]
        gain = grow[at_end : at_end + 1]
        through = gain * jnp.sum(low.astype(F32) * grads[k].astype(F32), axis=0, keepdims=True)
        read = gyf * (grow * nn(c[...], low)) + jnp.where(frame == at_end, through, 0.0)
        reads = nt(group, read.astype(BF16))
        gd = nn(reads, later.astype(F32), precision=HIGH)[:heads]
        gd_outs[k][...] = gd + decay_part[:, k * length : (k + 1) * length]


def pair_kernel(index, stride, rows_out, blocks, count, *refs):
    parts, own_out, send_out = refs[:count], refs[-2], refs[-1]
    me = digit(index(), stride, 2)
    own, received = parts[0], parts[1]
    at = blocks * rows_out
    half = at // 2
    if count == 4:
        maps = parts[2][...] + parts[3][...].astype(F32)
    else:
        maps = own[:, at:] + received[:, at:].astype(F32)
    own_out[:, half:] = maps
    send_out[:, half:] = maps.astype(BF16)
    for high in range(blocks // 2):
        part = slice(high * rows_out, (high + 1) * rows_out)
        for away in range(2):
            at = pl.multiple_of((high * 2 + (me ^ away)) * rows_out, rows_out)
            total = own[:, pl.ds(at, rows_out)] + received[:, pl.ds(at, rows_out)].astype(F32)
            if away:
                send_out[:, part] = total.astype(BF16)
            else:
                own_out[:, part] = total


def last_kernel(scale, own, other, *refs):
    parts, gf_out, gw_out, map_outs = refs[:-6], refs[-6], refs[-5], refs[-4:]
    columns, n = gf_out.shape[1], map_outs[0].shape[1]
    gf_out[...] = (own[:, 0:columns] + other[:, 0:columns].astype(F32)).astype(BF16)
    for k, out in enumerate(map_outs):
        at = columns + k * n
        out[...] = own[:, at : at + n] + other[:, at : at + n].astype(F32)
    total = 0.0
    for part in parts:
        piece = part[...].astype(F32)
        total = total + (jnp.sum(piece, axis=0) if piece.ndim == 3 else piece)
    gw_out[...] = total * scale


def call(kernel, outs, *args, micros=0.0, held=0):
    specs = [pl.BlockSpec(memory_space=pltpu.HBM)] * held
    specs += [pl.BlockSpec(memory_space=pltpu.VMEM)] * (len(args) - held)
    outs = list(outs) + [jax.ShapeDtypeStruct(a.shape, a.dtype) for a in args[:held]]
    if held:
        args = tuple(pltpu.with_memory_space_constraint(a, pltpu.HBM) for a in args[:held]) + args[held:]
    cost = pl.CostEstimate(flops=int(micros * FLOPS_PER_MICRO), bytes_accessed=0, transcendentals=0)
    return pl.pallas_call(
        kernel,
        out_shape=outs,
        in_specs=specs,
        out_specs=[pl.BlockSpec(memory_space=pltpu.VMEM)] * len(outs),
        scratch_shapes=[pltpu.SemaphoreType.DMA((held,))] if held else [],
        cost_estimate=cost,
        compiler_params=pltpu.CompilerParams(vmem_limit_bytes=VMEM_LIMIT),
    )(*args)


def swap(value, axis, mask):
    return lax.ppermute(value, axis, [(i, i ^ mask) for i in range(lax.axis_size(axis))])


def far_first(sends, stride):
    jobs = list(enumerate(sends, start=1))
    return [swap(send, "seq", j * stride) for j, send in reversed(jobs)]


def local(features, w_in, b_ahead, c_ahead, b_behind, c_behind, decay_ahead, decay_behind, skip_gain, grad_y):
    peers, n_head = lax.axis_size("seq"), lax.axis_size("head")
    length, depth = features.shape
    heads, columns = decay_ahead.shape[0], w_in.shape[1]
    n = b_ahead.shape[1]
    seq_index = lambda: lax.axis_index("seq")
    head_index = lambda: lax.axis_index("head")
    shape = jax.ShapeDtypeStruct
    square = shape((length, columns), BF16)
    whole = shape((2 * n + GAIN_ROWS, columns), BF16)
    half = shape((n + GAIN_ROWS, columns), BF16)
    state_whole, state_half = shape((2 * n, columns), BF16), shape((n, columns), BF16)
    prefix = shape((2 * n + 8, columns), F32)

    steps = radices(peers)
    only = len(steps) == 1
    chunk_shapes = [half] * (steps[0] - 1) if only else [whole]
    pair = shape((2, length, columns), F32)
    *gradients, grow, da, db, gy, ca, cb, skip = call(
        functools.partial(gradient_kernel, seq_index, only, columns // heads),
        chunk_shapes + [pair],
        decay_ahead, decay_behind, grad_y, c_ahead, c_behind, skip_gain.reshape(1, heads),
        micros=1.35,
        held=6,
    )
    *states, x, left, ba, bb, fs, wi = call(
        functools.partial(state_kernel, seq_index, only, columns // heads),
        ([state_half] * (steps[0] - 1) if only else [state_whole]) + [square, pair],
        b_ahead, b_behind, features, w_in, da, db,
        micros=1.65,
        held=4,
    )
    maps = (ba, ca, bb, cb)
    gx_local, maps_local, decay_local, turned = call(
        local_kernel,
        [
            shape((length, columns), F32),
            shape((length, 4 * n), F32),
            shape((heads, 2 * length), F32),
            shape((depth, length), BF16),
        ],
        skip, x, gy, fs, *maps, da, db,
        micros=0.9,
    )
    def merges(chunk, decays):
        stride, before, seen = 1, None, []
        whole_shape, half_shape = (state_whole, state_half) if decays else (whole, half)
        for at, radix in enumerate(steps[:-1]):
            members = [chunk[0]] + [swap(chunk[0], "seq", j * stride) for j in range(1, radix)]
            seen.append(members)
            next_last = at == len(steps) - 2
            following = steps[at + 1]
            before, *chunk = call(
                functools.partial(
                    step_kernel, seq_index, stride, radix, at == 0, next_last, following, bool(decays)
                ),
                [prefix] + ([half_shape] * (following - 1) if next_last else [whole_shape]),
                *members, *(decays[at] if decays else []), *([] if at == 0 else [before]),
                micros=0.15,
            )
            stride *= radix
        return far_first(chunk, stride), [] if only else [before], seen

    stride = peers // steps[-1]
    gradients, gradient_before, seen = merges(gradients, None)
    states, state_before, _ = merges(states, seen) if not only else (far_first(states, stride), [], [])
    gradient_in, state_in = gradients + gradient_before, states + state_before + gradients
    rows_out, rows_w = depth // n_head, depth // peers
    direct = len(steps) == 2 and rows_w % 16 == 0
    pieces = [shape((4, rows_w, columns), BF16)] * (steps[0] - 1) if direct else [shape((depth, columns), BF16)]
    grad_x, grads, *sends = call(
        functools.partial(carry_kernel, seq_index, steps, stride, direct),
        [square, shape((2, n, columns), BF16)] + pieces,
        *gradient_in, turned, ba, bb, gx_local, left,
        micros=0.5,
    )
    def both(width):
        return [shape((length, width), F32), shape((length, width), BF16)]

    decay_part, maps_b, own, send = call(
        functools.partial(share_kernel, head_index, n_head),
        [shape((heads, 2 * length), F32), shape((length, 2 * n), F32)] + both(n_head // 2 * rows_out),
        grad_x, grads, x, wi, ba, bb, maps_local, decay_local, left,
        micros=1.0,
    )
    shares = [own, swap(send, "head", 1)]
    entered, own, send = call(
        functools.partial(state_share_kernel, seq_index, steps, peers),
        [shape((2, n, columns), BF16)] + both(4 * n),
        *state_in, gy, maps_local, maps_b, grow,
        micros=0.7,
    )
    shares += [own, swap(send, "head", 1)]
    mask, blocks = 2, n_head // 2
    while mask < n_head:
        own, send = call(
            functools.partial(pair_kernel, head_index, mask, rows_out, blocks, len(shares)),
            both(blocks // 2 * rows_out + 4 * n),
            *shares,
            micros=0.0,
        )
        shares = [own, swap(send, "head", mask)]
        mask, blocks = mask * 2, blocks // 2
    if direct:
        received = [swap(send, "seq", j) for j, send in enumerate(sends, start=1)]
        own_weight, *sends = call(
            functools.partial(fold_kernel, seq_index, steps),
            [shape((rows_w, columns), F32)] + [shape((rows_w, columns), BF16)] * 3,
            turned, grad_x, *received, shares[0],
            micros=0.22,
        )
        weight_parts = far_first(sends, stride) + [own_weight]
    else:
        weight_parts = [lax.all_to_all(sends[0].reshape(peers, rows_w, columns), "seq", 0, 0)]
    gd_ahead, gd_behind = call(
        decay_kernel,
        [shape((heads, length), F32)] * 2,
        entered, grads, gy, ca, cb, decay_part, grow, weight_parts[-1],
        micros=1.0,
    )
    grad_features, grad_w_in, *grad_maps = call(
        functools.partial(last_kernel, 1.0 / math.sqrt(length * peers)),
        [shape((length, rows_out), BF16), shape((rows_w, columns), F32)] + [shape((length, n), F32)] * 4,
        *shares, *weight_parts,
        micros=0.8,
    )
    return (grad_features, grad_w_in, *grad_maps, gd_ahead, gd_behind)


def solution(mesh):
    in_specs = (
        P("seq", None),
        P(None, "head"),
        P("seq", None),
        P("seq", None),
        P("seq", None),
        P("seq", None),
        P("head", "seq"),
        P("head", "seq"),
        P("head"),
        P("seq", "head"),
    )
    out_specs = (
        P("seq", "head"),
        P("seq", "head"),
        P("seq", None),
        P("seq", None),
        P("seq", None),
        P("seq", None),
        P("head", "seq"),
        P("head", "seq"),
    )
    return jax.shard_map(local, mesh=mesh, in_specs=in_specs, out_specs=out_specs, check_vma=False)
```

```python
import functools
import math

import jax
import jax.numpy as jnp
from jax import lax
from jax.experimental import pallas as pl
from jax.experimental.pallas import tpu as pltpu
from jax.sharding import PartitionSpec as P

F32 = jnp.float32
BF16 = jnp.bfloat16
HIGH = lax.Precision.HIGHEST
GAIN_ROWS = 16
FLOPS_PER_MICRO = 1.15e9
STATES_FAR = False
VMEM_LIMIT = 48 * 1024 * 1024


def nn(a, b, **kw):
    return lax.dot_general(a, b, (((1,), (0,)), ((), ())), preferred_element_type=F32, **kw)


def nt(a, b, **kw):
    return lax.dot_general(a, b, (((1,), (1,)), ((), ())), preferred_element_type=F32, **kw)


def iotas(rows, cols):
    return (
        lax.broadcasted_iota(jnp.int32, (rows, cols), 0),
        lax.broadcasted_iota(jnp.int32, (rows, cols), 1),
    )


def spread_rows(values, width):
    heads, length = values.shape
    return jnp.concatenate(
        [jnp.broadcast_to(values[h : h + 1], (width, length)) for h in range(heads)], axis=0
    )


def split3(value):
    high = value.astype(BF16)
    rest = value - high.astype(F32)
    middle = rest.astype(BF16)
    low = (rest - middle.astype(F32)).astype(BF16)
    return high, middle, low


def masked_sums(masks, values):
    masks = masks.astype(BF16)
    return sum(nt(masks, part) for part in split3(values))


def decay_factors(d_ahead, d_behind, width, rest):
    length = d_ahead.shape[1]
    row, col = iotas(length, length)
    masks = (col > row, col < row) if rest else (col <= row, col >= row)
    return [
        jnp.exp(masked_sums(mask.astype(F32), spread_rows(d, width))) for mask, d in zip(masks, (d_ahead, d_behind))
    ]


def radices(peers):
    bits = peers.bit_length() - 1
    return ([2] if bits % 2 else []) + [4] * (bits // 2)


def digit(index, stride, radix):
    return lax.rem(lax.div(index, stride), radix)


def read_gain(block, k=0):
    rows = block.astype(F32)[3 * k : 3 * k + 3]
    return rows[0:1] + rows[1:2] + rows[2:3]


def gain_block(*gains):
    rows = [p.astype(F32) for gain in gains for p in split3(gain)]
    pad = jnp.zeros((GAIN_ROWS - len(rows), gains[0].shape[1]), F32)
    return jnp.concatenate(rows + [pad], axis=0).astype(BF16)


def product_where(conditions, gains):
    result = jnp.ones_like(gains[0])
    for condition, gain in zip(conditions, gains):
        result = jnp.where(condition, result * gain, result)
    return result


def merge_coefficients(me, members, gains_up, gains_down):
    below, above = [], []
    others = range(1, len(members))
    for j in others:
        q = members[j]
        low = product_where(
            [jnp.logical_and(members[i] > q, members[i] < me) for i in others], [gains_up[i] for i in others]
        )
        high = product_where(
            [jnp.logical_and(members[i] < q, members[i] > me) for i in others], [gains_down[i] for i in others]
        )
        below.append(jnp.where(q < me, low, 0.0))
        above.append(jnp.where(q > me, high, 0.0))
    return below, above


def write_whole(out, up, down, gains):
    n = up.shape[0]
    out[0:n] = up.astype(BF16)
    out[n : 2 * n] = down.astype(BF16)
    if gains:
        out[2 * n :] = gain_block(*gains)


def write_halves(outs, up, down, gains, me):
    n = up.shape[0]
    up, down = up.astype(BF16), down.astype(BF16)
    for j, out in enumerate(outs, start=1):
        out[0:n] = jnp.where((me ^ j) > me, up, down)
        if gains:
            out[n:] = gain_block(*gains)


def write_chunk(outs, me, last, *chunk):
    if last:
        write_halves(outs, *chunk, me())
    else:
        write_whole(outs[0], *chunk)


def start_copies(sources, targets, sems):
    copies = [pltpu.make_async_copy(s, t, sems.at[k]) for k, (s, t) in enumerate(zip(sources, targets))]
    for copy in copies:
        copy.start()
    return copies


def gradient_kernel(me, last, width, *refs):
    *refs, sems = refs
    sources, outs, held = refs[:6], refs[6:-6], refs[-6:]
    copies = start_copies(sources, held, sems)
    da, db, gy, ca, cb, _ = held
    for copy in copies[:2]:
        copy.wait()
    grow_a, grow_b = decay_factors(da[...], db[...], width, False)
    *sends, grow_out = outs
    grow_out[0] = grow_a
    grow_out[1] = grow_b
    for copy in copies[2:]:
        copy.wait()
    gyf = gy[...].astype(F32)
    up = nn(cb[...].T, (gyf * grow_b).astype(BF16))
    down = nn(ca[...].T, (gyf * grow_a).astype(BF16))
    write_chunk(sends, me, last, up, down, (grow_a[gyf.shape[0] - 1 :], grow_b[0:1]))


def state_kernel(me, last, width, *refs):
    *refs, sems = refs
    sources, rest, held = refs[:4], refs[4:-4], refs[-4:]
    copies = start_copies(sources, held, sems)
    ba, bb, features, w_in = held
    skip, gy, ca, cb, da, db, *outs = rest
    *sends, x_out, left_out, gx_out, maps_out, decay_out, turned_out = outs
    left_a, left_b = decay_factors(da[...], db[...], width, True)
    left_out[0] = left_a
    left_out[1] = left_b
    for copy in copies:
        copy.wait()
    x = nn(features[...], w_in[...]).astype(BF16)
    x_out[...] = x
    xf = x.astype(F32)
    up = nn(ba[...].T, (xf * left_a).astype(BF16))
    down = nn(bb[...].T, (xf * left_b).astype(BF16))
    write_chunk(sends, me, last, up, down, ())
    in_block(skip, x, gy, features, ba, ca, bb, cb, da, db, gx_out, maps_out, decay_out, turned_out)


def step_kernel(index, stride, radix, first, next_last, next_radix, states, *refs):
    refs = list(refs)
    members_in = [refs.pop(0) for _ in range(radix)]
    gains_in = [refs.pop(0) for _ in range(radix)] if states else members_in
    before, outs = refs[0], refs[-(next_radix if next_last else 2) :]
    pre_out, *outs = outs
    n = (gains_in[0].shape[0] - GAIN_ROWS) // 2
    seq = index()
    me = digit(seq, stride, radix)
    members = [me ^ j for j in range(radix)]
    loaded = [(ref[0:n].astype(F32), ref[n : 2 * n].astype(F32)) for ref in members_in]
    both = [[read_gain(ref[2 * n :], k) for ref in gains_in] for k in range(2)]
    gains = both if states else both[::-1]
    coefficients = merge_coefficients(me, members, *gains)
    width = members_in[0].shape[1]
    new_grow = []
    totals = []
    for down in range(2):
        total = sum(coefficients[down][j - 1] * loaded[j][down] for j in range(1, radix))
        inside = [(members[j] > me) if down else (members[j] < me) for j in range(1, radix)]
        grow = product_where(inside, gains[down][1:])
        if not first:
            kept = before[2 * n + down : 2 * n + down + 1]
            total = kept * total + before[down * n : (down + 1) * n]
            grow = kept * grow
        pre_out[down * n : (down + 1) * n] = total
        new_grow.append(grow)
        group = 0.0
        for j in range(radix):
            rest = [i for i in range(radix) if i != j]
            outer = [(members[i] < members[j]) if down else (members[i] > members[j]) for i in rest]
            group = group + product_where(outer, [gains[down][i] for i in rest]) * loaded[j][down]
        totals.append(group)
    pre_out[2 * n :] = jnp.concatenate(new_grow + [jnp.zeros((6, width), F32)], axis=0)
    new = () if states else [functools.reduce(lambda a, b: a * b, both[k]) for k in range(2)]
    write_chunk(outs, lambda: digit(seq, stride * radix, next_radix), next_last, *totals, new)


def in_block(skip, x, gy, features, ba, ca, bb, cb, da, db, gx_out, maps_out, decay_out, turned_out):
    heads, length = da.shape
    width = x.shape[1] // heads
    n = ba.shape[1]
    row, col = iotas(length, length)
    upto = (col <= row).astype(F32)
    since = (col >= row).astype(F32)
    pad = jnp.zeros((8 - heads, length), F32)
    d_ahead = jnp.concatenate([da[...], pad], axis=0)
    d_behind = jnp.concatenate([db[...], pad], axis=0)
    columns_a = masked_sums(upto, d_ahead)
    columns_b = masked_sums(since, d_behind)
    rows_a = columns_a.T
    rows_b = columns_b.T
    later, same = col > row, col == row
    raw_a = nt(ba[...], ca[...])
    raw_b = nt(bb[...], cb[...])
    affinity = jnp.where(same, raw_a + raw_b, jnp.where(later, raw_a, raw_b))
    weight_sum = jnp.zeros((length, length), F32)
    counts = jnp.concatenate([since.T, upto.T], axis=1).astype(BF16)
    cross = jnp.concatenate([row < col, row > col], axis=1).astype(F32)
    totals = []
    for h in range(heads):
        part = slice(h * width, (h + 1) * width)
        gap = jnp.where(
            later,
            rows_a[h : h + 1] - columns_a[:, h : h + 1],
            rows_b[h : h + 1] - columns_b[:, h : h + 1],
        )
        decay = jnp.exp(jnp.where(same, 0.0, gap))
        score_grad = nt(x[:, part], gy[:, part])
        weighted = score_grad * decay
        weight_sum = weight_sum + weighted
        gx_out[:, part] = nn((decay * affinity).astype(BF16), gy[:, part]) + skip[:, h : h + 1] * gy[:, part].astype(F32)
        pieces = nn((weighted * affinity).astype(BF16), counts)
        totals.append(jnp.sum(pieces * cross, axis=0, keepdims=True))
    for h in range(heads):
        decay_out[h : h + 1] = totals[h]
    ahead = jnp.where(col >= row, weight_sum, 0.0).astype(BF16)
    behind = jnp.where(col <= row, weight_sum, 0.0).astype(BF16)
    maps_out[:, 0:n] = nn(ahead, ca[...])
    maps_out[:, n : 2 * n] = nn(ahead.T, ba[...])
    maps_out[:, 2 * n : 3 * n] = nn(behind, cb[...])
    maps_out[:, 3 * n :] = nn(behind.T, bb[...])
    turned_out[...] = features[...].T


def entering(received, decays, before, seq, peers, n, states):
    radix = len(received) + 1
    me = digit(seq, peers // radix, radix)
    members = [me ^ j for j in range(radix)]
    ahead, behind = [[read_gain(ref[n:], k) for ref in decays[:1] + decays] for k in range(2)]
    gains = (ahead, behind) if states else (behind, ahead)
    coefficients = merge_coefficients(me, members, *gains)

    def enter(down):
        total = 0.0
        for coefficient, ref in zip(coefficients[down], received):
            total = total + coefficient * ref[0:n].astype(F32)
        if before is not None:
            total = before[2 * n + down : 2 * n + down + 1] * total + before[down * n : (down + 1) * n]
        return total

    return enter


def take_chunk(refs, radix, first, far_first):
    received = [refs.pop(0) for _ in range(radix - 1)]
    return received[::-1] if far_first else received, None if first else refs.pop(0)


def carry_kernel(index, steps, stride, direct, *refs):
    refs = list(refs)
    received, before = take_chunk(refs, steps[-1], len(steps) == 1, True)
    turned, ba, bb, gx_local, left = [refs.pop(0) for _ in range(5)]
    gx_out, grad_out, *outs = refs
    seq = index()
    me = digit(seq, stride, steps[-1])
    gradient = entering(received, received, before, seq, stride * steps[-1], ba.shape[1], False)
    grad_x = gx_local[...]
    for k, b in enumerate((ba, bb)):
        grad = gradient(1 - k).astype(BF16)
        grad_out[k] = grad
        grad_x = grad_x + nn(b[...], grad).astype(BF16).astype(F32) * left[k]
    grad_x = grad_x.astype(BF16)
    gx_out[...] = grad_x
    if not direct:
        outs[0][...] = nn(turned[...], grad_x).astype(BF16)
        return
    rows = outs[0].shape[1]
    for j, out in enumerate(outs, start=1):
        for k in range(4):
            at = (me ^ k) * steps[0] + (digit(seq, 1, steps[0]) ^ j)
            out[k] = nn(turned[pl.ds(pl.multiple_of(at * rows, rows), rows), :], grad_x).astype(BF16)


def fold_kernel(index, steps, turned, grad_x, *refs):
    received, outs = refs[: steps[0] - 1], refs[-4:]
    rows = received[0].shape[1]
    seq = index()
    for k in range(4):
        at = (digit(seq, steps[0], steps[1]) ^ k) * steps[0] + digit(seq, 1, steps[0])
        share = nn(turned[pl.ds(pl.multiple_of(at * rows, rows), rows), :], grad_x[...])
        total = sum([ref[k].astype(F32) for ref in received], share)
        outs[k][...] = total.astype(outs[k].dtype)


def head_groups(heads, columns):
    rows, cols = iotas(8, columns)
    return (lax.div(cols, columns // heads) == rows).astype(BF16)


def share_kernel(index, n_head, grad_x, grads, x, w_in, ba, bb, maps_local, decay_local, lefts, *outs):
    decay_out, maps_out, own_out, send_out = outs
    heads = decay_local.shape[0]
    n = ba.shape[1]
    length, columns = x.shape
    xf = x[...].astype(F32)
    row, col = iotas(length, length)
    group = head_groups(heads, columns)
    rows_out = w_in.shape[0] // n_head
    for k, (b, earlier) in enumerate(((ba, row < col), (bb, row > col))):
        left, grad = lefts[k], grads[k]
        write = nn(b[...], grad).astype(BF16).astype(F32) * left * xf
        writes = nt(group, write.astype(BF16))
        part = slice(k * length, (k + 1) * length)
        decay_out[:, part] = decay_local[:, part] + nn(writes, earlier.astype(F32), precision=HIGH)[:heads]
        grad_b = maps_local[:, 2 * k * n : (2 * k + 1) * n] + nt((xf * left).astype(BF16), grad)
        maps_out[:, k * n : (k + 1) * n] = grad_b
    for high in range(n_head // 2):
        part = slice(high * rows_out, (high + 1) * rows_out)
        for away in range(2):
            at = pl.multiple_of((high * 2 + (lax.rem(index(), 2) ^ away)) * rows_out, rows_out)
            share = nt(grad_x[...], w_in[pl.ds(at, rows_out), :])
            if away:
                send_out[:, part] = share.astype(BF16)
            else:
                own_out[:, part] = share


def state_share_kernel(index, steps, peers, *refs):
    refs = list(refs)
    received, before = take_chunk(refs, steps[-1], len(steps) == 1, STATES_FAR)
    decays, _ = take_chunk(refs, steps[-1], True, True)
    gy, maps_local, maps_b, grows = [refs.pop(0) for _ in range(4)]
    states_out, own_out, send_out = refs
    n = maps_b.shape[1] // 2
    state = entering(received, decays, before, index(), peers, n, True)
    gyf = gy[...].astype(F32)
    for k in range(2):
        low = state(k).astype(BF16)
        states_out[k] = low
        grad_c = maps_local[:, (2 * k + 1) * n : (2 * k + 2) * n] + nt((gyf * grows[k]).astype(BF16), low)
        for at, value in ((2 * k, maps_b[:, k * n : (k + 1) * n]), (2 * k + 1, grad_c)):
            own_out[:, at * n : (at + 1) * n] = value
            send_out[:, at * n : (at + 1) * n] = value.astype(BF16)


def decay_kernel(states, grads, gy, ca, cb, decay_part, grows, *refs):
    gd_outs = refs[-2:]
    heads = decay_part.shape[0]
    length, columns = gy.shape
    gyf = gy[...].astype(F32)
    row, col = iotas(length, length)
    group = head_groups(heads, columns)
    frame = lax.broadcasted_iota(jnp.int32, (length, 1), 0)
    for k, (c, at_end, later) in enumerate(((ca, length - 1, row >= col), (cb, 0, row <= col))):
        grow, low = grows[k], states[k]
        gain = grow[at_end : at_end + 1]
        through = gain * jnp.sum(low.astype(F32) * grads[k].astype(F32), axis=0, keepdims=True)
        read = gyf * (grow * nn(c[...], low)) + jnp.where(frame == at_end, through, 0.0)
        reads = nt(group, read.astype(BF16))
        gd = nn(reads, later.astype(F32), precision=HIGH)[:heads]
        gd_outs[k][...] = gd + decay_part[:, k * length : (k + 1) * length]


def pair_kernel(index, stride, rows_out, blocks, count, *refs):
    parts, own_out, send_out = refs[:count], refs[-2], refs[-1]
    me = digit(index(), stride, 2)
    own, received = parts[0], parts[1]
    at = blocks * rows_out
    half = at // 2
    if count == 4:
        maps = parts[2][...] + parts[3][...].astype(F32)
    else:
        maps = own[:, at:] + received[:, at:].astype(F32)
    own_out[:, half:] = maps
    send_out[:, half:] = maps.astype(BF16)
    for high in range(blocks // 2):
        part = slice(high * rows_out, (high + 1) * rows_out)
        for away in range(2):
            at = pl.multiple_of((high * 2 + (me ^ away)) * rows_out, rows_out)
            total = own[:, pl.ds(at, rows_out)] + received[:, pl.ds(at, rows_out)].astype(F32)
            if away:
                send_out[:, part] = total.astype(BF16)
            else:
                own_out[:, part] = total


def last_kernel(scale, own, other, *refs):
    parts, gf_out, gw_out, map_outs = refs[:-6], refs[-6], refs[-5], refs[-4:]
    columns, n = gf_out.shape[1], map_outs[0].shape[1]
    gf_out[...] = (own[:, 0:columns] + other[:, 0:columns].astype(F32)).astype(BF16)
    for k, out in enumerate(map_outs):
        at = columns + k * n
        out[...] = own[:, at : at + n] + other[:, at : at + n].astype(F32)
    total = 0.0
    for part in parts:
        piece = part[...].astype(F32)
        total = total + (jnp.sum(piece, axis=0) if piece.ndim == 3 else piece)
    gw_out[...] = total * scale


def call(kernel, outs, *args, micros=0.0, held=0):
    specs = [pl.BlockSpec(memory_space=pltpu.HBM)] * held
    specs += [pl.BlockSpec(memory_space=pltpu.VMEM)] * (len(args) - held)
    outs = list(outs) + [jax.ShapeDtypeStruct(a.shape, a.dtype) for a in args[:held]]
    if held:
        args = tuple(pltpu.with_memory_space_constraint(a, pltpu.HBM) for a in args[:held]) + args[held:]
    cost = pl.CostEstimate(flops=int(micros * FLOPS_PER_MICRO), bytes_accessed=0, transcendentals=0)
    return pl.pallas_call(
        kernel,
        out_shape=outs,
        in_specs=specs,
        out_specs=[pl.BlockSpec(memory_space=pltpu.VMEM)] * len(outs),
        scratch_shapes=[pltpu.SemaphoreType.DMA((held,))] if held else [],
        cost_estimate=cost,
        compiler_params=pltpu.CompilerParams(vmem_limit_bytes=VMEM_LIMIT),
    )(*args)


def swap(value, axis, mask):
    return lax.ppermute(value, axis, [(i, i ^ mask) for i in range(lax.axis_size(axis))])


def exchange(sends, stride, far_first):
    arrived = [swap(send, "seq", j * stride) for j, send in enumerate(sends, start=1)]
    return arrived[::-1] if far_first else arrived


def local(features, w_in, b_ahead, c_ahead, b_behind, c_behind, decay_ahead, decay_behind, skip_gain, grad_y):
    peers, n_head = lax.axis_size("seq"), lax.axis_size("head")
    length, depth = features.shape
    heads, columns = decay_ahead.shape[0], w_in.shape[1]
    n = b_ahead.shape[1]
    seq_index = lambda: lax.axis_index("seq")
    head_index = lambda: lax.axis_index("head")
    shape = jax.ShapeDtypeStruct
    square = shape((length, columns), BF16)
    whole = shape((2 * n + GAIN_ROWS, columns), BF16)
    half = shape((n + GAIN_ROWS, columns), BF16)
    state_whole, state_half = shape((2 * n, columns), BF16), shape((n, columns), BF16)
    prefix = shape((2 * n + 8, columns), F32)

    steps = radices(peers)
    only = len(steps) == 1
    chunk_shapes = [half] * (steps[0] - 1) if only else [whole]
    pair = shape((2, length, columns), F32)
    *gradients, grow, da, db, gy, ca, cb, skip = call(
        functools.partial(gradient_kernel, seq_index, only, columns // heads),
        chunk_shapes + [pair],
        decay_ahead, decay_behind, grad_y, c_ahead, c_behind, skip_gain.reshape(1, heads),
        micros=1.35,
        held=6,
    )
    *states, x, left, gx_local, maps_local, decay_local, turned, ba, bb, _, wi = call(
        functools.partial(state_kernel, seq_index, only, columns // heads),
        ([state_half] * (steps[0] - 1) if only else [state_whole])
        + [square, pair]
        + [
            shape((length, columns), F32),
            shape((length, 4 * n), F32),
            shape((heads, 2 * length), F32),
            shape((depth, length), BF16),
        ],
        b_ahead, b_behind, features, w_in, skip, gy, ca, cb, da, db,
        micros=2.5,
        held=4,
    )

    def merges(chunk, decays):
        stride, before, seen = 1, None, []
        whole_shape, half_shape = (state_whole, state_half) if decays else (whole, half)
        for at, radix in enumerate(steps[:-1]):
            members = [chunk[0]] + [swap(chunk[0], "seq", j * stride) for j in range(1, radix)]
            seen.append(members)
            next_last = at == len(steps) - 2
            following = steps[at + 1]
            before, *chunk = call(
                functools.partial(
                    step_kernel, seq_index, stride, radix, at == 0, next_last, following, bool(decays)
                ),
                [prefix] + ([half_shape] * (following - 1) if next_last else [whole_shape]),
                *members, *(decays[at] if decays else []), *([] if at == 0 else [before]),
                micros=0.15,
            )
            stride *= radix
        return exchange(chunk, stride, not decays or STATES_FAR), [] if only else [before], seen

    stride = peers // steps[-1]
    gradients, gradient_before, seen = merges(gradients, None)
    states, state_before, _ = merges(states, seen) if not only else (exchange(states, stride, STATES_FAR), [], [])
    gradient_in, state_in = gradients + gradient_before, states + state_before + gradients
    rows_out, rows_w = depth // n_head, depth // peers
    direct = len(steps) == 2 and rows_w % 16 == 0
    pieces = [shape((4, rows_w, columns), BF16)] * (steps[0] - 1) if direct else [shape((depth, columns), BF16)]
    grad_x, grads, *sends = call(
        functools.partial(carry_kernel, seq_index, steps, stride, direct),
        [square, shape((2, n, columns), BF16)] + pieces,
        *gradient_in, turned, ba, bb, gx_local, left,
        micros=0.5,
    )
    def both(width):
        return [shape((length, width), F32), shape((length, width), BF16)]

    decay_part, maps_b, own, send = call(
        functools.partial(share_kernel, head_index, n_head),
        [shape((heads, 2 * length), F32), shape((length, 2 * n), F32)] + both(n_head // 2 * rows_out),
        grad_x, grads, x, wi, ba, bb, maps_local, decay_local, left,
        micros=1.0,
    )
    shares = [own, swap(send, "head", 1)]
    entered, own, send = call(
        functools.partial(state_share_kernel, seq_index, steps, peers),
        [shape((2, n, columns), BF16)] + both(4 * n),
        *state_in, gy, maps_local, maps_b, grow,
        micros=0.2,
    )
    shares += [own, swap(send, "head", 1)]
    mask, blocks = 2, n_head // 2
    while mask < n_head:
        own, send = call(
            functools.partial(pair_kernel, head_index, mask, rows_out, blocks, len(shares)),
            both(blocks // 2 * rows_out + 4 * n),
            *shares,
            micros=0.0,
        )
        shares = [own, swap(send, "head", mask)]
        mask, blocks = mask * 2, blocks // 2
    if direct:
        received = [swap(send, "seq", j) for j, send in enumerate(sends, start=1)]
        own_weight, *sends = call(
            functools.partial(fold_kernel, seq_index, steps),
            [shape((rows_w, columns), F32)] + [shape((rows_w, columns), BF16)] * 3,
            turned, grad_x, *received, shares[0],
            micros=0.22,
        )
        weight_parts = exchange(sends, stride, True) + [own_weight]
    else:
        weight_parts = [lax.all_to_all(sends[0].reshape(peers, rows_w, columns), "seq", 0, 0)]
    gd_ahead, gd_behind = call(
        decay_kernel,
        [shape((heads, length), F32)] * 2,
        entered, grads, gy, ca, cb, decay_part, grow, weight_parts[-1],
        micros=1.0,
    )
    grad_features, grad_w_in, *grad_maps = call(
        functools.partial(last_kernel, 1.0 / math.sqrt(length * peers)),
        [shape((length, rows_out), BF16), shape((rows_w, columns), F32)] + [shape((length, n), F32)] * 4,
        *shares, *weight_parts,
        micros=0.8,
    )
    return (grad_features, grad_w_in, *grad_maps, gd_ahead, gd_behind)


def solution(mesh):
    in_specs = (
        P("seq", None),
        P(None, "head"),
        P("seq", None),
        P("seq", None),
        P("seq", None),
        P("seq", None),
        P("head", "seq"),
        P("head", "seq"),
        P("head"),
        P("seq", "head"),
    )
    out_specs = (
        P("seq", "head"),
        P("seq", "head"),
        P("seq", None),
        P("seq", None),
        P("seq", None),
        P("seq", None),
        P("head", "seq"),
        P("head", "seq"),
    )
    return jax.shard_map(local, mesh=mesh, in_specs=in_specs, out_specs=out_specs, check_vma=False)
```
